32 devices in a mesh: beam: 2 (over core), path: 4 (over y, x), gz: 4 (over z).
Axes of the slice: x: 2, y: 2, z: 4, core: 2. Of those that a mesh axis runs over, the one named last changes fastest.
Arguments:
- maps: float32 [8, 64, 16, 512], P(None, 'gz', 'beam', 'path'), may hold values from 0.02 to 1
- measured: float32 [8, 64, 16], P(None, 'gz', 'beam'), may hold values from 0 to 76.8
- beta_table: float32 [8, 8], replicated, may hold values from 0.3 to 2
- view: int32 [1], replicated, may hold values from 0 to 7
- kappa: float32 [16, 8], replicated, may hold values from 0.3 to 2
- line_of: int32 [8], replicated, may hold values from 0 to 15
- side: int32 [8], replicated, may hold values from 0 to 1, as said below
Outputs:
- emission: float32 [8, 64, 16], P(None, 'gz', 'beam')
- maps_out: float32 [8, 64, 16, 512], P(None, 'gz', 'beam', 'path')
- data_dual: float32 [8, 64, 16], P(None, 'gz', 'beam')
The draws below stay inside these ranges and needn't reach their ends.
Inputs may be any that keep to these rules, and one draw needn't show every extreme that they name: Exactly 4 elements have side 0.
All inputs are finite; a program needn't handle non-finite values.
Results may differ from the reference program's by a relative error of at most 0.0001.
Values sent between devices are 32-bit elements; how exact they have to be, the bound alone decides.
No kernel may reach another device: no remote copies, remote signals or barrier semaphores. Data moves between devices by JAX's collectives and lax.ppermute only.
A program may use at most 64 MiB of HBM per device.

```python
import math
import jax
import jax.numpy as jnp
from jax import lax

E = 8
L = 16
V = 8
ITERS = 2
NX = 16
NY = 512
NZ = 64


def draw_side(key, part):
    order = jax.random.permutation(key, E)
    return (order < E // 2).astype(jnp.int32)


def sparse_rows(key):
    offset = jax.random.randint(jax.random.fold_in(key, 7), (), 0, 4)
    elem_ids = jnp.arange(E, dtype=jnp.int32)[:, None]
    run_ids = (jnp.arange(NZ, dtype=jnp.int32) // 4)[None, :]
    return (elem_ids + run_ids + offset) % 4 == 0


def draw_maps(key, part):
    sparse = sparse_rows(key)
    uniform_cells = jax.random.uniform(jax.random.fold_in(key, 1), (E, NZ, NX, NY), jnp.float32)
    regular = 0.02 * jnp.exp(jnp.log(50.0) * uniform_cells)
    low_level = 0.02
    high_level = 1.0
    patch_z = (NZ + 3) // 4
    patch_x = (NX + 3) // 4
    patch_y = (NY + 7) // 8
    patches = jax.random.uniform(jax.random.fold_in(key, 2), (E, patch_z, patch_x, patch_y), jnp.float32)
    spread = jnp.repeat(jnp.repeat(jnp.repeat(patches, 4, axis=1), 4, axis=2), 8, axis=3)
    spread = spread[:, :NZ, :NX, :NY]
    levels = jnp.where(spread < 0.4, high_level, low_level)
    return jnp.where(sparse[:, :, None, None], levels, regular).astype(jnp.float32)


def draw_measured(key, part):
    sparse = sparse_rows(key)
    uniform_rows = jax.random.uniform(jax.random.fold_in(key, 3), (E, NZ, NX), jnp.float32)
    low_rows = uniform_rows * (0.004 * NY)
    high_rows = uniform_rows * (0.15 * NY)
    return jnp.where(sparse[:, :, None], low_rows, high_rows).astype(jnp.float32)


def with_ends(result, own_key, low, high):
    place = [jax.random.randint(jax.random.fold_in(own_key, axis), (), 0, length) for axis, length in enumerate(result.shape)]
    main_axis = result.shape.index(max(result.shape))
    neighbour = place[:main_axis] + [(place[main_axis] + 1) % result.shape[main_axis]] + place[main_axis + 1:]
    return result.at[tuple(place)].set(low).at[tuple(neighbour)].set(high)


def setup_inputs(seed: int = 0) -> dict:
    splits = jax.random.split(jax.random.key(seed), 8)
    return {
        "maps": draw_maps(jax.random.fold_in(splits[7], 71), 0),
        "measured": draw_measured(jax.random.fold_in(splits[7], 71), 0),
        "beta_table": jnp.clip(jnp.exp(jax.random.uniform(splits[2], (V, E), jnp.float32, math.log(0.3), math.log(2.0))), 0.3, 2.0),
        "view": jax.random.randint(splits[3], (1,), 0, V).astype(jnp.int32),
        "kappa": jnp.clip(jnp.exp(jax.random.uniform(splits[4], (L, E), jnp.float32, math.log(0.3), math.log(2.0))), 0.3, 2.0),
        "line_of": with_ends(jax.random.randint(splits[5], (E,), 0, L), jax.random.fold_in(splits[5], 1), 0, L - 1).astype(jnp.int32),
        "side": draw_side(jax.random.fold_in(splits[7], 71), 0),
    }


LAM = 0.1
HIGHP = lax.Precision.HIGHEST


def exclusive(values, axis):
    running = jnp.cumsum(values, axis=axis)
    count = values.shape[axis]
    head = jnp.zeros_like(lax.slice_in_dim(values, 0, 1, axis=axis))
    return jnp.concatenate([head, lax.slice_in_dim(running, 0, count - 1, axis=axis)], axis=axis)


def reverse_exclusive(values, axis):
    return jnp.flip(exclusive(jnp.flip(values, axis), axis), axis)


def forward_diff(values, axis):
    count = values.shape[axis]
    ahead = lax.slice_in_dim(values, 1, count, axis=axis) - lax.slice_in_dim(values, 0, count - 1, axis=axis)
    tail = jnp.zeros_like(lax.slice_in_dim(values, 0, 1, axis=axis))
    return jnp.concatenate([ahead, tail], axis=axis)


def back_diff(duals, axis):
    count = duals.shape[axis]
    head = jnp.zeros_like(lax.slice_in_dim(duals, 0, 1, axis=axis))
    earlier = jnp.concatenate([head, lax.slice_in_dim(duals, 0, count - 1, axis=axis)], axis=axis)
    return earlier - duals


def reference(maps, measured, beta_table, view, kappa, line_of, side):
    pick = (jnp.arange(V, dtype=jnp.int32) == view[0]).astype(jnp.float32)
    beta = jnp.dot(pick, beta_table, precision=HIGHP)
    mu_in = jnp.einsum('e,ezxy->zxy', beta, maps, precision=HIGHP)
    att_in = jnp.exp(-exclusive(mu_in, 1) / NX)
    onehot = (line_of[:, None] == jnp.arange(L, dtype=jnp.int32)[None, :]).astype(jnp.float32)
    absorb = jnp.dot(onehot, kappa, precision=HIGHP)
    mu_out = jnp.einsum('ef,fzxy->ezxy', absorb, maps, precision=HIGHP)
    depth = jnp.where(side[:, None, None, None] == 0, exclusive(mu_out, 3), reverse_exclusive(mu_out, 3))
    weight = att_in[None] * jnp.exp(-depth / NY)
    proj = jnp.sum(weight * maps, axis=3)
    total = jnp.sum(weight, axis=3)
    sig_q = 1.0 / total
    tau = 1.0 / (weight + 6.0)
    current = maps
    extrap = maps
    data_dual = jnp.zeros_like(proj)
    dual_z = jnp.zeros_like(maps)
    dual_x = jnp.zeros_like(maps)
    dual_y = jnp.zeros_like(maps)
    for step in range(ITERS):
        image = proj if step == 0 else jnp.sum(weight * extrap, axis=3)
        data_dual = (data_dual + sig_q * (image - measured)) / (1.0 + sig_q)
        dual_z = jnp.clip(dual_z + 0.5 * forward_diff(extrap, 1), -LAM, LAM)
        dual_x = jnp.clip(dual_x + 0.5 * forward_diff(extrap, 2), -LAM, LAM)
        dual_y = jnp.clip(dual_y + 0.5 * forward_diff(extrap, 3), -LAM, LAM)
        adjoint = back_diff(dual_z, 1) + back_diff(dual_x, 2) + back_diff(dual_y, 3)
        updated = jnp.maximum(current - tau * (weight * data_dual[..., None] + adjoint), 0.0)
        extrap = 2.0 * updated - current
        current = updated
    return proj / NY, current, data_dual
```

```python
import functools

import jax
import jax.numpy as jnp
from jax import lax
from jax.experimental import pallas as pl
from jax.experimental.pallas import tpu as pltpu
from jax.sharding import PartitionSpec as P

ITERS = 2
LAM = 0.1
F32 = jnp.float32
VMEM = pltpu.VMEM
SMEM = pltpu.SMEM
VMEM_LIMIT = 32 * 1024 * 1024


def clip(value):
    return jnp.clip(value, -LAM, LAM)


def call(body, ins, outs, spaces, scratch=(), flops=1_000_000):
    specs = [pl.BlockSpec(memory_space=space) for space in spaces]
    moved = sum(a.size * 4 for a in ins) + sum(o.size * 4 for o in outs)
    return pl.pallas_call(
        body,
        out_shape=outs,
        in_specs=specs,
        out_specs=[pl.BlockSpec(memory_space=VMEM)] * len(outs),
        scratch_shapes=list(scratch),
        compiler_params=pltpu.CompilerParams(vmem_limit_bytes=VMEM_LIMIT),
        cost_estimate=pl.CostEstimate(flops=flops, bytes_accessed=moved, transcendentals=0),
    )(*ins)


def f32(*shape):
    return jax.ShapeDtypeStruct(shape, F32)


def shifted(block, axis, distance):
    devices = range(lax.axis_size(axis))
    route = [(i - distance, i) for i in devices if i - distance in devices]
    return lax.ppermute(block, axis, route)


def around(block, axis):
    n = lax.axis_size(axis)
    return [lax.ppermute(block, axis, [(i, (i + s) % n) for i in range(n)]) for s in range(1, n)]


def beam_sides(cells):
    count, rank = lax.axis_size("beam"), lax.axis_index("beam")
    if count == 2:
        return [
            (
                jnp.where(rank == 0, cells - 1, 0),
                jnp.where(rank == 0, F32(-1.0), F32(1.0)),
                None,
            )
        ]
    return [(cells - 1, F32(-1.0), rank < count - 1), (0, F32(1.0), rank > 0)]


def beam_rows(first, last):
    count, rank = lax.axis_size("beam"), lax.axis_index("beam")
    if count == 2:
        return [jnp.where(rank == 0, last, first)]
    return [last, first]


def face(own, other, sign, there):
    step = (own - other) * sign
    return step if there is None else jnp.where(there, step, 0.0)


def exchange_beam(rows):
    if lax.axis_size("beam") == 2:
        return [lax.ppermute(rows[0], "beam", [(0, 1), (1, 0)])]
    return [shifted(rows[1], "beam", -1), shifted(rows[0], "beam", 1)]


def open_kernel(total, maps_ref, beta_ref, view_ref, inside_ref, slab_ref, zfirst_ref, zlast_ref, *face_refs):
    elems, slices, cells, _ = maps_ref.shape
    view = view_ref[0]
    beta = [beta_ref[view, e] for e in range(elems)]
    sub = lax.broadcasted_iota(jnp.int32, maps_ref.shape[2:], 0)
    for z in range(slices):
        tiles = [maps_ref[e, z] for e in range(elems)]
        mu = beta[0] * tiles[0]
        for e in range(1, elems):
            mu = mu + beta[e] * tiles[e]
        run = mu
        reach = 1
        while reach < cells:
            run = run + jnp.where(sub >= reach, pltpu.roll(run, reach, axis=0), 0.0)
            reach *= 2
        inside_ref[z] = jnp.where(sub >= 1, pltpu.roll(run, 1, axis=0), 0.0)
        slab_ref[z : z + 1] = run[cells - 1 : cells]
        for e in range(elems):
            rows = beam_rows(tiles[e][0:1], tiles[e][cells - 1 : cells])
            for ref, row in zip(face_refs, rows):
                ref[e * slices + z : e * slices + z + 1] = row
    for e in range(elems):
        zfirst_ref[e] = maps_ref[e, 0]
        zlast_ref[e] = maps_ref[e, slices - 1]


def depth_kernel(total, maps_ref, kappa_ref, line_ref, side_ref, local_ref, pack_ref, mu_ref, parts_ref, sums_ref):
    elems, slices, cells, width = maps_ref.shape
    rows = slices * cells
    row = lax.broadcasted_iota(jnp.int32, (2 * width, 2 * width), 0)
    col = lax.broadcasted_iota(jnp.int32, (2 * width, 2 * width), 1)
    row = jnp.where(row >= width, row - width, row)
    table = jnp.where((row < col) | (col >= width), 1.0, 0.0).astype(jnp.bfloat16)
    for e in range(elems):
        line = line_ref[e]
        mu = kappa_ref[0, line] * maps_ref[0]
        for f in range(1, elems):
            mu = mu + kappa_ref[f, line] * maps_ref[f]
        mu_ref[e] = mu
        flat = mu.reshape(rows, width)
        high = flat.astype(jnp.bfloat16)
        low = (flat - high.astype(F32)).astype(jnp.bfloat16)
        parts_ref[e * rows : (e + 1) * rows, 0:width] = high
        parts_ref[e * rows : (e + 1) * rows, width:] = low
    sums_ref[...] = jnp.dot(parts_ref[...], table, preferred_element_type=F32)
    lane = lax.broadcasted_iota(jnp.int32, (cells, elems * slices), 1)
    forward = [side_ref[e] == 0 for e in range(elems)]
    scale = -1.0 / total

    def step(z, packs):
        strip, first, last = packs
        place = lane - z
        for e in range(elems):
            at = pl.ds(pl.multiple_of((e * slices + z) * cells, cells), cells)
            before = sums_ref[at, 0:width]
            whole = sums_ref[at, width:]
            after = whole - before - mu_ref[e, z]
            local_ref[e, z] = jnp.exp(jnp.where(forward[e], before, after) * scale)
            here = place == e * slices
            tile = maps_ref[e, z]
            strip = jnp.where(here, whole[:, 0:1], strip)
            first = jnp.where(here, tile[:, 0:1], first)
            last = jnp.where(here, tile[:, width - 1 : width], last)
        return strip, first, last

    zero = jnp.zeros((cells, elems * slices), F32)
    strip, first, last = lax.fori_loop(0, slices, step, (zero, zero, zero))
    pack_ref[0] = strip
    pack_ref[1] = first
    pack_ref[2] = last


def weight_kernel(total, maps_ref, inside_ref, carry_ref, local_ref, pack_ref, weight_ref, out_ref):
    elems, slices, cells, width = maps_ref.shape
    lane = lax.broadcasted_iota(jnp.int32, (cells, elems * slices), 1)
    there = lax.axis_index("beam") > 0
    scale = -1.0 / total

    def step(z, packs):
        proj, whole = packs
        place = lane - z
        carry = jnp.where(there, carry_ref[pl.ds(z, 1)], 0.0)
        att = jnp.exp((inside_ref[z] + carry) * scale)
        for e in range(elems):
            weight = att * local_ref[e, z]
            weight_ref[e, z] = weight
            here = place == e * slices
            proj = jnp.where(here, jnp.sum(weight * maps_ref[e, z], axis=1, keepdims=True), proj)
            whole = jnp.where(here, jnp.sum(weight, axis=1, keepdims=True), whole)
        return proj, whole

    zero = jnp.zeros((cells, elems * slices), F32)
    proj, whole = lax.fori_loop(0, slices, step, (zero, zero))
    out_ref[0] = proj
    out_ref[1] = whole
    out_ref[2] = pack_ref[0]
    out_ref[3] = pack_ref[1]
    out_ref[4] = pack_ref[2]


def dual_step(field, ahead, dual, last):
    step = 0.5 * (ahead - field)
    return jnp.where(last, 0.0, clip(step if dual is None else dual + step))


def tile_duals(tile, dual_x, dual_y, sub, lane, shape):
    cells, width = shape
    new_x = dual_step(tile, pltpu.roll(tile, cells - 1, axis=0), dual_x, sub == cells - 1)
    new_y = dual_step(tile, pltpu.roll(tile, width - 1, axis=1), dual_y, lane == width - 1)
    spread = pltpu.roll(new_x, 1, axis=0) - new_x + (pltpu.roll(new_y, 1, axis=1) - new_y)
    return new_x, new_y, spread


def first_dual_kernel(maps_ref, zahead_ref, zbehind_ref, *refs):
    elems, slices, cells, width = maps_ref.shape
    sides = beam_sides(cells)
    own_refs, refs = refs[: len(sides)], refs[len(sides) :]
    other_refs, refs = refs[: len(sides)], refs[len(sides) :]
    dual_z_ref, dual_x_ref, dual_y_ref, behind_ref, adj_ref, *edge_refs = refs
    count, rank = lax.axis_size("gz"), lax.axis_index("gz")
    sub = lax.broadcasted_iota(jnp.int32, (cells, width), 0)
    lane = lax.broadcasted_iota(jnp.int32, (cells, width), 1)
    for (row, sign, there), own, other, edge in zip(sides, own_refs, other_refs, edge_refs):
        edge[...] = clip(0.5 * face(own[...], other[...], sign, there))
    for e in range(elems):
        behind_ref[e] = jnp.where(rank > 0, clip(0.5 * (maps_ref[e, 0] - zbehind_ref[e])), 0.0)

    def step(z, behind):
        at_end = z == slices - 1
        zero_end = jnp.logical_and(at_end, rank == count - 1)
        duals = []
        for e in range(elems):
            tile = maps_ref[e, z]
            inner = maps_ref[e, jnp.minimum(z + 1, slices - 1)]
            ahead = jnp.where(at_end, zahead_ref[e], inner)
            dual_z = jnp.where(zero_end, 0.0, clip(0.5 * (ahead - tile)))
            dual_x, dual_y, spread = tile_duals(tile, None, None, sub, lane, (cells, width))
            dual_z_ref[e, z] = dual_z
            dual_x_ref[e, z] = dual_x
            dual_y_ref[e, z] = dual_y
            spread = spread + (behind[e] - dual_z)
            for (row, sign, there), edge in zip(sides, edge_refs):
                spread = spread + jnp.where(sub == row, sign * edge[pl.ds(e * slices + z, 1)], 0.0)
            adj_ref[e, z] = spread
            duals.append(dual_z)
        return tuple(duals)

    lax.fori_loop(0, slices, step, tuple(behind_ref[e] for e in range(elems)))


def by_rank(blocks, size):
    mine = lax.axis_index("path")
    ordered = []
    for rank in range(size):
        value = blocks[0]
        for s in range(1, size):
            value = jnp.where(lax.rem(mine - s + size, size) == rank, blocks[s], value)
        ordered.append(value)
    return ordered


def turned(pack, z):
    size = pack.shape[1]
    return pltpu.roll(pack, lax.rem(size - z, size), axis=1)


def join(ref):
    return jnp.concatenate([ref[e] for e in range(ref.shape[0])], axis=1)


def part(ref, pack):
    slices = ref.shape[2]
    for e in range(ref.shape[0]):
        ref[e] = pack[:, e * slices : (e + 1) * slices]


def first_update_kernel(total, size, maps_ref, weight_ref, adj_ref, side_ref, measured_ref, *refs):
    elems, slices, cells, width = maps_ref.shape
    sides = beam_sides(cells)
    pack_refs, refs = refs[:size], refs[size:]
    full_ref, cur_ref, ext_ref, dd_ref, yedge_ref, out_ref, emission_ref, zfirst_ref, zlast_ref, *face_refs = refs
    mine = lax.axis_index("path")
    pack_shape = (cells, elems * slices)
    pack_lane = lax.broadcasted_iota(jnp.int32, pack_shape, 1)
    proj, whole, strip = [by_rank([ref[i] for ref in pack_refs], size) for i in range(3)]
    far = jnp.zeros(pack_shape, jnp.bool_)
    for e in range(elems):
        inside = (pack_lane >= e * slices) & (pack_lane < (e + 1) * slices)
        far = far | (inside & (side_ref[e] != 0))
    below = [jnp.zeros(pack_shape, F32)]
    above = [jnp.zeros(pack_shape, F32)]
    for r in range(1, size):
        below.append(below[-1] + strip[r - 1])
        above.append(above[-1] + strip[size - r])
    factor = [jnp.exp(jnp.where(far, above[size - 1 - r], below[r]) * (-1.0 / total)) for r in range(size)]
    image = factor[0] * proj[0]
    weights = factor[0] * whole[0]
    own = factor[0]
    for r in range(1, size):
        image = image + factor[r] * proj[r]
        weights = weights + factor[r] * whole[r]
        own = jnp.where(mine == r, factor[r], own)
    sig = 1.0 / weights
    data_dual = sig * (image - join(measured_ref)) / (1.0 + sig)
    dd_ref[0] = data_dual
    dd_ref[1] = sig
    part(emission_ref, image * (1.0 / total))
    ahead, behind = pack_refs[size - 1], pack_refs[min(1, size - 1)]
    first, last = pack_refs[0][3], pack_refs[0][4]
    y_ahead = jnp.where(mine < size - 1, clip(0.5 * (ahead[3] - last)), 0.0)
    y_behind = jnp.where(mine > 0, clip(0.5 * (first - behind[4])), 0.0)
    yedge_ref[0] = y_ahead
    yedge_ref[1] = y_behind
    sub = lax.broadcasted_iota(jnp.int32, (cells, width), 0)
    lane = lax.broadcasted_iota(jnp.int32, (cells, width), 1)

    def step(z, packs):
        image, first, last = packs
        place = pack_lane - z
        own_z, dd_z, ahead_z, behind_z = [turned(p, z) for p in (own, data_dual, y_ahead, y_behind)]
        for e in range(elems):
            k = e * slices
            weight = weight_ref[e, z] * own_z[:, k : k + 1]
            full_ref[e, z] = weight
            tile = maps_ref[e, z]
            adj = adj_ref[e, z] - jnp.where(lane == width - 1, ahead_z[:, k : k + 1], 0.0)
            adj = adj + jnp.where(lane == 0, behind_z[:, k : k + 1], 0.0)
            new = jnp.maximum(tile - (weight * dd_z[:, k : k + 1] + adj) / (weight + 6.0), 0.0)
            ext = 2.0 * new - tile
            cur_ref[e, z] = new
            ext_ref[e, z] = ext
            here = place == k
            image = jnp.where(here, jnp.sum(weight * ext, axis=1, keepdims=True), image)
            first = jnp.where(here, ext[:, 0:1], first)
            last = jnp.where(here, ext[:, width - 1 : width], last)
            for ref, row in zip(face_refs, beam_rows(ext[0:1], ext[cells - 1 : cells])):
                ref[pl.ds(k + z, 1)] = row
        return image, first, last

    zero = jnp.zeros(pack_shape, F32)
    image, first, last = lax.fori_loop(0, slices, step, (zero, zero, zero))
    out_ref[0] = image
    out_ref[1] = first
    out_ref[2] = last
    for e in range(elems):
        zfirst_ref[e] = ext_ref[e, 0]
        zlast_ref[e] = ext_ref[e, slices - 1]


def second_dual_kernel(ext_ref, dual_z_ref, dual_x_ref, dual_y_ref, adj_ref):
    elems, slices, cells, width = ext_ref.shape
    sub = lax.broadcasted_iota(jnp.int32, (cells, width), 0)
    lane = lax.broadcasted_iota(jnp.int32, (cells, width), 1)

    def step(z, behind):
        at_end = z == slices - 1
        duals = []
        for e in range(elems):
            tile = ext_ref[e, z]
            ahead = ext_ref[e, jnp.minimum(z + 1, slices - 1)]
            dual_z = jnp.where(at_end, 0.0, clip(dual_z_ref[e, z] + 0.5 * (ahead - tile)))
            _, _, spread = tile_duals(tile, dual_x_ref[e, z], dual_y_ref[e, z], sub, lane, (cells, width))
            adj_ref[e, z] = spread + (behind[e] - dual_z)
            duals.append(dual_z)
        return tuple(duals)

    zero = jnp.zeros((cells, width), F32)
    lax.fori_loop(0, slices, step, (zero,) * elems)


def last_update_kernel(size, cur_ref, weight_ref, adj_ref, measured_ref, dd_ref, yedge_ref, zedge_ref, zbehind_ref,
                       zfirst_ref, zlast_ref, zother_ahead_ref, zother_behind_ref, *refs):
    elems, slices, cells, width = cur_ref.shape
    sides = beam_sides(cells)
    pack_refs, refs = refs[:size], refs[size:]
    edge_refs, refs = refs[: len(sides)], refs[len(sides) :]
    own_refs, refs = refs[: len(sides)], refs[len(sides) :]
    other_refs, refs = refs[: len(sides)], refs[len(sides) :]
    new_ref, dual_ref, zface_ref, *face_refs = refs
    mine = lax.axis_index("path")
    count, rank = lax.axis_size("gz"), lax.axis_index("gz")
    images = by_rank([ref[0] for ref in pack_refs], size)
    image = images[0]
    for r in range(1, size):
        image = image + images[r]
    sig = dd_ref[1]
    data_dual = (dd_ref[0] + sig * (image - join(measured_ref))) / (1.0 + sig)
    part(dual_ref, data_dual)
    ahead, behind = pack_refs[size - 1], pack_refs[min(1, size - 1)]
    first, last = pack_refs[0][1], pack_refs[0][2]
    y_ahead = jnp.where(mine < size - 1, clip(yedge_ref[0] + 0.5 * (ahead[1] - last)), 0.0)
    y_behind = jnp.where(mine > 0, clip(yedge_ref[1] + 0.5 * (first - behind[2])), 0.0)
    for (row, sign, there), edge, own, other, out in zip(sides, edge_refs, own_refs, other_refs, face_refs):
        out[...] = clip(edge[...] + 0.5 * face(own[...], other[...], sign, there)) * sign
    sub = lax.broadcasted_iota(jnp.int32, (cells, width), 0)
    lane = lax.broadcasted_iota(jnp.int32, (cells, width), 1)
    for e in range(elems):
        z_behind = clip(zbehind_ref[e] + 0.5 * (zfirst_ref[e] - zother_behind_ref[e]))
        z_ahead = clip(zedge_ref[e, slices - 1] + 0.5 * (zother_ahead_ref[e] - zlast_ref[e]))
        zface_ref[0, e] = jnp.where(rank > 0, z_behind, 0.0)
        zface_ref[1, e] = jnp.where(rank < count - 1, z_ahead, 0.0)

    def step(z, none):
        dd_z, ahead_z, behind_z = [turned(p, z) for p in (data_dual, y_ahead, y_behind)]
        for e in range(elems):
            k = e * slices
            weight = weight_ref[e, z]
            adj = adj_ref[e, z] + jnp.where(z == 0, zface_ref[0, e], 0.0)
            adj = adj - jnp.where(z == slices - 1, zface_ref[1, e], 0.0)
            adj = adj - jnp.where(lane == width - 1, ahead_z[:, k : k + 1], 0.0)
            adj = adj + jnp.where(lane == 0, behind_z[:, k : k + 1], 0.0)
            for (row, sign, there), out in zip(sides, face_refs):
                adj = adj + jnp.where(sub == row, out[pl.ds(k + z, 1)], 0.0)
            step = (weight * dd_z[:, k : k + 1] + adj) / (weight + 6.0)
            new_ref[e, z] = jnp.maximum(cur_ref[e, z] - step, 0.0)
        return none

    lax.fori_loop(0, slices, step, 0)


def shards(maps, measured, beta_table, view, kappa, line_of, side):
    elems, slices, cells, width = maps.shape
    total_x = cells * lax.axis_size("beam")
    total_y = width * lax.axis_size("path")
    size = lax.axis_size("path")
    block = f32(elems, slices, cells, width)
    plane = f32(elems, cells, width)
    rows = f32(elems * slices, width)
    faces = len(beam_sides(cells))
    measured = measured.transpose(0, 2, 1)
    kappa = kappa.T

    inside, slab, zfirst, zlast, *own = call(
        functools.partial(open_kernel, total_x),
        [maps, beta_table, view],
        [f32(slices, cells, width), f32(slices, width), plane, plane] + [rows] * faces,
        [VMEM, SMEM, SMEM],
    )
    carry = shifted(slab, "beam", 1)
    reach = 1
    while reach < lax.axis_size("beam") - 1:
        carry = carry + shifted(carry, "beam", reach)
        reach *= 2
    other = exchange_beam(own)
    zahead, zbehind = shifted(zfirst, "gz", -1), shifted(zlast, "gz", 1)
    local, pack = call(
        functools.partial(depth_kernel, total_y),
        [maps, kappa, line_of, side],
        [block, f32(3, cells, elems * slices)],
        [VMEM, SMEM, SMEM, SMEM],
        [
            pltpu.VMEM(maps.shape, F32),
            pltpu.VMEM((elems * slices * cells, 2 * width), jnp.bfloat16),
            pltpu.VMEM((elems * slices * cells, 2 * width), F32),
        ],
    )
    weight, pack = call(
        functools.partial(weight_kernel, total_x),
        [maps, inside, carry, local, pack],
        [block, f32(5, cells, elems * slices)],
        [VMEM] * 5,
    )
    packs = [pack] + around(pack, "path")
    dual_z, dual_x, dual_y, zdual, adj, *edge = call(
        first_dual_kernel,
        [maps, zahead, zbehind, *own, *other],
        [block, block, block, plane, block] + [rows] * faces,
        [VMEM] * (3 + 2 * faces),
    )
    weight, current, extrap, dd, yedge, pack, emission, zfirst, zlast, *own = call(
        functools.partial(first_update_kernel, total_y, size),
        [maps, weight, adj, side, measured, *packs],
        [block, block, block, f32(2, cells, elems * slices), f32(2, cells, elems * slices),
         f32(3, cells, elems * slices), f32(elems, cells, slices), plane, plane] + [rows] * faces,
        [VMEM, VMEM, VMEM, SMEM] + [VMEM] * (1 + size),
    )
    packs = [pack] + around(pack, "path")
    zahead, zbehind = shifted(zfirst, "gz", -1), shifted(zlast, "gz", 1)
    other = exchange_beam(own)
    (adj,) = call(second_dual_kernel, [extrap, dual_z, dual_x, dual_y], [block], [VMEM] * 4)
    current, data_dual = call(
        functools.partial(last_update_kernel, size),
        [current, weight, adj, measured, dd, yedge, dual_z, zdual, zfirst, zlast, zahead, zbehind,
         *packs, *edge, *own, *other],
        [block, f32(elems, cells, slices)],
        [VMEM] * (12 + size + 3 * faces),
        [pltpu.VMEM((2, elems, cells, width), F32)] + [pltpu.VMEM((elems * slices, width), F32)] * faces,
    )
    return emission.transpose(0, 2, 1), current, data_dual.transpose(0, 2, 1)


def solution(mesh):
    return jax.shard_map(
        shards,
        mesh=mesh,
        in_specs=(P(None, "gz", "beam", "path"), P(None, "gz", "beam"), P(), P(), P(), P(), P()),
        out_specs=(P(None, "gz", "beam"), P(None, "gz", "beam", "path"), P(None, "gz", "beam")),
        check_vma=False,
    )
```

```python
import functools

import jax
import jax.numpy as jnp
from jax import lax
from jax.experimental import pallas as pl
from jax.experimental.pallas import tpu as pltpu
from jax.sharding import PartitionSpec as P

ITERS = 2
LAM = 0.1
F32 = jnp.float32
VMEM = pltpu.VMEM
SMEM = pltpu.SMEM
UNROLL = 4
VMEM_LIMIT = 32 * 1024 * 1024


def clip(value):
    return jnp.clip(value, -LAM, LAM)


def call(body, ins, outs, spaces, scratch=(), flops=1_000_000):
    specs = [pl.BlockSpec(memory_space=space) for space in spaces]
    moved = sum(a.size * 4 for a in ins) + sum(o.size * 4 for o in outs)
    return pl.pallas_call(
        body,
        out_shape=outs,
        in_specs=specs,
        out_specs=[pl.BlockSpec(memory_space=VMEM)] * len(outs),
        scratch_shapes=list(scratch),
        compiler_params=pltpu.CompilerParams(vmem_limit_bytes=VMEM_LIMIT),
        cost_estimate=pl.CostEstimate(flops=flops, bytes_accessed=moved, transcendentals=0),
    )(*ins)


def f32(*shape):
    return jax.ShapeDtypeStruct(shape, F32)


def shifted(block, axis, distance):
    n = lax.axis_size(axis)
    return lax.ppermute(block, axis, [((i - distance) % n, i) for i in range(n)])


def swapped(block, axis, start):
    n = lax.axis_size(axis)
    route = {i: i for i in range(n)}
    for i in range(start, n - 1, 2):
        route[i], route[i + 1] = i + 1, i
    return lax.ppermute(block, axis, sorted(route.items()))


def pair_order(ahead, behind):
    even = lax.rem(lax.axis_index("gz"), 2) == 0
    return jnp.where(even, ahead, behind), jnp.where(even, behind, ahead)


def around(block, axis):
    n = lax.axis_size(axis)
    return [shifted(block, axis, s) for s in range(1, n)]


def beam_sides(cells):
    count, rank = lax.axis_size("beam"), lax.axis_index("beam")
    if count == 2:
        return [
            (
                jnp.where(rank == 0, cells - 1, 0),
                jnp.where(rank == 0, F32(-1.0), F32(1.0)),
                None,
            )
        ]
    return [(cells - 1, F32(-1.0), rank < count - 1), (0, F32(1.0), rank > 0)]


def beam_rows(first, last):
    count, rank = lax.axis_size("beam"), lax.axis_index("beam")
    if count == 2:
        return [jnp.where(rank == 0, last, first)]
    return [last, first]


def face(own, other, sign, there):
    step = (own - other) * sign
    return step if there is None else jnp.where(there, step, 0.0)


def exchange_beam(rows):
    if lax.axis_size("beam") == 2:
        return [lax.ppermute(rows[0], "beam", [(0, 1), (1, 0)])]
    return [shifted(rows[1], "beam", -1), shifted(rows[0], "beam", 1)]


def open_kernel(total, source_ref, *refs):
    small, refs = refs[:5], refs[5:]
    maps_ref, inside_ref, coef_ref, zone_ref, ztwo_ref, *refs = refs
    elems, slices, cells, width = maps_ref.shape
    faces = len(beam_sides(cells))
    face_refs, refs = refs[:faces], refs[faces:]
    beta_ref, view_ref, kappa_ref, line_ref, side_ref, sems = refs
    fetch = [pltpu.make_async_copy(source_ref, maps_ref, sems.at[0])]
    for i, (ref, kept) in enumerate(zip(small, (beta_ref, view_ref, kappa_ref, line_ref, side_ref))):
        fetch.append(pltpu.make_async_copy(ref, kept, sems.at[i + 1]))
    for copy in fetch:
        copy.start()
    for copy in fetch[1:]:
        copy.wait()
    for e in range(elems):
        line = line_ref[e]
        for f in range(elems):
            coef_ref[e * elems + f : e * elems + f + 1] = jnp.full((1, width), kappa_ref[f, line])
        coef_ref[elems * elems + e : elems * elems + e + 1] = jnp.full((1, width), side_ref[e].astype(F32))
    fetch[0].wait()
    view = view_ref[0]
    beta = [beta_ref[view, e] for e in range(elems)]
    sub = lax.broadcasted_iota(jnp.int32, maps_ref.shape[2:], 0)
    for z in range(slices):
        tiles = [maps_ref[e, z] for e in range(elems)]
        mu = beta[0] * tiles[0]
        for e in range(1, elems):
            mu = mu + beta[e] * tiles[e]
        run = mu
        reach = 1
        while reach < cells:
            run = run + jnp.where(sub >= reach, pltpu.roll(run, reach, axis=0), 0.0)
            reach *= 2
        inside_ref[z] = jnp.where(sub >= 1, pltpu.roll(run, 1, axis=0), 0.0)
        face_refs[0][elems * slices + z : elems * slices + z + 1] = run[cells - 1 : cells]
        for e in range(elems):
            rows = beam_rows(tiles[e][0:1], tiles[e][cells - 1 : cells])
            for ref, row in zip(face_refs, rows):
                ref[e * slices + z : e * slices + z + 1] = row
    for e in range(elems):
        zone_ref[e], ztwo_ref[e] = pair_order(maps_ref[e, slices - 1], maps_ref[e, 0])


def depth_kernel(total, maps_ref, coef_ref, local_ref, pack_ref, mu_ref, parts_ref, sums_ref):
    elems, slices, cells, width = maps_ref.shape
    rows = slices * cells
    row = lax.broadcasted_iota(jnp.int32, (2 * width, 2 * width), 0)
    col = lax.broadcasted_iota(jnp.int32, (2 * width, 2 * width), 1)
    row = jnp.where(row >= width, row - width, row)
    table = jnp.where((row < col) | (col >= width), 1.0, 0.0).astype(jnp.bfloat16)
    for e in range(elems):
        mu = coef_ref[e * elems : e * elems + 1][None] * maps_ref[0]
        for f in range(1, elems):
            mu = mu + coef_ref[e * elems + f : e * elems + f + 1][None] * maps_ref[f]
        mu_ref[e] = mu
        flat = mu.reshape(rows, width)
        high = flat.astype(jnp.bfloat16)
        low = (flat - high.astype(F32)).astype(jnp.bfloat16)
        parts_ref[e * rows : (e + 1) * rows, 0:width] = high
        parts_ref[e * rows : (e + 1) * rows, width:] = low
    sums_ref[...] = jnp.dot(parts_ref[...], table, preferred_element_type=F32)
    lane = lax.broadcasted_iota(jnp.int32, (cells, elems * slices), 1)
    forward = [coef_ref[pl.ds(elems * elems + e, 1)] == 0.0 for e in range(elems)]
    scale = -1.0 / total

    def step(z, packs):
        strip, first, last = packs
        place = lane - z
        for e in range(elems):
            at = pl.ds(pl.multiple_of((e * slices + z) * cells, cells), cells)
            before = sums_ref[at, 0:width]
            whole = sums_ref[at, width:]
            after = whole - before - mu_ref[e, z]
            local_ref[e, z] = jnp.exp(jnp.where(forward[e], before, after) * scale)
            here = place == e * slices
            tile = maps_ref[e, z]
            strip = jnp.where(here, whole[:, 0:1], strip)
            first = jnp.where(here, tile[:, 0:1], first)
            last = jnp.where(here, tile[:, width - 1 : width], last)
        return strip, first, last

    zero = jnp.zeros((cells, elems * slices), F32)
    strip, first, last = lax.fori_loop(0, slices, step, (zero, zero, zero), unroll=UNROLL)
    pack_ref[0] = strip
    pack_ref[1] = first
    pack_ref[2] = last


def weight_kernel(total, skip, maps_ref, inside_ref, carry_ref, local_ref, pack_ref, weight_ref, out_ref):
    elems, slices, cells, width = maps_ref.shape
    lane = lax.broadcasted_iota(jnp.int32, (cells, elems * slices), 1)
    there = lax.axis_index("beam") > 0
    scale = -1.0 / total

    def step(z, packs):
        proj, whole = packs
        place = lane - z
        carry = jnp.where(there, carry_ref[pl.ds(skip + z, 1)], 0.0)
        att = jnp.exp((inside_ref[z] + carry) * scale)
        for e in range(elems):
            weight = att * local_ref[e, z]
            weight_ref[e, z] = weight
            here = place == e * slices
            proj = jnp.where(here, jnp.sum(weight * maps_ref[e, z], axis=1, keepdims=True), proj)
            whole = jnp.where(here, jnp.sum(weight, axis=1, keepdims=True), whole)
        return proj, whole

    zero = jnp.zeros((cells, elems * slices), F32)
    proj, whole = lax.fori_loop(0, slices, step, (zero, zero), unroll=UNROLL)
    out_ref[0] = proj
    out_ref[1] = whole
    out_ref[2] = pack_ref[0]
    out_ref[3] = pack_ref[1]
    out_ref[4] = pack_ref[2]


def dual_step(field, ahead, dual, last):
    step = 0.5 * (ahead - field)
    return jnp.where(last, 0.0, clip(step if dual is None else dual + step))


def tile_duals(tile, dual_x, dual_y, sub, lane, shape):
    cells, width = shape
    new_x = dual_step(tile, pltpu.roll(tile, cells - 1, axis=0), dual_x, sub == cells - 1)
    new_y = dual_step(tile, pltpu.roll(tile, width - 1, axis=1), dual_y, lane == width - 1)
    spread = pltpu.roll(new_x, 1, axis=0) - new_x + (pltpu.roll(new_y, 1, axis=1) - new_y)
    return new_x, new_y, spread


def first_dual_kernel(maps_ref, zone_ref, ztwo_ref, *refs):
    elems, slices, cells, width = maps_ref.shape
    sides = beam_sides(cells)
    own_refs, refs = refs[: len(sides)], refs[len(sides) :]
    other_refs, refs = refs[: len(sides)], refs[len(sides) :]
    dual_z_ref, dual_x_ref, dual_y_ref, behind_ref, adj_ref, *edge_refs, ahead_ref = refs
    count, rank = lax.axis_size("gz"), lax.axis_index("gz")
    sub = lax.broadcasted_iota(jnp.int32, (cells, width), 0)
    lane = lax.broadcasted_iota(jnp.int32, (cells, width), 1)
    for (row, sign, there), own, other, edge in zip(sides, own_refs, other_refs, edge_refs):
        rows = pl.ds(0, elems * slices)
        edge[...] = clip(0.5 * face(own[rows], other[rows], sign, there))
    for e in range(elems):
        ahead, behind = pair_order(zone_ref[e], ztwo_ref[e])
        ahead_ref[e] = ahead
        behind_ref[e] = jnp.where(rank > 0, clip(0.5 * (maps_ref[e, 0] - behind)), 0.0)

    def step(z, behind):
        at_end = z == slices - 1
        zero_end = jnp.logical_and(at_end, rank == count - 1)
        duals = []
        for e in range(elems):
            tile = maps_ref[e, z]
            inner = maps_ref[e, jnp.minimum(z + 1, slices - 1)]
            ahead = jnp.where(at_end, ahead_ref[e], inner)
            dual_z = jnp.where(zero_end, 0.0, clip(0.5 * (ahead - tile)))
            dual_x, dual_y, spread = tile_duals(tile, None, None, sub, lane, (cells, width))
            dual_z_ref[e, z] = dual_z
            dual_x_ref[e, z] = dual_x
            dual_y_ref[e, z] = dual_y
            spread = spread + (behind[e] - dual_z)
            for (row, sign, there), edge in zip(sides, edge_refs):
                spread = spread + jnp.where(sub == row, sign * edge[pl.ds(e * slices + z, 1)], 0.0)
            adj_ref[e, z] = spread
            duals.append(dual_z)
        return tuple(duals)

    lax.fori_loop(0, slices, step, tuple(behind_ref[e] for e in range(elems)), unroll=UNROLL)


def by_rank(blocks, size):
    mine = lax.axis_index("path")
    ordered = []
    for rank in range(size):
        value = blocks[0]
        for s in range(1, size):
            value = jnp.where(lax.rem(mine - s + size, size) == rank, blocks[s], value)
        ordered.append(value)
    return ordered


def turned(pack, z):
    size = pack.shape[1]
    return pltpu.roll(pack, lax.rem(size - z, size), axis=1)


def join(ref):
    return jnp.concatenate([ref[e] for e in range(ref.shape[0])], axis=1)


def part(ref, pack):
    slices = ref.shape[2]
    for e in range(ref.shape[0]):
        ref[e] = pack[:, e * slices : (e + 1) * slices]


def first_update_kernel(total, size, maps_ref, weight_ref, adj_ref, coef_ref, measured_ref, *refs):
    elems, slices, cells, width = maps_ref.shape
    sides = beam_sides(cells)
    pack_refs, refs = refs[:size], refs[size:]
    full_ref, cur_ref, ext_ref, dd_ref, yedge_ref, out_ref, emission_ref, zone_ref, ztwo_ref, *face_refs = refs
    mine = lax.axis_index("path")
    pack_shape = (cells, elems * slices)
    pack_lane = lax.broadcasted_iota(jnp.int32, pack_shape, 1)
    proj, whole, strip = [by_rank([ref[i] for ref in pack_refs], size) for i in range(3)]
    far = jnp.zeros(pack_shape, jnp.bool_)
    for e in range(elems):
        inside = (pack_lane >= e * slices) & (pack_lane < (e + 1) * slices)
        far = far | (inside & (coef_ref[elems * elems + e : elems * elems + e + 1][:, 0:1] != 0.0))
    below = [jnp.zeros(pack_shape, F32)]
    above = [jnp.zeros(pack_shape, F32)]
    for r in range(1, size):
        below.append(below[-1] + strip[r - 1])
        above.append(above[-1] + strip[size - r])
    factor = [jnp.exp(jnp.where(far, above[size - 1 - r], below[r]) * (-1.0 / total)) for r in range(size)]
    image = factor[0] * proj[0]
    weights = factor[0] * whole[0]
    own = factor[0]
    for r in range(1, size):
        image = image + factor[r] * proj[r]
        weights = weights + factor[r] * whole[r]
        own = jnp.where(mine == r, factor[r], own)
    sig = 1.0 / weights
    data_dual = sig * (image - join(measured_ref)) / (1.0 + sig)
    dd_ref[0] = data_dual
    dd_ref[1] = sig
    part(emission_ref, image * (1.0 / total))
    ahead, behind = pack_refs[size - 1], pack_refs[min(1, size - 1)]
    first, last = pack_refs[0][3], pack_refs[0][4]
    y_ahead = jnp.where(mine < size - 1, clip(0.5 * (ahead[3] - last)), 0.0)
    y_behind = jnp.where(mine > 0, clip(0.5 * (first - behind[4])), 0.0)
    yedge_ref[0] = y_ahead
    yedge_ref[1] = y_behind
    sub = lax.broadcasted_iota(jnp.int32, (cells, width), 0)
    lane = lax.broadcasted_iota(jnp.int32, (cells, width), 1)

    def step(z, packs):
        image, first, last = packs
        place = pack_lane - z
        own_z, dd_z, ahead_z, behind_z = [turned(p, z) for p in (own, data_dual, y_ahead, y_behind)]
        for e in range(elems):
            k = e * slices
            weight = weight_ref[e, z] * own_z[:, k : k + 1]
            full_ref[e, z] = weight
            tile = maps_ref[e, z]
            adj = adj_ref[e, z] - jnp.where(lane == width - 1, ahead_z[:, k : k + 1], 0.0)
            adj = adj + jnp.where(lane == 0, behind_z[:, k : k + 1], 0.0)
            new = jnp.maximum(tile - (weight * dd_z[:, k : k + 1] + adj) / (weight + 6.0), 0.0)
            ext = 2.0 * new - tile
            cur_ref[e, z] = new
            ext_ref[e, z] = ext
            here = place == k
            image = jnp.where(here, jnp.sum(weight * ext, axis=1, keepdims=True), image)
            first = jnp.where(here, ext[:, 0:1], first)
            last = jnp.where(here, ext[:, width - 1 : width], last)
            for ref, row in zip(face_refs, beam_rows(ext[0:1], ext[cells - 1 : cells])):
                ref[pl.ds(k + z, 1)] = row
        return image, first, last

    zero = jnp.zeros(pack_shape, F32)
    image, first, last = lax.fori_loop(0, slices, step, (zero, zero, zero), unroll=UNROLL)
    out_ref[0] = image
    out_ref[1] = first
    out_ref[2] = last
    for e in range(elems):
        zone_ref[e], ztwo_ref[e] = pair_order(ext_ref[e, slices - 1], ext_ref[e, 0])


def second_dual_kernel(ext_ref, dual_z_ref, dual_x_ref, dual_y_ref, adj_ref):
    elems, slices, cells, width = ext_ref.shape
    sub = lax.broadcasted_iota(jnp.int32, (cells, width), 0)
    lane = lax.broadcasted_iota(jnp.int32, (cells, width), 1)

    def step(z, behind):
        at_end = z == slices - 1
        duals = []
        for e in range(elems):
            tile = ext_ref[e, z]
            ahead = ext_ref[e, jnp.minimum(z + 1, slices - 1)]
            dual_z = jnp.where(at_end, 0.0, clip(dual_z_ref[e, z] + 0.5 * (ahead - tile)))
            _, _, spread = tile_duals(tile, dual_x_ref[e, z], dual_y_ref[e, z], sub, lane, (cells, width))
            adj_ref[e, z] = spread + (behind[e] - dual_z)
            duals.append(dual_z)
        return tuple(duals)

    zero = jnp.zeros((cells, width), F32)
    lax.fori_loop(0, slices, step, (zero,) * elems, unroll=UNROLL)


def last_update_kernel(size, cur_ref, ext_ref, weight_ref, adj_ref, measured_ref, dd_ref, yedge_ref, zedge_ref,
                       zbehind_ref, zone_ref, ztwo_ref, *refs):
    elems, slices, cells, width = cur_ref.shape
    sides = beam_sides(cells)
    pack_refs, refs = refs[:size], refs[size:]
    edge_refs, refs = refs[: len(sides)], refs[len(sides) :]
    own_refs, refs = refs[: len(sides)], refs[len(sides) :]
    other_refs, refs = refs[: len(sides)], refs[len(sides) :]
    new_ref, dual_ref, zface_ref, *face_refs = refs
    mine = lax.axis_index("path")
    count, rank = lax.axis_size("gz"), lax.axis_index("gz")
    images = by_rank([ref[0] for ref in pack_refs], size)
    image = images[0]
    for r in range(1, size):
        image = image + images[r]
    sig = dd_ref[1]
    data_dual = (dd_ref[0] + sig * (image - join(measured_ref))) / (1.0 + sig)
    part(dual_ref, data_dual)
    ahead, behind = pack_refs[size - 1], pack_refs[min(1, size - 1)]
    first, last = pack_refs[0][1], pack_refs[0][2]
    y_ahead = jnp.where(mine < size - 1, clip(yedge_ref[0] + 0.5 * (ahead[1] - last)), 0.0)
    y_behind = jnp.where(mine > 0, clip(yedge_ref[1] + 0.5 * (first - behind[2])), 0.0)
    for (row, sign, there), edge, own, other, out in zip(sides, edge_refs, own_refs, other_refs, face_refs):
        out[...] = clip(edge[...] + 0.5 * face(own[...], other[...], sign, there)) * sign
    sub = lax.broadcasted_iota(jnp.int32, (cells, width), 0)
    lane = lax.broadcasted_iota(jnp.int32, (cells, width), 1)
    for e in range(elems):
        other_ahead, other_behind = pair_order(zone_ref[e], ztwo_ref[e])
        z_behind = clip(zbehind_ref[e] + 0.5 * (ext_ref[e, 0] - other_behind))
        z_ahead = clip(zedge_ref[e, slices - 1] + 0.5 * (other_ahead - ext_ref[e, slices - 1]))
        zface_ref[0, e] = jnp.where(rank > 0, z_behind, 0.0)
        zface_ref[1, e] = jnp.where(rank < count - 1, z_ahead, 0.0)

    def step(z, none):
        dd_z, ahead_z, behind_z = [turned(p, z) for p in (data_dual, y_ahead, y_behind)]
        for e in range(elems):
            k = e * slices
            weight = weight_ref[e, z]
            adj = adj_ref[e, z] + jnp.where(z == 0, zface_ref[0, e], 0.0)
            adj = adj - jnp.where(z == slices - 1, zface_ref[1, e], 0.0)
            adj = adj - jnp.where(lane == width - 1, ahead_z[:, k : k + 1], 0.0)
            adj = adj + jnp.where(lane == 0, behind_z[:, k : k + 1], 0.0)
            for (row, sign, there), out in zip(sides, face_refs):
                adj = adj + jnp.where(sub == row, out[pl.ds(k + z, 1)], 0.0)
            step = (weight * dd_z[:, k : k + 1] + adj) / (weight + 6.0)
            new_ref[e, z] = jnp.maximum(cur_ref[e, z] - step, 0.0)
        return none

    lax.fori_loop(0, slices, step, 0, unroll=UNROLL)


def shards(maps, measured, beta_table, view, kappa, line_of, side):
    elems, slices, cells, width = maps.shape
    total_x = cells * lax.axis_size("beam")
    total_y = width * lax.axis_size("path")
    size = lax.axis_size("path")
    block = f32(elems, slices, cells, width)
    plane = f32(elems, cells, width)
    rows = f32(elems * slices, width)
    faces = len(beam_sides(cells))
    measured = measured.transpose(0, 2, 1)
    kappa = kappa.T

    tall = f32((elems + 1) * slices, width)
    maps, inside, coef, zone, ztwo, *own = call(
        functools.partial(open_kernel, total_x),
        [maps, beta_table, view, kappa, line_of, side],
        [block, f32(slices, cells, width), f32(elems * elems + elems, width), plane, plane, tall] + [rows] * (faces - 1),
        [pltpu.HBM] * 6,
        [
            pltpu.SMEM(beta_table.shape, F32),
            pltpu.SMEM(view.shape, jnp.int32),
            pltpu.SMEM(kappa.shape, F32),
            pltpu.SMEM(line_of.shape, jnp.int32),
            pltpu.SMEM(side.shape, jnp.int32),
            pltpu.SemaphoreType.DMA((6,)),
        ],
    )
    other = exchange_beam(own)
    carry, skip = other[-1], elems * slices
    beams = lax.axis_size("beam")
    if beams > 2:
        carry, skip = carry[skip:], 0
        reach = 1
        while reach < beams - 1:
            far = lax.axis_index("beam") > reach
            carry = carry + jnp.where(far, shifted(carry, "beam", reach), 0.0)
            reach *= 2
    zone, ztwo = swapped(zone, "gz", 0), swapped(ztwo, "gz", 1)
    local, pack = call(
        functools.partial(depth_kernel, total_y),
        [maps, coef],
        [block, f32(3, cells, elems * slices)],
        [VMEM] * 2,
        [
            pltpu.VMEM(maps.shape, F32),
            pltpu.VMEM((elems * slices * cells, 2 * width), jnp.bfloat16),
            pltpu.VMEM((elems * slices * cells, 2 * width), F32),
        ],
    )
    weight, pack = call(
        functools.partial(weight_kernel, total_x, skip),
        [maps, inside, carry, local, pack],
        [block, f32(5, cells, elems * slices)],
        [VMEM] * 5,
    )
    packs = [pack] + around(pack, "path")
    dual_z, dual_x, dual_y, zdual, adj, *edge = call(
        first_dual_kernel,
        [maps, zone, ztwo, *own, *other],
        [block, block, block, plane, block] + [rows] * faces,
        [VMEM] * (3 + 2 * faces),
        [pltpu.VMEM(plane.shape, F32)],
    )
    weight, current, extrap, dd, yedge, pack, emission, zone, ztwo, *own = call(
        functools.partial(first_update_kernel, total_y, size),
        [maps, weight, adj, coef, measured, *packs],
        [block, block, block, f32(2, cells, elems * slices), f32(2, cells, elems * slices),
         f32(3, cells, elems * slices), f32(elems, cells, slices), plane, plane] + [rows] * faces,
        [VMEM] * (5 + size),
    )
    packs = [pack] + around(pack, "path")
    zone, ztwo = swapped(zone, "gz", 0), swapped(ztwo, "gz", 1)
    other = exchange_beam(own)
    (adj,) = call(second_dual_kernel, [extrap, dual_z, dual_x, dual_y], [block], [VMEM] * 4)
    current, data_dual = call(
        functools.partial(last_update_kernel, size),
        [current, extrap, weight, adj, measured, dd, yedge, dual_z, zdual, zone, ztwo, *packs, *edge, *own, *other],
        [block, f32(elems, cells, slices)],
        [VMEM] * (11 + size + 3 * faces),
        [pltpu.VMEM((2, elems, cells, width), F32)] + [pltpu.VMEM((elems * slices, width), F32)] * faces,
    )
    return emission.transpose(0, 2, 1), current, data_dual.transpose(0, 2, 1)


def solution(mesh):
    return jax.shard_map(
        shards,
        mesh=mesh,
        in_specs=(P(None, "gz", "beam", "path"), P(None, "gz", "beam"), P(), P(), P(), P(), P()),
        out_specs=(P(None, "gz", "beam"), P(None, "gz", "beam", "path"), P(None, "gz", "beam")),
        check_vma=False,
    )
```

```python
import functools

import jax
import jax.numpy as jnp
from jax import lax
from jax.experimental import pallas as pl
from jax.experimental.pallas import tpu as pltpu
from jax.sharding import PartitionSpec as P

ITERS = 2
LAM = 0.1
F32 = jnp.float32
VMEM = pltpu.VMEM
SMEM = pltpu.SMEM
UNROLL = 4
VMEM_LIMIT = 32 * 1024 * 1024


def clip(value):
    return jnp.clip(value, -LAM, LAM)


def call(body, ins, outs, spaces, scratch=(), flops=1_000_000):
    specs = [pl.BlockSpec(memory_space=space) for space in spaces]
    moved = sum(a.size * 4 for a in ins) + sum(o.size * 4 for o in outs)
    return pl.pallas_call(
        body,
        out_shape=outs,
        in_specs=specs,
        out_specs=[pl.BlockSpec(memory_space=VMEM)] * len(outs),
        scratch_shapes=list(scratch),
        compiler_params=pltpu.CompilerParams(vmem_limit_bytes=VMEM_LIMIT),
        cost_estimate=pl.CostEstimate(flops=flops, bytes_accessed=moved, transcendentals=0),
    )(*ins)


def f32(*shape):
    return jax.ShapeDtypeStruct(shape, F32)


def shifted(block, axis, distance):
    n = lax.axis_size(axis)
    return lax.ppermute(block, axis, [((i - distance) % n, i) for i in range(n)])


def swapped(block, axis, start):
    n = lax.axis_size(axis)
    route = {i: i for i in range(n)}
    for i in range(start, n - 1, 2):
        route[i], route[i + 1] = i + 1, i
    return lax.ppermute(block, axis, sorted(route.items()))


def pair_order(ahead, behind):
    even = lax.rem(lax.axis_index("gz"), 2) == 0
    return jnp.where(even, ahead, behind), jnp.where(even, behind, ahead)


def around(copies, axis):
    return lax.all_to_all(copies, axis, 0, 0, tiled=True)


def beam_sides(cells):
    count, rank = lax.axis_size("beam"), lax.axis_index("beam")
    if count == 2:
        return [
            (
                jnp.where(rank == 0, cells - 1, 0),
                jnp.where(rank == 0, F32(-1.0), F32(1.0)),
                None,
            )
        ]
    return [(cells - 1, F32(-1.0), rank < count - 1), (0, F32(1.0), rank > 0)]


def beam_rows(first, last):
    count, rank = lax.axis_size("beam"), lax.axis_index("beam")
    if count == 2:
        return [jnp.where(rank == 0, last, first)]
    return [last, first]


def face(own, other, sign, there):
    step = (own - other) * sign
    return step if there is None else jnp.where(there, step, 0.0)


def exchange_beam(rows):
    if lax.axis_size("beam") == 2:
        return [lax.ppermute(rows[0], "beam", [(0, 1), (1, 0)])]
    return [shifted(rows[1], "beam", -1), shifted(rows[0], "beam", 1)]


def open_kernel(total, view_ref, source_ref, *refs):
    small, refs = refs[:4], refs[4:]
    maps_ref, inside_ref, coef_ref, zone_ref, ztwo_ref, *refs = refs
    elems, slices, cells, width = maps_ref.shape
    faces = len(beam_sides(cells))
    face_refs, refs = refs[:faces], refs[faces:]
    beta_ref, kappa_ref, line_ref, side_ref, sems = refs
    fetch = [pltpu.make_async_copy(source_ref, maps_ref, sems.at[0])]
    for i, (ref, kept) in enumerate(zip(small, (beta_ref, kappa_ref, line_ref, side_ref))):
        fetch.append(pltpu.make_async_copy(ref, kept, sems.at[i + 1]))
    for copy in fetch:
        copy.start()
    for copy in fetch[1:]:
        copy.wait()
    for e in range(elems):
        line = line_ref[e]
        for f in range(elems):
            coef_ref[e * elems + f : e * elems + f + 1] = jnp.full((1, width), kappa_ref[f, line])
        coef_ref[elems * elems + e : elems * elems + e + 1] = jnp.full((1, width), side_ref[e].astype(F32))
    fetch[0].wait()
    view = view_ref[0]
    beta = [beta_ref[view, e] for e in range(elems)]
    sub = lax.broadcasted_iota(jnp.int32, maps_ref.shape[2:], 0)
    for z in range(slices):
        tiles = [maps_ref[e, z] for e in range(elems)]
        mu = beta[0] * tiles[0]
        for e in range(1, elems):
            mu = mu + beta[e] * tiles[e]
        run = mu
        reach = 1
        while reach < cells:
            run = run + jnp.where(sub >= reach, pltpu.roll(run, reach, axis=0), 0.0)
            reach *= 2
        inside_ref[z] = jnp.where(sub >= 1, pltpu.roll(run, 1, axis=0), 0.0)
        face_refs[0][elems * slices + z : elems * slices + z + 1] = run[cells - 1 : cells]
        for e in range(elems):
            rows = beam_rows(tiles[e][0:1], tiles[e][cells - 1 : cells])
            for ref, row in zip(face_refs, rows):
                ref[e * slices + z : e * slices + z + 1] = row
    for e in range(elems):
        zone_ref[e], ztwo_ref[e] = pair_order(maps_ref[e, slices - 1], maps_ref[e, 0])


def depth_kernel(total, maps_ref, coef_ref, local_ref, pack_ref, mu_ref, parts_ref, sums_ref):
    elems, slices, cells, width = maps_ref.shape
    rows = slices * cells
    row = lax.broadcasted_iota(jnp.int32, (2 * width, 2 * width), 0)
    col = lax.broadcasted_iota(jnp.int32, (2 * width, 2 * width), 1)
    row = jnp.where(row >= width, row - width, row)
    table = jnp.where((row < col) | (col >= width), 1.0, 0.0).astype(jnp.bfloat16)
    for e in range(elems):
        mu = coef_ref[e * elems : e * elems + 1][None] * maps_ref[0]
        for f in range(1, elems):
            mu = mu + coef_ref[e * elems + f : e * elems + f + 1][None] * maps_ref[f]
        mu_ref[e] = mu
        flat = mu.reshape(rows, width)
        high = flat.astype(jnp.bfloat16)
        low = (flat - high.astype(F32)).astype(jnp.bfloat16)
        parts_ref[e * rows : (e + 1) * rows, 0:width] = high
        parts_ref[e * rows : (e + 1) * rows, width:] = low
    sums_ref[...] = jnp.dot(parts_ref[...], table, preferred_element_type=F32)
    lane = lax.broadcasted_iota(jnp.int32, (cells, elems * slices), 1)
    forward = [coef_ref[pl.ds(elems * elems + e, 1)] == 0.0 for e in range(elems)]
    scale = -1.0 / total

    def step(z, packs):
        strip, first, last = packs
        place = lane - z
        for e in range(elems):
            at = pl.ds(pl.multiple_of((e * slices + z) * cells, cells), cells)
            before = sums_ref[at, 0:width]
            whole = sums_ref[at, width:]
            after = whole - before - mu_ref[e, z]
            local_ref[e, z] = jnp.exp(jnp.where(forward[e], before, after) * scale)
            here = place == e * slices
            tile = maps_ref[e, z]
            strip = jnp.where(here, whole[:, 0:1], strip)
            first = jnp.where(here, tile[:, 0:1], first)
            last = jnp.where(here, tile[:, width - 1 : width], last)
        return strip, first, last

    zero = jnp.zeros((cells, elems * slices), F32)
    strip, first, last = lax.fori_loop(0, slices, step, (zero, zero, zero), unroll=UNROLL)
    pack_ref[0] = strip
    pack_ref[1] = first
    pack_ref[2] = last


def weight_kernel(total, skip, maps_ref, inside_ref, carry_ref, local_ref, pack_ref, weight_ref, out_ref):
    elems, slices, cells, width = maps_ref.shape
    lane = lax.broadcasted_iota(jnp.int32, (cells, elems * slices), 1)
    there = lax.axis_index("beam") > 0
    scale = -1.0 / total

    def step(z, packs):
        proj, whole = packs
        place = lane - z
        carry = jnp.where(there, carry_ref[pl.ds(skip + z, 1)], 0.0)
        att = jnp.exp((inside_ref[z] + carry) * scale)
        for e in range(elems):
            weight = att * local_ref[e, z]
            weight_ref[e, z] = weight
            here = place == e * slices
            proj = jnp.where(here, jnp.sum(weight * maps_ref[e, z], axis=1, keepdims=True), proj)
            whole = jnp.where(here, jnp.sum(weight, axis=1, keepdims=True), whole)
        return proj, whole

    zero = jnp.zeros((cells, elems * slices), F32)
    proj, whole = lax.fori_loop(0, slices, step, (zero, zero), unroll=UNROLL)
    for copy in range(out_ref.shape[0]):
        out_ref[copy, 0] = proj
        out_ref[copy, 1] = whole
        out_ref[copy, 2] = pack_ref[0]
        out_ref[copy, 3] = pack_ref[1]
        out_ref[copy, 4] = pack_ref[2]


def dual_step(field, ahead, dual, last):
    step = 0.5 * (ahead - field)
    return jnp.where(last, 0.0, clip(step if dual is None else dual + step))


def tile_duals(tile, dual_x, dual_y, sub, lane, shape):
    cells, width = shape
    new_x = dual_step(tile, pltpu.roll(tile, cells - 1, axis=0), dual_x, sub == cells - 1)
    new_y = dual_step(tile, pltpu.roll(tile, width - 1, axis=1), dual_y, lane == width - 1)
    spread = pltpu.roll(new_x, 1, axis=0) - new_x + (pltpu.roll(new_y, 1, axis=1) - new_y)
    return new_x, new_y, spread


def first_dual_kernel(maps_ref, zone_ref, ztwo_ref, *refs):
    elems, slices, cells, width = maps_ref.shape
    sides = beam_sides(cells)
    own_refs, refs = refs[: len(sides)], refs[len(sides) :]
    other_refs, refs = refs[: len(sides)], refs[len(sides) :]
    dual_z_ref, dual_x_ref, dual_y_ref, behind_ref, adj_ref, *edge_refs, ahead_ref = refs
    count, rank = lax.axis_size("gz"), lax.axis_index("gz")
    sub = lax.broadcasted_iota(jnp.int32, (cells, width), 0)
    lane = lax.broadcasted_iota(jnp.int32, (cells, width), 1)
    for (row, sign, there), own, other, edge in zip(sides, own_refs, other_refs, edge_refs):
        rows = pl.ds(0, elems * slices)
        edge[...] = clip(0.5 * face(own[rows], other[rows], sign, there))
    for e in range(elems):
        ahead, behind = pair_order(zone_ref[e], ztwo_ref[e])
        ahead_ref[e] = ahead
        behind_ref[e] = jnp.where(rank > 0, clip(0.5 * (maps_ref[e, 0] - behind)), 0.0)

    def step(z, behind):
        at_end = z == slices - 1
        zero_end = jnp.logical_and(at_end, rank == count - 1)
        duals = []
        for e in range(elems):
            tile = maps_ref[e, z]
            inner = maps_ref[e, jnp.minimum(z + 1, slices - 1)]
            ahead = jnp.where(at_end, ahead_ref[e], inner)
            dual_z = jnp.where(zero_end, 0.0, clip(0.5 * (ahead - tile)))
            dual_x, dual_y, spread = tile_duals(tile, None, None, sub, lane, (cells, width))
            dual_z_ref[e, z] = dual_z
            dual_x_ref[e, z] = dual_x
            dual_y_ref[e, z] = dual_y
            spread = spread + (behind[e] - dual_z)
            for (row, sign, there), edge in zip(sides, edge_refs):
                spread = spread + jnp.where(sub == row, sign * edge[pl.ds(e * slices + z, 1)], 0.0)
            adj_ref[e, z] = spread
            duals.append(dual_z)
        return tuple(duals)

    lax.fori_loop(0, slices, step, tuple(behind_ref[e] for e in range(elems)), unroll=UNROLL)


def join(ref):
    return jnp.concatenate([ref[e] for e in range(ref.shape[0])], axis=1)


def part(ref, pack):
    slices = ref.shape[2]
    for e in range(ref.shape[0]):
        ref[e] = pack[:, e * slices : (e + 1) * slices]


def first_update_kernel(total, size, maps_ref, weight_ref, adj_ref, coef_ref, measured_ref, packs_ref, *refs):
    elems, slices, cells, width = maps_ref.shape
    full_ref, cur_ref, ext_ref, dd_ref, yedge_ref, out_ref, emission_ref, zone_ref, ztwo_ref, *face_refs = refs
    mine = lax.axis_index("path")
    pack_shape = (cells, elems * slices)
    pack_lane = lax.broadcasted_iota(jnp.int32, pack_shape, 1)
    proj, whole, strip = [[packs_ref[r, i] for r in range(size)] for i in range(3)]
    far = jnp.zeros(pack_shape, jnp.bool_)
    for e in range(elems):
        inside = (pack_lane >= e * slices) & (pack_lane < (e + 1) * slices)
        far = far | (inside & (coef_ref[elems * elems + e : elems * elems + e + 1][:, 0:1] != 0.0))
    below = [jnp.zeros(pack_shape, F32)]
    above = [jnp.zeros(pack_shape, F32)]
    for r in range(1, size):
        below.append(below[-1] + strip[r - 1])
        above.append(above[-1] + strip[size - r])
    factor = [jnp.exp(jnp.where(far, above[size - 1 - r], below[r]) * (-1.0 / total)) for r in range(size)]
    image = factor[0] * proj[0]
    weights = factor[0] * whole[0]
    own = factor[0]
    for r in range(1, size):
        image = image + factor[r] * proj[r]
        weights = weights + factor[r] * whole[r]
        own = jnp.where(mine == r, factor[r], own)
    sig = 1.0 / weights
    data_dual = sig * (image - join(measured_ref)) / (1.0 + sig)
    dd_ref[0] = data_dual
    dd_ref[1] = sig
    part(emission_ref, image * (1.0 / total))
    after, before = jnp.minimum(mine + 1, size - 1), jnp.maximum(mine - 1, 0)
    y_ahead = jnp.where(mine < size - 1, clip(0.5 * (packs_ref[after, 3] - packs_ref[mine, 4])), 0.0)
    y_behind = jnp.where(mine > 0, clip(0.5 * (packs_ref[mine, 3] - packs_ref[before, 4])), 0.0)
    yedge_ref[0] = y_ahead
    yedge_ref[1] = y_behind
    sub = lax.broadcasted_iota(jnp.int32, (cells, width), 0)
    lane = lax.broadcasted_iota(jnp.int32, (cells, width), 1)

    image = first = last = jnp.zeros(pack_shape, F32)
    for z in range(slices):
        for e in range(elems):
            k = e * slices + z
            weight = weight_ref[e, z] * own[:, k : k + 1]
            full_ref[e, z] = weight
            tile = maps_ref[e, z]
            adj = adj_ref[e, z] - jnp.where(lane == width - 1, y_ahead[:, k : k + 1], 0.0)
            adj = adj + jnp.where(lane == 0, y_behind[:, k : k + 1], 0.0)
            new = jnp.maximum(tile - (weight * data_dual[:, k : k + 1] + adj) / (weight + 6.0), 0.0)
            ext = 2.0 * new - tile
            cur_ref[e, z] = new
            ext_ref[e, z] = ext
            here = pack_lane == k
            image = jnp.where(here, jnp.sum(weight * ext, axis=1, keepdims=True), image)
            first = jnp.where(here, ext[:, 0:1], first)
            last = jnp.where(here, ext[:, width - 1 : width], last)
            for ref, row in zip(face_refs, beam_rows(ext[0:1], ext[cells - 1 : cells])):
                ref[k : k + 1] = row
    for copy in range(size):
        out_ref[copy, 0] = image
        out_ref[copy, 1] = first
        out_ref[copy, 2] = last
    for e in range(elems):
        zone_ref[e], ztwo_ref[e] = pair_order(ext_ref[e, slices - 1], ext_ref[e, 0])


def second_dual_kernel(ext_ref, dual_z_ref, dual_x_ref, dual_y_ref, adj_ref):
    elems, slices, cells, width = ext_ref.shape
    sub = lax.broadcasted_iota(jnp.int32, (cells, width), 0)
    lane = lax.broadcasted_iota(jnp.int32, (cells, width), 1)

    def step(z, behind):
        at_end = z == slices - 1
        duals = []
        for e in range(elems):
            tile = ext_ref[e, z]
            ahead = ext_ref[e, jnp.minimum(z + 1, slices - 1)]
            dual_z = jnp.where(at_end, 0.0, clip(dual_z_ref[e, z] + 0.5 * (ahead - tile)))
            _, _, spread = tile_duals(tile, dual_x_ref[e, z], dual_y_ref[e, z], sub, lane, (cells, width))
            adj_ref[e, z] = spread + (behind[e] - dual_z)
            duals.append(dual_z)
        return tuple(duals)

    zero = jnp.zeros((cells, width), F32)
    lax.fori_loop(0, slices, step, (zero,) * elems, unroll=UNROLL)


def last_update_kernel(size, cur_ref, ext_ref, weight_ref, adj_ref, measured_ref, dd_ref, yedge_ref, zedge_ref,
                       zbehind_ref, zone_ref, ztwo_ref, packs_ref, *refs):
    elems, slices, cells, width = cur_ref.shape
    sides = beam_sides(cells)
    edge_refs, refs = refs[: len(sides)], refs[len(sides) :]
    own_refs, refs = refs[: len(sides)], refs[len(sides) :]
    other_refs, refs = refs[: len(sides)], refs[len(sides) :]
    new_ref, dual_ref, zface_ref, *face_refs = refs
    mine = lax.axis_index("path")
    count, rank = lax.axis_size("gz"), lax.axis_index("gz")
    image = packs_ref[0, 0]
    for r in range(1, size):
        image = image + packs_ref[r, 0]
    sig = dd_ref[1]
    data_dual = (dd_ref[0] + sig * (image - join(measured_ref))) / (1.0 + sig)
    part(dual_ref, data_dual)
    after, before = jnp.minimum(mine + 1, size - 1), jnp.maximum(mine - 1, 0)
    y_ahead = clip(yedge_ref[0] + 0.5 * (packs_ref[after, 1] - packs_ref[mine, 2]))
    y_behind = clip(yedge_ref[1] + 0.5 * (packs_ref[mine, 1] - packs_ref[before, 2]))
    y_ahead = jnp.where(mine < size - 1, y_ahead, 0.0)
    y_behind = jnp.where(mine > 0, y_behind, 0.0)
    for (row, sign, there), edge, own, other, out in zip(sides, edge_refs, own_refs, other_refs, face_refs):
        out[...] = clip(edge[...] + 0.5 * face(own[...], other[...], sign, there)) * sign
    sub = lax.broadcasted_iota(jnp.int32, (cells, width), 0)
    lane = lax.broadcasted_iota(jnp.int32, (cells, width), 1)
    for e in range(elems):
        other_ahead, other_behind = pair_order(zone_ref[e], ztwo_ref[e])
        z_behind = clip(zbehind_ref[e] + 0.5 * (ext_ref[e, 0] - other_behind))
        z_ahead = clip(zedge_ref[e, slices - 1] + 0.5 * (other_ahead - ext_ref[e, slices - 1]))
        zface_ref[0, e] = jnp.where(rank > 0, z_behind, 0.0)
        zface_ref[1, e] = jnp.where(rank < count - 1, z_ahead, 0.0)

    for z in range(slices):
        for e in range(elems):
            k = e * slices + z
            weight = weight_ref[e, z]
            adj = adj_ref[e, z]
            if z == 0:
                adj = adj + zface_ref[0, e]
            if z == slices - 1:
                adj = adj - zface_ref[1, e]
            adj = adj - jnp.where(lane == width - 1, y_ahead[:, k : k + 1], 0.0)
            adj = adj + jnp.where(lane == 0, y_behind[:, k : k + 1], 0.0)
            for (row, sign, there), out in zip(sides, face_refs):
                adj = adj + jnp.where(sub == row, out[k : k + 1], 0.0)
            step = (weight * data_dual[:, k : k + 1] + adj) / (weight + 6.0)
            new_ref[e, z] = jnp.maximum(cur_ref[e, z] - step, 0.0)


def shards(maps, measured, beta_table, view, kappa, line_of, side):
    elems, slices, cells, width = maps.shape
    total_x = cells * lax.axis_size("beam")
    total_y = width * lax.axis_size("path")
    size = lax.axis_size("path")
    block = f32(elems, slices, cells, width)
    plane = f32(elems, cells, width)
    rows = f32(elems * slices, width)
    faces = len(beam_sides(cells))
    measured = measured.transpose(0, 2, 1)
    kappa = kappa.T

    tall = f32((elems + 1) * slices, width)
    maps, inside, coef, zone, ztwo, *own = call(
        functools.partial(open_kernel, total_x),
        [view] + [pltpu.with_memory_space_constraint(a, pltpu.HBM) for a in (maps, beta_table, kappa, line_of, side)],
        [block, f32(slices, cells, width), f32(elems * elems + elems, width), plane, plane, tall] + [rows] * (faces - 1),
        [SMEM] + [pltpu.HBM] * 5,
        [
            pltpu.SMEM(beta_table.shape, F32),
            pltpu.SMEM(kappa.shape, F32),
            pltpu.SMEM(line_of.shape, jnp.int32),
            pltpu.SMEM(side.shape, jnp.int32),
            pltpu.SemaphoreType.DMA((5,)),
        ],
    )
    other = exchange_beam(own)
    carry, skip = other[-1], elems * slices
    beams = lax.axis_size("beam")
    if beams > 2:
        carry, skip = carry[skip:], 0
        reach = 1
        while reach < beams - 1:
            far = lax.axis_index("beam") > reach
            carry = carry + jnp.where(far, shifted(carry, "beam", reach), 0.0)
            reach *= 2
    zone, ztwo = swapped(zone, "gz", 0), swapped(ztwo, "gz", 1)
    local, pack = call(
        functools.partial(depth_kernel, total_y),
        [maps, coef],
        [block, f32(3, cells, elems * slices)],
        [VMEM] * 2,
        [
            pltpu.VMEM(maps.shape, F32),
            pltpu.VMEM((elems * slices * cells, 2 * width), jnp.bfloat16),
            pltpu.VMEM((elems * slices * cells, 2 * width), F32),
        ],
    )
    weight, pack = call(
        functools.partial(weight_kernel, total_x, skip),
        [maps, inside, carry, local, pack],
        [block, f32(size, 5, cells, elems * slices)],
        [VMEM] * 5,
    )
    packs = around(pack, "path")
    dual_z, dual_x, dual_y, zdual, adj, *edge = call(
        first_dual_kernel,
        [maps, zone, ztwo, *own, *other],
        [block, block, block, plane, block] + [rows] * faces,
        [VMEM] * (3 + 2 * faces),
        [pltpu.VMEM(plane.shape, F32)],
    )
    weight, current, extrap, dd, yedge, pack, emission, zone, ztwo, *own = call(
        functools.partial(first_update_kernel, total_y, size),
        [maps, weight, adj, coef, measured, packs],
        [block, block, block, f32(2, cells, elems * slices), f32(2, cells, elems * slices),
         f32(size, 3, cells, elems * slices), f32(elems, cells, slices), plane, plane] + [rows] * faces,
        [VMEM] * 6,
    )
    packs = around(pack, "path")
    zone, ztwo = swapped(zone, "gz", 0), swapped(ztwo, "gz", 1)
    other = exchange_beam(own)
    (adj,) = call(second_dual_kernel, [extrap, dual_z, dual_x, dual_y], [block], [VMEM] * 4)
    current, data_dual = call(
        functools.partial(last_update_kernel, size),
        [current, extrap, weight, adj, measured, dd, yedge, dual_z, zdual, zone, ztwo, packs, *edge, *own, *other],
        [block, f32(elems, cells, slices)],
        [VMEM] * (12 + 3 * faces),
        [pltpu.VMEM((2, elems, cells, width), F32)] + [pltpu.VMEM((elems * slices, width), F32)] * faces,
    )
    return emission.transpose(0, 2, 1), current, data_dual.transpose(0, 2, 1)


def solution(mesh):
    return jax.shard_map(
        shards,
        mesh=mesh,
        in_specs=(P(None, "gz", "beam", "path"), P(None, "gz", "beam"), P(), P(), P(), P(), P()),
        out_specs=(P(None, "gz", "beam"), P(None, "gz", "beam", "path"), P(None, "gz", "beam")),
        check_vma=False,
    )
```

```python
import functools

import jax
import jax.numpy as jnp
from jax import lax
from jax.experimental import pallas as pl
from jax.experimental.pallas import tpu as pltpu
from jax.sharding import PartitionSpec as P

ITERS = 2
LAM = 0.1
F32 = jnp.float32
VMEM = pltpu.VMEM
SMEM = pltpu.SMEM
UNROLL = 4
VMEM_LIMIT = 32 * 1024 * 1024


def clip(value):
    return jnp.clip(value, -LAM, LAM)


def call(body, ins, outs, spaces, scratch=(), flops=1_000_000):
    specs = [pl.BlockSpec(memory_space=space) for space in spaces]
    moved = sum(a.size * 4 for a in ins) + sum(o.size * 4 for o in outs)
    return pl.pallas_call(
        body,
        out_shape=outs,
        in_specs=specs,
        out_specs=[pl.BlockSpec(memory_space=VMEM)] * len(outs),
        scratch_shapes=list(scratch),
        compiler_params=pltpu.CompilerParams(vmem_limit_bytes=VMEM_LIMIT),
        cost_estimate=pl.CostEstimate(flops=flops, bytes_accessed=moved, transcendentals=0),
    )(*ins)


def f32(*shape):
    return jax.ShapeDtypeStruct(shape, F32)


def shifted(block, axis, distance):
    n = lax.axis_size(axis)
    return lax.ppermute(block, axis, [((i - distance) % n, i) for i in range(n)])


def swapped(block, axis, start):
    n = lax.axis_size(axis)
    route = {i: i for i in range(n)}
    for i in range(start, n - 1, 2):
        route[i], route[i + 1] = i + 1, i
    return lax.ppermute(block, axis, sorted(route.items()))


def pair_order(ahead, behind):
    even = lax.rem(lax.axis_index("gz"), 2) == 0
    return jnp.where(even, ahead, behind), jnp.where(even, behind, ahead)


def around(block, axis):
    return [block] + [shifted(block, axis, s) for s in range(1, lax.axis_size(axis))]


def by_rank(blocks, size):
    mine = lax.axis_index("path")
    ordered = []
    for rank in range(size):
        value = blocks[0]
        for s in range(1, size):
            value = jnp.where(lax.rem(mine - s + size, size) == rank, blocks[s], value)
        ordered.append(value)
    return ordered


def spread(pack, lane, k):
    return jnp.sum(jnp.where(lane == k, pack, 0.0), axis=1, keepdims=True)


def gather_edges(edges, tile, lane, k):
    width = tile.shape[1]
    here = (lane == k) | (lane == (k - 1) % width)
    edges[k % 2] = jnp.where(here, pltpu.roll(tile, k, axis=1) if k else tile, edges[k % 2])


def packed_edges(edges, lane):
    even = lane % 2 == 0
    first = jnp.where(even, edges[0], edges[1])
    return first, pltpu.roll(jnp.where(even, edges[1], edges[0]), 1, axis=1)


def join_edges(first, last, lane):
    width = first.shape[1]
    last = pltpu.roll(last, width - 1, axis=1)
    even = lane % 2 == 0
    return jnp.where(even, first, last), jnp.where(even, last, first)


def edge_columns(joined, rim, k):
    pack = joined[k % 2]
    return jnp.where(rim, pltpu.roll(pack, pack.shape[1] - k, axis=1) if k else pack, 0.0)


def beam_sides(cells):
    count, rank = lax.axis_size("beam"), lax.axis_index("beam")
    if count == 2:
        return [
            (
                jnp.where(rank == 0, cells - 1, 0),
                jnp.where(rank == 0, F32(-1.0), F32(1.0)),
                None,
            )
        ]
    return [(cells - 1, F32(-1.0), rank < count - 1), (0, F32(1.0), rank > 0)]


def beam_rows(first, last):
    count, rank = lax.axis_size("beam"), lax.axis_index("beam")
    if count == 2:
        return [jnp.where(rank == 0, last, first)]
    return [last, first]


def face(own, other, sign, there):
    step = (own - other) * sign
    return step if there is None else jnp.where(there, step, 0.0)


def exchange_beam(rows):
    if lax.axis_size("beam") == 2:
        return [lax.ppermute(rows[0], "beam", [(0, 1), (1, 0)])]
    return [shifted(rows[1], "beam", -1), shifted(rows[0], "beam", 1)]


def open_kernel(total, view_ref, source_ref, *refs):
    small, refs = refs[:4], refs[4:]
    maps_ref, inside_ref, coef_ref, zone_ref, ztwo_ref, *refs = refs
    elems, slices, cells, width = maps_ref.shape
    faces = len(beam_sides(cells))
    face_refs, refs = refs[:faces], refs[faces:]
    beta_ref, kappa_ref, line_ref, side_ref, sems = refs
    fetch = [pltpu.make_async_copy(source_ref, maps_ref, sems.at[0])]
    for i, (ref, kept) in enumerate(zip(small, (beta_ref, kappa_ref, line_ref, side_ref))):
        fetch.append(pltpu.make_async_copy(ref, kept, sems.at[i + 1]))
    for copy in fetch:
        copy.start()
    for copy in fetch[1:]:
        copy.wait()
    for e in range(elems):
        line = line_ref[e]
        for f in range(elems):
            coef_ref[e * elems + f : e * elems + f + 1] = jnp.full((1, width), kappa_ref[f, line])
        coef_ref[elems * elems + e : elems * elems + e + 1] = jnp.full((1, width), side_ref[e].astype(F32))
    fetch[0].wait()
    view = view_ref[0]
    beta = [beta_ref[view, e] for e in range(elems)]
    sub = lax.broadcasted_iota(jnp.int32, maps_ref.shape[2:], 0)
    for z in range(slices):
        tiles = [maps_ref[e, z] for e in range(elems)]
        mu = beta[0] * tiles[0]
        for e in range(1, elems):
            mu = mu + beta[e] * tiles[e]
        run = mu
        reach = 1
        while reach < cells:
            run = run + jnp.where(sub >= reach, pltpu.roll(run, reach, axis=0), 0.0)
            reach *= 2
        inside_ref[z] = jnp.where(sub >= 1, pltpu.roll(run, 1, axis=0), 0.0)
        face_refs[0][elems * slices + z : elems * slices + z + 1] = run[cells - 1 : cells]
        for e in range(elems):
            rows = beam_rows(tiles[e][0:1], tiles[e][cells - 1 : cells])
            for ref, row in zip(face_refs, rows):
                ref[e * slices + z : e * slices + z + 1] = row
    for e in range(elems):
        zone_ref[e], ztwo_ref[e] = pair_order(maps_ref[e, slices - 1], maps_ref[e, 0])


def depth_kernel(total, maps_ref, coef_ref, local_ref, pack_ref, mu_ref, parts_ref, sums_ref):
    elems, slices, cells, width = maps_ref.shape
    rows = slices * cells
    row = lax.broadcasted_iota(jnp.int32, (2 * width, 2 * width), 0)
    col = lax.broadcasted_iota(jnp.int32, (2 * width, 2 * width), 1)
    row = jnp.where(row >= width, row - width, row)
    table = jnp.where((row < col) | (col >= width), 1.0, 0.0).astype(jnp.bfloat16)
    for e in range(elems):
        mu = coef_ref[e * elems : e * elems + 1][None] * maps_ref[0]
        for f in range(1, elems):
            mu = mu + coef_ref[e * elems + f : e * elems + f + 1][None] * maps_ref[f]
        mu_ref[e] = mu
        flat = mu.reshape(rows, width)
        high = flat.astype(jnp.bfloat16)
        low = (flat - high.astype(F32)).astype(jnp.bfloat16)
        parts_ref[e * rows : (e + 1) * rows, 0:width] = high
        parts_ref[e * rows : (e + 1) * rows, width:] = low
    sums_ref[...] = jnp.dot(parts_ref[...], table, preferred_element_type=F32)
    lane = lax.broadcasted_iota(jnp.int32, (cells, width), 1)
    scale = -1.0 / total
    strip = jnp.zeros((cells, width), F32)
    edges = [strip, strip]
    for e in range(elems):
        forward = coef_ref[elems * elems + e : elems * elems + e + 1] == 0.0
        for z in range(slices):
            k = e * slices + z
            before = sums_ref[k * cells : (k + 1) * cells, 0:width]
            whole = sums_ref[k * cells : (k + 1) * cells, width:]
            after = whole - before - mu_ref[e, z]
            local_ref[e, z] = jnp.exp(jnp.where(forward, before, after) * scale)
            strip = jnp.where(lane == k, whole, strip)
            gather_edges(edges, maps_ref[e, z], lane, k)
    pack_ref[0] = strip
    pack_ref[1], pack_ref[2] = packed_edges(edges, lane)


def weight_kernel(total, skip, maps_ref, inside_ref, carry_ref, local_ref, pack_ref, weight_ref, out_ref):
    elems, slices, cells, width = maps_ref.shape
    lane = lax.broadcasted_iota(jnp.int32, (cells, width), 1)
    there = lax.axis_index("beam") > 0
    scale = -1.0 / total

    def step(z, packs):
        proj, whole = packs
        place = lane - z
        carry = jnp.where(there, carry_ref[pl.ds(skip + z, 1)], 0.0)
        att = jnp.exp((inside_ref[z] + carry) * scale)
        for e in range(elems):
            weight = att * local_ref[e, z]
            weight_ref[e, z] = weight
            here = place == e * slices
            proj = jnp.where(here, jnp.sum(weight * maps_ref[e, z], axis=1, keepdims=True), proj)
            whole = jnp.where(here, jnp.sum(weight, axis=1, keepdims=True), whole)
        return proj, whole

    zero = jnp.zeros((cells, width), F32)
    proj, whole = lax.fori_loop(0, slices, step, (zero, zero), unroll=UNROLL)
    out_ref[0] = proj
    out_ref[1] = whole
    out_ref[2] = pack_ref[0]
    out_ref[3] = pack_ref[1]
    out_ref[4] = pack_ref[2]


def dual_step(field, ahead, dual, last):
    step = 0.5 * (ahead - field)
    return jnp.where(last, 0.0, clip(step if dual is None else dual + step))


def tile_duals(tile, dual_x, dual_y, sub, lane, shape):
    cells, width = shape
    new_x = dual_step(tile, pltpu.roll(tile, cells - 1, axis=0), dual_x, sub == cells - 1)
    new_y = dual_step(tile, pltpu.roll(tile, width - 1, axis=1), dual_y, lane == width - 1)
    spread = pltpu.roll(new_x, 1, axis=0) - new_x + (pltpu.roll(new_y, 1, axis=1) - new_y)
    return new_x, new_y, spread


def first_dual_kernel(maps_ref, zone_ref, ztwo_ref, *refs):
    elems, slices, cells, width = maps_ref.shape
    sides = beam_sides(cells)
    own_refs, refs = refs[: len(sides)], refs[len(sides) :]
    other_refs, refs = refs[: len(sides)], refs[len(sides) :]
    dual_z_ref, dual_x_ref, dual_y_ref, behind_ref, adj_ref, *edge_refs, ahead_ref = refs
    count, rank = lax.axis_size("gz"), lax.axis_index("gz")
    sub = lax.broadcasted_iota(jnp.int32, (cells, width), 0)
    lane = lax.broadcasted_iota(jnp.int32, (cells, width), 1)
    for (row, sign, there), own, other, edge in zip(sides, own_refs, other_refs, edge_refs):
        rows = pl.ds(0, elems * slices)
        edge[...] = clip(0.5 * face(own[rows], other[rows], sign, there))
    for e in range(elems):
        ahead, behind = pair_order(zone_ref[e], ztwo_ref[e])
        ahead_ref[e] = ahead
        behind_ref[e] = jnp.where(rank > 0, clip(0.5 * (maps_ref[e, 0] - behind)), 0.0)

    def step(z, behind):
        at_end = z == slices - 1
        zero_end = jnp.logical_and(at_end, rank == count - 1)
        duals = []
        for e in range(elems):
            tile = maps_ref[e, z]
            inner = maps_ref[e, jnp.minimum(z + 1, slices - 1)]
            ahead = jnp.where(at_end, ahead_ref[e], inner)
            dual_z = jnp.where(zero_end, 0.0, clip(0.5 * (ahead - tile)))
            dual_x, dual_y, spread = tile_duals(tile, None, None, sub, lane, (cells, width))
            dual_z_ref[e, z] = dual_z
            dual_x_ref[e, z] = dual_x
            dual_y_ref[e, z] = dual_y
            spread = spread + (behind[e] - dual_z)
            for (row, sign, there), edge in zip(sides, edge_refs):
                spread = spread + jnp.where(sub == row, sign * edge[pl.ds(e * slices + z, 1)], 0.0)
            adj_ref[e, z] = spread
            duals.append(dual_z)
        return tuple(duals)

    lax.fori_loop(0, slices, step, tuple(behind_ref[e] for e in range(elems)), unroll=UNROLL)


def join(ref, width):
    elems, cells, slices = ref.shape
    parts = [ref[e] for e in range(elems)]
    if elems * slices < width:
        parts.append(jnp.zeros((cells, width - elems * slices), F32))
    return jnp.concatenate(parts, axis=1)


def part(ref, pack):
    slices = ref.shape[2]
    for e in range(ref.shape[0]):
        ref[e] = pack[:, e * slices : (e + 1) * slices]


def first_update_kernel(total, size, maps_ref, weight_ref, adj_ref, coef_ref, measured_ref, *refs):
    elems, slices, cells, width = maps_ref.shape
    pack_refs, refs = refs[:size], refs[size:]
    full_ref, cur_ref, ext_ref, dd_ref, yedge_ref, out_ref, emission_ref, zone_ref, ztwo_ref, *face_refs = refs
    mine = lax.axis_index("path")
    pack_shape = (cells, width)
    lane = lax.broadcasted_iota(jnp.int32, pack_shape, 1)
    rim = (lane == 0) | (lane == width - 1)
    proj, whole, strip = [by_rank([ref[i] for ref in pack_refs], size) for i in range(3)]
    far = jnp.zeros(pack_shape, jnp.bool_)
    for e in range(elems):
        inside = (lane >= e * slices) & (lane < (e + 1) * slices)
        far = far | (inside & (coef_ref[elems * elems + e : elems * elems + e + 1][:, 0:1] != 0.0))
    below = [jnp.zeros(pack_shape, F32)]
    above = [jnp.zeros(pack_shape, F32)]
    for r in range(1, size):
        below.append(below[-1] + strip[r - 1])
        above.append(above[-1] + strip[size - r])
    factor = [jnp.exp(jnp.where(far, above[size - 1 - r], below[r]) * (-1.0 / total)) for r in range(size)]
    image = factor[0] * proj[0]
    weights = factor[0] * whole[0]
    own = factor[0]
    for r in range(1, size):
        image = image + factor[r] * proj[r]
        weights = weights + factor[r] * whole[r]
        own = jnp.where(mine == r, factor[r], own)
    sig = 1.0 / weights
    data_dual = sig * (image - join(measured_ref, width)) / (1.0 + sig)
    dd_ref[0] = data_dual
    dd_ref[1] = sig
    part(emission_ref, image * (1.0 / total))
    own_ref, after, before = pack_refs[0], pack_refs[size - 1], pack_refs[min(1, size - 1)]
    y_ahead = jnp.where(mine < size - 1, clip(0.5 * (after[3] - own_ref[4])), 0.0)
    y_behind = jnp.where(mine > 0, clip(0.5 * (own_ref[3] - before[4])), 0.0)
    joined = join_edges(y_behind, -y_ahead, lane)
    yedge_ref[0] = y_ahead
    yedge_ref[1] = y_behind

    image = jnp.zeros(pack_shape, F32)
    edges = [image, image]
    for z in range(slices):
        for e in range(elems):
            k = e * slices + z
            weight = weight_ref[e, z] * spread(own, lane, k)
            full_ref[e, z] = weight
            tile = maps_ref[e, z]
            adj = adj_ref[e, z] + edge_columns(joined, rim, k)
            new = jnp.maximum(tile - (weight * spread(data_dual, lane, k) + adj) / (weight + 6.0), 0.0)
            ext = 2.0 * new - tile
            cur_ref[e, z] = new
            ext_ref[e, z] = ext
            image = jnp.where(lane == k, jnp.sum(weight * ext, axis=1, keepdims=True), image)
            gather_edges(edges, ext, lane, k)
            for ref, row in zip(face_refs, beam_rows(ext[0:1], ext[cells - 1 : cells])):
                ref[k : k + 1] = row
    out_ref[0] = image
    out_ref[1], out_ref[2] = packed_edges(edges, lane)
    for e in range(elems):
        zone_ref[e], ztwo_ref[e] = pair_order(ext_ref[e, slices - 1], ext_ref[e, 0])


def second_dual_kernel(ext_ref, dual_z_ref, dual_x_ref, dual_y_ref, adj_ref):
    elems, slices, cells, width = ext_ref.shape
    sub = lax.broadcasted_iota(jnp.int32, (cells, width), 0)
    lane = lax.broadcasted_iota(jnp.int32, (cells, width), 1)

    def step(z, behind):
        at_end = z == slices - 1
        duals = []
        for e in range(elems):
            tile = ext_ref[e, z]
            ahead = ext_ref[e, jnp.minimum(z + 1, slices - 1)]
            dual_z = jnp.where(at_end, 0.0, clip(dual_z_ref[e, z] + 0.5 * (ahead - tile)))
            _, _, spread = tile_duals(tile, dual_x_ref[e, z], dual_y_ref[e, z], sub, lane, (cells, width))
            adj_ref[e, z] = spread + (behind[e] - dual_z)
            duals.append(dual_z)
        return tuple(duals)

    zero = jnp.zeros((cells, width), F32)
    lax.fori_loop(0, slices, step, (zero,) * elems, unroll=UNROLL)


def last_update_kernel(size, cur_ref, ext_ref, weight_ref, adj_ref, measured_ref, dd_ref, yedge_ref, zedge_ref,
                       zbehind_ref, zone_ref, ztwo_ref, *refs):
    elems, slices, cells, width = cur_ref.shape
    sides = beam_sides(cells)
    pack_refs, refs = refs[:size], refs[size:]
    edge_refs, refs = refs[: len(sides)], refs[len(sides) :]
    own_refs, refs = refs[: len(sides)], refs[len(sides) :]
    other_refs, refs = refs[: len(sides)], refs[len(sides) :]
    new_ref, dual_ref, zface_ref, *face_refs = refs
    mine = lax.axis_index("path")
    count, rank = lax.axis_size("gz"), lax.axis_index("gz")
    images = by_rank([ref[0] for ref in pack_refs], size)
    image = images[0]
    for r in range(1, size):
        image = image + images[r]
    sig = dd_ref[1]
    data_dual = (dd_ref[0] + sig * (image - join(measured_ref, width))) / (1.0 + sig)
    part(dual_ref, data_dual)
    own_ref, after, before = pack_refs[0], pack_refs[size - 1], pack_refs[min(1, size - 1)]
    y_ahead = jnp.where(mine < size - 1, clip(yedge_ref[0] + 0.5 * (after[1] - own_ref[2])), 0.0)
    y_behind = jnp.where(mine > 0, clip(yedge_ref[1] + 0.5 * (own_ref[1] - before[2])), 0.0)
    for (row, sign, there), edge, own, other, out in zip(sides, edge_refs, own_refs, other_refs, face_refs):
        out[...] = clip(edge[...] + 0.5 * face(own[...], other[...], sign, there)) * sign
    sub = lax.broadcasted_iota(jnp.int32, (cells, width), 0)
    lane = lax.broadcasted_iota(jnp.int32, (cells, width), 1)
    rim = (lane == 0) | (lane == width - 1)
    joined = join_edges(y_behind, -y_ahead, lane)
    for e in range(elems):
        other_ahead, other_behind = pair_order(zone_ref[e], ztwo_ref[e])
        z_behind = clip(zbehind_ref[e] + 0.5 * (ext_ref[e, 0] - other_behind))
        z_ahead = clip(zedge_ref[e, slices - 1] + 0.5 * (other_ahead - ext_ref[e, slices - 1]))
        zface_ref[0, e] = jnp.where(rank > 0, z_behind, 0.0)
        zface_ref[1, e] = jnp.where(rank < count - 1, z_ahead, 0.0)

    for z in range(slices):
        for e in range(elems):
            k = e * slices + z
            weight = weight_ref[e, z]
            adj = adj_ref[e, z]
            if z == 0:
                adj = adj + zface_ref[0, e]
            if z == slices - 1:
                adj = adj - zface_ref[1, e]
            adj = adj + edge_columns(joined, rim, k)
            for (row, sign, there), out in zip(sides, face_refs):
                adj = adj + jnp.where(sub == row, out[k : k + 1], 0.0)
            step = (weight * spread(data_dual, lane, k) + adj) / (weight + 6.0)
            new_ref[e, z] = jnp.maximum(cur_ref[e, z] - step, 0.0)


def shards(maps, measured, beta_table, view, kappa, line_of, side):
    elems, slices, cells, width = maps.shape
    total_x = cells * lax.axis_size("beam")
    total_y = width * lax.axis_size("path")
    size = lax.axis_size("path")
    block = f32(elems, slices, cells, width)
    plane = f32(elems, cells, width)
    rows = f32(elems * slices, width)
    faces = len(beam_sides(cells))
    measured = measured.transpose(0, 2, 1)
    kappa = kappa.T

    tall = f32((elems + 1) * slices, width)
    maps, inside, coef, zone, ztwo, *own = call(
        functools.partial(open_kernel, total_x),
        [view] + [pltpu.with_memory_space_constraint(a, pltpu.HBM) for a in (maps, beta_table, kappa, line_of, side)],
        [block, f32(slices, cells, width), f32(elems * elems + elems, width), plane, plane, tall] + [rows] * (faces - 1),
        [SMEM] + [pltpu.HBM] * 5,
        [
            pltpu.SMEM(beta_table.shape, F32),
            pltpu.SMEM(kappa.shape, F32),
            pltpu.SMEM(line_of.shape, jnp.int32),
            pltpu.SMEM(side.shape, jnp.int32),
            pltpu.SemaphoreType.DMA((5,)),
        ],
    )
    other = exchange_beam(own)
    carry, skip = other[-1], elems * slices
    beams = lax.axis_size("beam")
    if beams > 2:
        carry, skip = carry[skip:], 0
        reach = 1
        while reach < beams - 1:
            far = lax.axis_index("beam") > reach
            carry = carry + jnp.where(far, shifted(carry, "beam", reach), 0.0)
            reach *= 2
    zone, ztwo = swapped(zone, "gz", 0), swapped(ztwo, "gz", 1)
    local, pack = call(
        functools.partial(depth_kernel, total_y),
        [maps, coef],
        [block, f32(3, cells, width)],
        [VMEM] * 2,
        [
            pltpu.VMEM(maps.shape, F32),
            pltpu.VMEM((elems * slices * cells, 2 * width), jnp.bfloat16),
            pltpu.VMEM((elems * slices * cells, 2 * width), F32),
        ],
    )
    weight, pack = call(
        functools.partial(weight_kernel, total_x, skip),
        [maps, inside, carry, local, pack],
        [block, f32(5, cells, width)],
        [VMEM] * 5,
    )
    packs = around(pack, "path")
    dual_z, dual_x, dual_y, zdual, adj, *edge = call(
        first_dual_kernel,
        [maps, zone, ztwo, *own, *other],
        [block, block, block, plane, block] + [rows] * faces,
        [VMEM] * (3 + 2 * faces),
        [pltpu.VMEM(plane.shape, F32)],
    )
    weight, current, extrap, dd, yedge, pack, emission, zone, ztwo, *own = call(
        functools.partial(first_update_kernel, total_y, size),
        [maps, weight, adj, coef, measured, *packs],
        [block, block, block, f32(2, cells, width), f32(2, cells, width),
         f32(3, cells, width), f32(elems, cells, slices), plane, plane] + [rows] * faces,
        [VMEM] * (5 + size),
    )
    packs = around(pack, "path")
    zone, ztwo = swapped(zone, "gz", 0), swapped(ztwo, "gz", 1)
    other = exchange_beam(own)
    (adj,) = call(second_dual_kernel, [extrap, dual_z, dual_x, dual_y], [block], [VMEM] * 4)
    current, data_dual = call(
        functools.partial(last_update_kernel, size),
        [current, extrap, weight, adj, measured, dd, yedge, dual_z, zdual, zone, ztwo, *packs, *edge, *own, *other],
        [block, f32(elems, cells, slices)],
        [VMEM] * (11 + size + 3 * faces),
        [pltpu.VMEM((2, elems, cells, width), F32)] + [pltpu.VMEM((elems * slices, width), F32)] * faces,
    )
    return emission.transpose(0, 2, 1), current, data_dual.transpose(0, 2, 1)


def solution(mesh):
    return jax.shard_map(
        shards,
        mesh=mesh,
        in_specs=(P(None, "gz", "beam", "path"), P(None, "gz", "beam"), P(), P(), P(), P(), P()),
        out_specs=(P(None, "gz", "beam"), P(None, "gz", "beam", "path"), P(None, "gz", "beam")),
        check_vma=False,
    )
```

```python
import functools

import jax
import jax.numpy as jnp
from jax import lax
from jax.experimental import pallas as pl
from jax.experimental.pallas import tpu as pltpu
from jax.sharding import PartitionSpec as P

ITERS = 2
LAM = 0.1
F32 = jnp.float32
VMEM = pltpu.VMEM
SMEM = pltpu.SMEM
UNROLL = 4
VMEM_LIMIT = 32 * 1024 * 1024


def clip(value):
    return jnp.clip(value, -LAM, LAM)


def call(body, ins, outs, spaces, scratch=(), flops=1_000_000):
    specs = [pl.BlockSpec(memory_space=space) for space in spaces]
    moved = sum(a.size * 4 for a in ins) + sum(o.size * 4 for o in outs)
    return pl.pallas_call(
        body,
        out_shape=outs,
        in_specs=specs,
        out_specs=[pl.BlockSpec(memory_space=VMEM)] * len(outs),
        scratch_shapes=list(scratch),
        compiler_params=pltpu.CompilerParams(vmem_limit_bytes=VMEM_LIMIT),
        cost_estimate=pl.CostEstimate(flops=flops, bytes_accessed=moved, transcendentals=0),
    )(*ins)


def f32(*shape):
    return jax.ShapeDtypeStruct(shape, F32)


def shifted(block, axis, distance):
    n = lax.axis_size(axis)
    return lax.ppermute(block, axis, [((i - distance) % n, i) for i in range(n)])


def swapped(block, axis, start):
    n = lax.axis_size(axis)
    route = {i: i for i in range(n)}
    for i in range(start, n - 1, 2):
        route[i], route[i + 1] = i + 1, i
    return lax.ppermute(block, axis, sorted(route.items()))


def pair_order(ahead, behind):
    even = lax.rem(lax.axis_index("gz"), 2) == 0
    return jnp.where(even, ahead, behind), jnp.where(even, behind, ahead)


def around(block, axis):
    return [block] + [shifted(block, axis, s) for s in range(1, lax.axis_size(axis))]


def by_rank(blocks, size):
    mine = lax.axis_index("path")
    ordered = []
    for rank in range(size):
        value = blocks[0]
        for s in range(1, size):
            value = jnp.where(lax.rem(mine - s + size, size) == rank, blocks[s], value)
        ordered.append(value)
    return ordered


def spread(pack, lane, k):
    return jnp.sum(jnp.where(lane == k, pack, 0.0), axis=1, keepdims=True)


def gather_edges(pack, tile, lane, k):
    width = tile.shape[1]
    here = (lane == k) | (lane == lax.rem(k + width - 1, width))
    return jnp.where(here, pltpu.roll(tile, k, axis=1), pack)


def packed_edges(edges, lane):
    even = lane % 2 == 0
    first = jnp.where(even, edges[0], edges[1])
    return first, pltpu.roll(jnp.where(even, edges[1], edges[0]), 1, axis=1)


def join_edges(first, last, lane):
    width = first.shape[1]
    last = pltpu.roll(last, width - 1, axis=1)
    even = lane % 2 == 0
    return jnp.where(even, first, last), jnp.where(even, last, first)


def edge_columns(pack, rim, k):
    width = pack.shape[1]
    return jnp.where(rim, pltpu.roll(pack, lax.rem(width - k, width), axis=1), 0.0)


def sweep(slices, body, carry):
    group = UNROLL if slices % UNROLL == 0 else slices

    def step(i, carry):
        for offset in range(group):
            carry = body(group * i + offset, offset, carry)
        return carry

    return lax.fori_loop(0, slices // group, step, carry)


def beam_sides(cells):
    count, rank = lax.axis_size("beam"), lax.axis_index("beam")
    if count == 2:
        return [
            (
                jnp.where(rank == 0, cells - 1, 0),
                jnp.where(rank == 0, F32(-1.0), F32(1.0)),
                None,
            )
        ]
    return [(cells - 1, F32(-1.0), rank < count - 1), (0, F32(1.0), rank > 0)]


def beam_rows(first, last):
    count, rank = lax.axis_size("beam"), lax.axis_index("beam")
    if count == 2:
        return [jnp.where(rank == 0, last, first)]
    return [last, first]


def face(own, other, sign, there):
    step = (own - other) * sign
    return step if there is None else jnp.where(there, step, 0.0)


def exchange_beam(rows):
    if lax.axis_size("beam") == 2:
        return [lax.ppermute(rows[0], "beam", [(0, 1), (1, 0)])]
    return [shifted(rows[1], "beam", -1), shifted(rows[0], "beam", 1)]


def open_kernel(total, view_ref, source_ref, *refs):
    small, refs = refs[:4], refs[4:]
    maps_ref, inside_ref, coef_ref, zone_ref, ztwo_ref, *refs = refs
    elems, slices, cells, width = maps_ref.shape
    faces = len(beam_sides(cells))
    face_refs, refs = refs[:faces], refs[faces:]
    beta_ref, kappa_ref, line_ref, side_ref, sems = refs
    fetch = [pltpu.make_async_copy(source_ref, maps_ref, sems.at[0])]
    for i, (ref, kept) in enumerate(zip(small, (beta_ref, kappa_ref, line_ref, side_ref))):
        fetch.append(pltpu.make_async_copy(ref, kept, sems.at[i + 1]))
    for copy in fetch:
        copy.start()
    for copy in fetch[1:]:
        copy.wait()
    for e in range(elems):
        line = line_ref[e]
        for f in range(elems):
            coef_ref[e * elems + f : e * elems + f + 1] = jnp.full((1, width), kappa_ref[f, line])
        coef_ref[elems * elems + e : elems * elems + e + 1] = jnp.full((1, width), side_ref[e].astype(F32))
    fetch[0].wait()
    view = view_ref[0]
    beta = [beta_ref[view, e] for e in range(elems)]
    sub = lax.broadcasted_iota(jnp.int32, maps_ref.shape[2:], 0)
    for z in range(slices):
        tiles = [maps_ref[e, z] for e in range(elems)]
        mu = beta[0] * tiles[0]
        for e in range(1, elems):
            mu = mu + beta[e] * tiles[e]
        run = mu
        reach = 1
        while reach < cells:
            run = run + jnp.where(sub >= reach, pltpu.roll(run, reach, axis=0), 0.0)
            reach *= 2
        inside_ref[z] = jnp.where(sub >= 1, pltpu.roll(run, 1, axis=0), 0.0)
        face_refs[0][elems * slices + z : elems * slices + z + 1] = run[cells - 1 : cells]
        for e in range(elems):
            rows = beam_rows(tiles[e][0:1], tiles[e][cells - 1 : cells])
            for ref, row in zip(face_refs, rows):
                ref[e * slices + z : e * slices + z + 1] = row
    for e in range(elems):
        zone_ref[e], ztwo_ref[e] = pair_order(maps_ref[e, slices - 1], maps_ref[e, 0])


def depth_kernel(total, maps_ref, coef_ref, local_ref, pack_ref, mu_ref, parts_ref, sums_ref):
    elems, slices, cells, width = maps_ref.shape
    rows = slices * cells
    row = lax.broadcasted_iota(jnp.int32, (2 * width, 2 * width), 0)
    col = lax.broadcasted_iota(jnp.int32, (2 * width, 2 * width), 1)
    row = jnp.where(row >= width, row - width, row)
    table = jnp.where((row < col) | (col >= width), 1.0, 0.0).astype(jnp.bfloat16)
    for e in range(elems):
        mu = coef_ref[e * elems : e * elems + 1][None] * maps_ref[0]
        for f in range(1, elems):
            mu = mu + coef_ref[e * elems + f : e * elems + f + 1][None] * maps_ref[f]
        mu_ref[e] = mu
        flat = mu.reshape(rows, width)
        high = flat.astype(jnp.bfloat16)
        low = (flat - high.astype(F32)).astype(jnp.bfloat16)
        parts_ref[e * rows : (e + 1) * rows, 0:width] = high
        parts_ref[e * rows : (e + 1) * rows, width:] = low
    sums_ref[...] = jnp.dot(parts_ref[...], table, preferred_element_type=F32)
    lane = lax.broadcasted_iota(jnp.int32, (cells, width), 1)
    scale = -1.0 / total
    strip = jnp.zeros((cells, width), F32)
    edges = [strip, strip]
    for e in range(elems):
        forward = coef_ref[elems * elems + e : elems * elems + e + 1] == 0.0
        for z in range(slices):
            k = e * slices + z
            before = sums_ref[k * cells : (k + 1) * cells, 0:width]
            whole = sums_ref[k * cells : (k + 1) * cells, width:]
            after = whole - before - mu_ref[e, z]
            local_ref[e, z] = jnp.exp(jnp.where(forward, before, after) * scale)
            strip = jnp.where(lane == k, whole, strip)
            edges[k % 2] = gather_edges(edges[k % 2], maps_ref[e, z], lane, k)
    pack_ref[0] = strip
    pack_ref[1], pack_ref[2] = packed_edges(edges, lane)


def weight_kernel(total, skip, maps_ref, inside_ref, carry_ref, local_ref, pack_ref, weight_ref, out_ref):
    elems, slices, cells, width = maps_ref.shape
    lane = lax.broadcasted_iota(jnp.int32, (cells, width), 1)
    there = lax.axis_index("beam") > 0
    scale = -1.0 / total

    def step(z, packs):
        proj, whole = packs
        place = lane - z
        carry = jnp.where(there, carry_ref[pl.ds(skip + z, 1)], 0.0)
        att = jnp.exp((inside_ref[z] + carry) * scale)
        for e in range(elems):
            weight = att * local_ref[e, z]
            weight_ref[e, z] = weight
            here = place == e * slices
            proj = jnp.where(here, jnp.sum(weight * maps_ref[e, z], axis=1, keepdims=True), proj)
            whole = jnp.where(here, jnp.sum(weight, axis=1, keepdims=True), whole)
        return proj, whole

    zero = jnp.zeros((cells, width), F32)
    proj, whole = lax.fori_loop(0, slices, step, (zero, zero), unroll=UNROLL)
    out_ref[0] = proj
    out_ref[1] = whole
    out_ref[2] = pack_ref[0]
    out_ref[3] = pack_ref[1]
    out_ref[4] = pack_ref[2]


def dual_step(field, ahead, dual, last):
    step = 0.5 * (ahead - field)
    return jnp.where(last, 0.0, clip(step if dual is None else dual + step))


def tile_duals(tile, dual_x, dual_y, sub, lane, shape):
    cells, width = shape
    new_x = dual_step(tile, pltpu.roll(tile, cells - 1, axis=0), dual_x, sub == cells - 1)
    new_y = dual_step(tile, pltpu.roll(tile, width - 1, axis=1), dual_y, lane == width - 1)
    spread = pltpu.roll(new_x, 1, axis=0) - new_x + (pltpu.roll(new_y, 1, axis=1) - new_y)
    return new_x, new_y, spread


def first_dual_kernel(maps_ref, zone_ref, ztwo_ref, *refs):
    elems, slices, cells, width = maps_ref.shape
    sides = beam_sides(cells)
    own_refs, refs = refs[: len(sides)], refs[len(sides) :]
    other_refs, refs = refs[: len(sides)], refs[len(sides) :]
    dual_z_ref, dual_x_ref, dual_y_ref, behind_ref, adj_ref, *edge_refs, ahead_ref = refs
    count, rank = lax.axis_size("gz"), lax.axis_index("gz")
    sub = lax.broadcasted_iota(jnp.int32, (cells, width), 0)
    lane = lax.broadcasted_iota(jnp.int32, (cells, width), 1)
    for (row, sign, there), own, other, edge in zip(sides, own_refs, other_refs, edge_refs):
        rows = pl.ds(0, elems * slices)
        edge[...] = clip(0.5 * face(own[rows], other[rows], sign, there))
    for e in range(elems):
        ahead, behind = pair_order(zone_ref[e], ztwo_ref[e])
        ahead_ref[e] = ahead
        behind_ref[e] = jnp.where(rank > 0, clip(0.5 * (maps_ref[e, 0] - behind)), 0.0)

    def step(z, behind):
        at_end = z == slices - 1
        zero_end = jnp.logical_and(at_end, rank == count - 1)
        duals = []
        for e in range(elems):
            tile = maps_ref[e, z]
            inner = maps_ref[e, jnp.minimum(z + 1, slices - 1)]
            ahead = jnp.where(at_end, ahead_ref[e], inner)
            dual_z = jnp.where(zero_end, 0.0, clip(0.5 * (ahead - tile)))
            dual_x, dual_y, spread = tile_duals(tile, None, None, sub, lane, (cells, width))
            dual_z_ref[e, z] = dual_z
            dual_x_ref[e, z] = dual_x
            dual_y_ref[e, z] = dual_y
            spread = spread + (behind[e] - dual_z)
            for (row, sign, there), edge in zip(sides, edge_refs):
                spread = spread + jnp.where(sub == row, sign * edge[pl.ds(e * slices + z, 1)], 0.0)
            adj_ref[e, z] = spread
            duals.append(dual_z)
        return tuple(duals)

    lax.fori_loop(0, slices, step, tuple(behind_ref[e] for e in range(elems)), unroll=UNROLL)


def join(ref, width):
    elems, cells, slices = ref.shape
    parts = [ref[e] for e in range(elems)]
    if elems * slices < width:
        parts.append(jnp.zeros((cells, width - elems * slices), F32))
    return jnp.concatenate(parts, axis=1)


def part(ref, pack):
    slices = ref.shape[2]
    for e in range(ref.shape[0]):
        ref[e] = pack[:, e * slices : (e + 1) * slices]


def first_update_kernel(total, size, maps_ref, weight_ref, adj_ref, coef_ref, measured_ref, *refs):
    elems, slices, cells, width = maps_ref.shape
    pack_refs, refs = refs[:size], refs[size:]
    full_ref, cur_ref, ext_ref, dd_ref, yedge_ref, out_ref, emission_ref, zone_ref, ztwo_ref, *face_refs = refs
    mine = lax.axis_index("path")
    pack_shape = (cells, width)
    lane = lax.broadcasted_iota(jnp.int32, pack_shape, 1)
    rim = (lane == 0) | (lane == width - 1)
    proj, whole, strip = [by_rank([ref[i] for ref in pack_refs], size) for i in range(3)]
    far = jnp.zeros(pack_shape, jnp.bool_)
    for e in range(elems):
        inside = (lane >= e * slices) & (lane < (e + 1) * slices)
        far = far | (inside & (coef_ref[elems * elems + e : elems * elems + e + 1][:, 0:1] != 0.0))
    below = [jnp.zeros(pack_shape, F32)]
    above = [jnp.zeros(pack_shape, F32)]
    for r in range(1, size):
        below.append(below[-1] + strip[r - 1])
        above.append(above[-1] + strip[size - r])
    factor = [jnp.exp(jnp.where(far, above[size - 1 - r], below[r]) * (-1.0 / total)) for r in range(size)]
    image = factor[0] * proj[0]
    weights = factor[0] * whole[0]
    own = factor[0]
    for r in range(1, size):
        image = image + factor[r] * proj[r]
        weights = weights + factor[r] * whole[r]
        own = jnp.where(mine == r, factor[r], own)
    sig = 1.0 / weights
    data_dual = sig * (image - join(measured_ref, width)) / (1.0 + sig)
    dd_ref[0] = data_dual
    dd_ref[1] = sig
    part(emission_ref, image * (1.0 / total))
    own_ref, after, before = pack_refs[0], pack_refs[size - 1], pack_refs[min(1, size - 1)]
    y_ahead = jnp.where(mine < size - 1, clip(0.5 * (after[3] - own_ref[4])), 0.0)
    y_behind = jnp.where(mine > 0, clip(0.5 * (own_ref[3] - before[4])), 0.0)
    joined = join_edges(y_behind, -y_ahead, lane)
    yedge_ref[0] = y_ahead
    yedge_ref[1] = y_behind

    def weigh(z, offset, none):
        for e in range(elems):
            weight = weight_ref[e, z] * spread(own, lane, e * slices + z)
            full_ref[e, z] = weight
            ext_ref[e, z] = weight * spread(data_dual, lane, e * slices + z) + adj_ref[e, z]
        return none

    def update(z, offset, edges):
        edges = list(edges)
        for e in range(elems):
            k, odd = e * slices + z, (e * slices + offset) % 2
            tile = maps_ref[e, z]
            new = tile - (ext_ref[e, z] + edge_columns(joined[odd], rim, k)) / (full_ref[e, z] + 6.0)
            new = jnp.maximum(new, 0.0)
            ext = 2.0 * new - tile
            cur_ref[e, z] = new
            ext_ref[e, z] = ext
            edges[odd] = gather_edges(edges[odd], ext, lane, k)
        return tuple(edges)

    def project(z, offset, image):
        for e in range(elems):
            row = jnp.sum(full_ref[e, z] * ext_ref[e, z], axis=1, keepdims=True)
            image = jnp.where(lane == e * slices + z, row, image)
        return image

    zero = jnp.zeros(pack_shape, F32)
    sweep(slices, weigh, 0)
    edges = sweep(slices, update, (zero, zero))
    out_ref[0] = sweep(slices, project, zero)
    out_ref[1], out_ref[2] = packed_edges(edges, lane)
    for e in range(elems):
        for z in range(slices):
            rows = beam_rows(ext_ref[e, z, 0:1], ext_ref[e, z, cells - 1 : cells])
            for ref, row in zip(face_refs, rows):
                ref[e * slices + z : e * slices + z + 1] = row
    for e in range(elems):
        zone_ref[e], ztwo_ref[e] = pair_order(ext_ref[e, slices - 1], ext_ref[e, 0])


def second_dual_kernel(ext_ref, dual_z_ref, dual_x_ref, dual_y_ref, adj_ref):
    elems, slices, cells, width = ext_ref.shape
    sub = lax.broadcasted_iota(jnp.int32, (cells, width), 0)
    lane = lax.broadcasted_iota(jnp.int32, (cells, width), 1)

    def step(z, behind):
        at_end = z == slices - 1
        duals = []
        for e in range(elems):
            tile = ext_ref[e, z]
            ahead = ext_ref[e, jnp.minimum(z + 1, slices - 1)]
            dual_z = jnp.where(at_end, 0.0, clip(dual_z_ref[e, z] + 0.5 * (ahead - tile)))
            _, _, spread = tile_duals(tile, dual_x_ref[e, z], dual_y_ref[e, z], sub, lane, (cells, width))
            adj_ref[e, z] = spread + (behind[e] - dual_z)
            duals.append(dual_z)
        return tuple(duals)

    zero = jnp.zeros((cells, width), F32)
    lax.fori_loop(0, slices, step, (zero,) * elems, unroll=UNROLL)


def last_update_kernel(size, cur_ref, ext_ref, weight_ref, adj_ref, measured_ref, dd_ref, yedge_ref, zedge_ref,
                       zbehind_ref, zone_ref, ztwo_ref, *refs):
    elems, slices, cells, width = cur_ref.shape
    sides = beam_sides(cells)
    pack_refs, refs = refs[:size], refs[size:]
    edge_refs, refs = refs[: len(sides)], refs[len(sides) :]
    own_refs, refs = refs[: len(sides)], refs[len(sides) :]
    other_refs, refs = refs[: len(sides)], refs[len(sides) :]
    new_ref, dual_ref, zface_ref, *face_refs = refs
    mine = lax.axis_index("path")
    count, rank = lax.axis_size("gz"), lax.axis_index("gz")
    images = by_rank([ref[0] for ref in pack_refs], size)
    image = images[0]
    for r in range(1, size):
        image = image + images[r]
    sig = dd_ref[1]
    data_dual = (dd_ref[0] + sig * (image - join(measured_ref, width))) / (1.0 + sig)
    part(dual_ref, data_dual)
    own_ref, after, before = pack_refs[0], pack_refs[size - 1], pack_refs[min(1, size - 1)]
    y_ahead = jnp.where(mine < size - 1, clip(yedge_ref[0] + 0.5 * (after[1] - own_ref[2])), 0.0)
    y_behind = jnp.where(mine > 0, clip(yedge_ref[1] + 0.5 * (own_ref[1] - before[2])), 0.0)
    for (row, sign, there), edge, own, other, out in zip(sides, edge_refs, own_refs, other_refs, face_refs):
        out[...] = clip(edge[...] + 0.5 * face(own[...], other[...], sign, there)) * sign
    sub = lax.broadcasted_iota(jnp.int32, (cells, width), 0)
    lane = lax.broadcasted_iota(jnp.int32, (cells, width), 1)
    rim = (lane == 0) | (lane == width - 1)
    joined = join_edges(y_behind, -y_ahead, lane)
    for e in range(elems):
        other_ahead, other_behind = pair_order(zone_ref[e], ztwo_ref[e])
        z_behind = clip(zbehind_ref[e] + 0.5 * (ext_ref[e, 0] - other_behind))
        z_ahead = clip(zedge_ref[e, slices - 1] + 0.5 * (other_ahead - ext_ref[e, slices - 1]))
        zface_ref[0, e] = jnp.where(rank > 0, z_behind, 0.0)
        zface_ref[1, e] = jnp.where(rank < count - 1, z_ahead, 0.0)

    def weigh(z, offset, none):
        for e in range(elems):
            new_ref[e, z] = weight_ref[e, z] * spread(data_dual, lane, e * slices + z) + adj_ref[e, z]
        return none

    def update(z, offset, none):
        for e in range(elems):
            k, odd = e * slices + z, (e * slices + offset) % 2
            step = new_ref[e, z] + edge_columns(joined[odd], rim, k)
            for (row, sign, there), out in zip(sides, face_refs):
                step = step + jnp.where(sub == row, out[pl.ds(k, 1)], 0.0)
            new_ref[e, z] = jnp.maximum(cur_ref[e, z] - step / (weight_ref[e, z] + 6.0), 0.0)
        return none

    sweep(slices, weigh, 0)
    for e in range(elems):
        new_ref[e, 0] = new_ref[e, 0] + zface_ref[0, e]
        new_ref[e, slices - 1] = new_ref[e, slices - 1] - zface_ref[1, e]
    sweep(slices, update, 0)


def shards(maps, measured, beta_table, view, kappa, line_of, side):
    elems, slices, cells, width = maps.shape
    total_x = cells * lax.axis_size("beam")
    total_y = width * lax.axis_size("path")
    size = lax.axis_size("path")
    block = f32(elems, slices, cells, width)
    plane = f32(elems, cells, width)
    rows = f32(elems * slices, width)
    faces = len(beam_sides(cells))
    measured = measured.transpose(0, 2, 1)
    kappa = kappa.T

    tall = f32((elems + 1) * slices, width)
    maps, inside, coef, zone, ztwo, *own = call(
        functools.partial(open_kernel, total_x),
        [view] + [pltpu.with_memory_space_constraint(a, pltpu.HBM) for a in (maps, beta_table, kappa, line_of, side)],
        [block, f32(slices, cells, width), f32(elems * elems + elems, width), plane, plane, tall] + [rows] * (faces - 1),
        [SMEM] + [pltpu.HBM] * 5,
        [
            pltpu.SMEM(beta_table.shape, F32),
            pltpu.SMEM(kappa.shape, F32),
            pltpu.SMEM(line_of.shape, jnp.int32),
            pltpu.SMEM(side.shape, jnp.int32),
            pltpu.SemaphoreType.DMA((5,)),
        ],
    )
    other = exchange_beam(own)
    carry, skip = other[-1], elems * slices
    beams = lax.axis_size("beam")
    if beams > 2:
        carry, skip = carry[skip:], 0
        reach = 1
        while reach < beams - 1:
            far = lax.axis_index("beam") > reach
            carry = carry + jnp.where(far, shifted(carry, "beam", reach), 0.0)
            reach *= 2
    zone, ztwo = swapped(zone, "gz", 0), swapped(ztwo, "gz", 1)
    local, pack = call(
        functools.partial(depth_kernel, total_y),
        [maps, coef],
        [block, f32(3, cells, width)],
        [VMEM] * 2,
        [
            pltpu.VMEM(maps.shape, F32),
            pltpu.VMEM((elems * slices * cells, 2 * width), jnp.bfloat16),
            pltpu.VMEM((elems * slices * cells, 2 * width), F32),
        ],
    )
    weight, pack = call(
        functools.partial(weight_kernel, total_x, skip),
        [maps, inside, carry, local, pack],
        [block, f32(5, cells, width)],
        [VMEM] * 5,
    )
    packs = around(pack, "path")
    dual_z, dual_x, dual_y, zdual, adj, *edge = call(
        first_dual_kernel,
        [maps, zone, ztwo, *own, *other],
        [block, block, block, plane, block] + [rows] * faces,
        [VMEM] * (3 + 2 * faces),
        [pltpu.VMEM(plane.shape, F32)],
    )
    weight, current, extrap, dd, yedge, pack, emission, zone, ztwo, *own = call(
        functools.partial(first_update_kernel, total_y, size),
        [maps, weight, adj, coef, measured, *packs],
        [block, block, block, f32(2, cells, width), f32(2, cells, width),
         f32(3, cells, width), f32(elems, cells, slices), plane, plane] + [rows] * faces,
        [VMEM] * (5 + size),
    )
    packs = around(pack, "path")
    zone, ztwo = swapped(zone, "gz", 0), swapped(ztwo, "gz", 1)
    other = exchange_beam(own)
    (adj,) = call(second_dual_kernel, [extrap, dual_z, dual_x, dual_y], [block], [VMEM] * 4)
    current, data_dual = call(
        functools.partial(last_update_kernel, size),
        [current, extrap, weight, adj, measured, dd, yedge, dual_z, zdual, zone, ztwo, *packs, *edge, *own, *other],
        [block, f32(elems, cells, slices)],
        [VMEM] * (11 + size + 3 * faces),
        [pltpu.VMEM((2, elems, cells, width), F32)] + [pltpu.VMEM((elems * slices, width), F32)] * faces,
    )
    return emission.transpose(0, 2, 1), current, data_dual.transpose(0, 2, 1)


def solution(mesh):
    return jax.shard_map(
        shards,
        mesh=mesh,
        in_specs=(P(None, "gz", "beam", "path"), P(None, "gz", "beam"), P(), P(), P(), P(), P()),
        out_specs=(P(None, "gz", "beam"), P(None, "gz", "beam", "path"), P(None, "gz", "beam")),
        check_vma=False,
    )
```

```python
import functools

import jax
import jax.numpy as jnp
from jax import lax
from jax.experimental import pallas as pl
from jax.experimental.pallas import tpu as pltpu
from jax.sharding import PartitionSpec as P

ITERS = 2
LAM = 0.1
F32 = jnp.float32
VMEM = pltpu.VMEM
SMEM = pltpu.SMEM
UNROLL = 4
VMEM_LIMIT = 32 * 1024 * 1024


def clip(value):
    return jnp.clip(value, -LAM, LAM)


def call(body, ins, outs, spaces, scratch=(), flops=1_000_000):
    specs = [pl.BlockSpec(memory_space=space) for space in spaces]
    moved = sum(a.size * 4 for a in ins) + sum(o.size * 4 for o in outs)
    return pl.pallas_call(
        body,
        out_shape=outs,
        in_specs=specs,
        out_specs=[pl.BlockSpec(memory_space=VMEM)] * len(outs),
        scratch_shapes=list(scratch),
        compiler_params=pltpu.CompilerParams(vmem_limit_bytes=VMEM_LIMIT),
        cost_estimate=pl.CostEstimate(flops=flops, bytes_accessed=moved, transcendentals=0),
    )(*ins)


def f32(*shape):
    return jax.ShapeDtypeStruct(shape, F32)


def shifted(block, axis, distance):
    n = lax.axis_size(axis)
    return lax.ppermute(block, axis, [((i - distance) % n, i) for i in range(n)])


def swapped(block, axis, start):
    n = lax.axis_size(axis)
    route = {i: i for i in range(n)}
    for i in range(start, n - 1, 2):
        route[i], route[i + 1] = i + 1, i
    if start and n % 2 == 0:
        route[0], route[n - 1] = n - 1, 0
    return lax.ppermute(block, axis, sorted(route.items()))


def pair_order(ahead, behind):
    even = lax.rem(lax.axis_index("gz"), 2) == 0
    return jnp.where(even, ahead, behind), jnp.where(even, behind, ahead)


def after(value, other):
    return lax.optimization_barrier((value, other))[0]


def halves(size):
    return 2 if size > 1 and size & (size - 1) == 0 else 1


def join_kernel(bit, axis, mine_ref, other_ref, out_ref):
    upper = (lax.axis_index(axis) & bit) != 0
    count = mine_ref.shape[0]
    for i in range(count):
        out_ref[i] = jnp.where(upper, other_ref[i], mine_ref[i])
        out_ref[count + i] = jnp.where(upper, mine_ref[i], other_ref[i])


def around(block, axis):
    n = lax.axis_size(axis)
    if halves(n) == 1:
        return [lax.all_gather(block, axis, axis=0, tiled=True)], block
    bit = 1
    while True:
        other = lax.ppermute(block, axis, [(i, i ^ bit) for i in range(n)])
        if 2 * bit == n:
            return [block, other], block
        count, *shape = block.shape
        (block,) = call(
            functools.partial(join_kernel, bit, axis), [block, other], [f32(2 * count, *shape)], [VMEM] * 2
        )
        bit *= 2


def by_rank(refs, size, count):
    if len(refs) == 1:
        return lambda rank, i: refs[0][rank * count + i]
    upper = (lax.axis_index("path") & (size // 2)) != 0

    def pick(rank, i):
        at = rank % (size // 2) * count + i
        mine, other = refs[0][at], refs[1][at]
        return jnp.where(upper, mine, other) if rank >= size // 2 else jnp.where(upper, other, mine)

    return pick


def neighbours(pick, size, first, last):
    mine = lax.axis_index("path")
    ahead, behind = pick(size - 1, first), pick(0, last)
    for rank in range(1, size):
        ahead = jnp.where(mine + 1 == rank, pick(rank, first), ahead)
        behind = jnp.where(mine - 1 == rank, pick(rank, last), behind)
    return ahead, behind


def spread(pack, lane, k):
    return jnp.sum(jnp.where(lane == k, pack, 0.0), axis=1, keepdims=True)


def gather_edges(pack, tile, lane, k):
    width = tile.shape[1]
    here = (lane == k) | (lane == lax.rem(k + width - 1, width))
    return jnp.where(here, pltpu.roll(tile, k, axis=1), pack)


def packed_edges(edges, lane):
    even = lane % 2 == 0
    first = jnp.where(even, edges[0], edges[1])
    return first, pltpu.roll(jnp.where(even, edges[1], edges[0]), 1, axis=1)


def join_edges(first, last, lane):
    width = first.shape[1]
    last = pltpu.roll(last, width - 1, axis=1)
    even = lane % 2 == 0
    return jnp.where(even, first, last), jnp.where(even, last, first)


def edge_columns(pack, rim, k):
    width = pack.shape[1]
    return jnp.where(rim, pltpu.roll(pack, lax.rem(width - k, width), axis=1), 0.0)


def sweep(slices, body, carry):
    group = UNROLL if slices % UNROLL == 0 else slices

    def step(i, carry):
        for offset in range(group):
            carry = body(group * i + offset, offset, carry)
        return carry

    return lax.fori_loop(0, slices // group, step, carry)


def beam_sides(cells):
    count, rank = lax.axis_size("beam"), lax.axis_index("beam")
    if count == 2:
        return [
            (
                jnp.where(rank == 0, cells - 1, 0),
                jnp.where(rank == 0, F32(-1.0), F32(1.0)),
                None,
            )
        ]
    return [(cells - 1, F32(-1.0), rank < count - 1), (0, F32(1.0), rank > 0)]


def beam_rows(first, last):
    count, rank = lax.axis_size("beam"), lax.axis_index("beam")
    if count == 2:
        return [jnp.where(rank == 0, last, first)]
    return [last, first]


def face(own, other, sign, there):
    step = (own - other) * sign
    return step if there is None else jnp.where(there, step, 0.0)


def exchange_beam(rows):
    if lax.axis_size("beam") == 2:
        return [lax.ppermute(rows[0], "beam", [(0, 1), (1, 0)])]
    return [shifted(rows[1], "beam", -1), shifted(rows[0], "beam", 1)]


def open_kernel(total, view_ref, source_ref, *refs):
    small, refs = refs[:4], refs[4:]
    maps_ref, inside_ref, coef_ref, zone_ref, ztwo_ref, *refs = refs
    elems, slices, cells, width = maps_ref.shape
    faces = len(beam_sides(cells))
    face_refs, refs = refs[:faces], refs[faces:]
    beta_ref, kappa_ref, line_ref, side_ref, sems = refs
    fetch = [pltpu.make_async_copy(source_ref, maps_ref, sems.at[0])]
    for i, (ref, kept) in enumerate(zip(small, (beta_ref, kappa_ref, line_ref, side_ref))):
        fetch.append(pltpu.make_async_copy(ref, kept, sems.at[i + 1]))
    for copy in fetch:
        copy.start()
    for copy in fetch[1:]:
        copy.wait()
    for e in range(elems):
        line = line_ref[e]
        for f in range(elems):
            coef_ref[e * elems + f : e * elems + f + 1] = jnp.full((1, width), kappa_ref[f, line])
        coef_ref[elems * elems + e : elems * elems + e + 1] = jnp.full((1, width), side_ref[e].astype(F32))
    fetch[0].wait()
    view = view_ref[0]
    beta = [beta_ref[view, e] for e in range(elems)]
    sub = lax.broadcasted_iota(jnp.int32, maps_ref.shape[2:], 0)
    for z in range(slices):
        tiles = [maps_ref[e, z] for e in range(elems)]
        mu = beta[0] * tiles[0]
        for e in range(1, elems):
            mu = mu + beta[e] * tiles[e]
        run = mu
        reach = 1
        while reach < cells:
            run = run + jnp.where(sub >= reach, pltpu.roll(run, reach, axis=0), 0.0)
            reach *= 2
        inside_ref[z] = jnp.where(sub >= 1, pltpu.roll(run, 1, axis=0), 0.0)
        face_refs[0][elems * slices + z : elems * slices + z + 1] = run[cells - 1 : cells]
        for e in range(elems):
            rows = beam_rows(tiles[e][0:1], tiles[e][cells - 1 : cells])
            for ref, row in zip(face_refs, rows):
                ref[e * slices + z : e * slices + z + 1] = row
    for e in range(elems):
        zone_ref[e], ztwo_ref[e] = pair_order(maps_ref[e, slices - 1], maps_ref[e, 0])


def depth_kernel(total, maps_ref, coef_ref, local_ref, pack_ref, mu_ref, parts_ref, sums_ref):
    elems, slices, cells, width = maps_ref.shape
    rows = slices * cells
    row = lax.broadcasted_iota(jnp.int32, (2 * width, 2 * width), 0)
    col = lax.broadcasted_iota(jnp.int32, (2 * width, 2 * width), 1)
    row = jnp.where(row >= width, row - width, row)
    table = jnp.where((row < col) | (col >= width), 1.0, 0.0).astype(jnp.bfloat16)
    for e in range(elems):
        mu = coef_ref[e * elems : e * elems + 1][None] * maps_ref[0]
        for f in range(1, elems):
            mu = mu + coef_ref[e * elems + f : e * elems + f + 1][None] * maps_ref[f]
        mu_ref[e] = mu
        flat = mu.reshape(rows, width)
        high = flat.astype(jnp.bfloat16)
        low = (flat - high.astype(F32)).astype(jnp.bfloat16)
        parts_ref[e * rows : (e + 1) * rows, 0:width] = high
        parts_ref[e * rows : (e + 1) * rows, width:] = low
    sums_ref[...] = jnp.dot(parts_ref[...], table, preferred_element_type=F32)
    lane = lax.broadcasted_iota(jnp.int32, (cells, width), 1)
    scale = -1.0 / total
    strip = jnp.zeros((cells, width), F32)
    edges = [strip, strip]
    for e in range(elems):
        forward = coef_ref[elems * elems + e : elems * elems + e + 1] == 0.0
        for z in range(slices):
            k = e * slices + z
            before = sums_ref[k * cells : (k + 1) * cells, 0:width]
            whole = sums_ref[k * cells : (k + 1) * cells, width:]
            after = whole - before - mu_ref[e, z]
            local_ref[e, z] = jnp.exp(jnp.where(forward, before, after) * scale)
            strip = jnp.where(lane == k, whole, strip)
            edges[k % 2] = gather_edges(edges[k % 2], maps_ref[e, z], lane, k)
    pack_ref[0] = strip
    pack_ref[1], pack_ref[2] = packed_edges(edges, lane)


def weight_kernel(total, skip, maps_ref, inside_ref, carry_ref, local_ref, pack_ref, weight_ref, out_ref):
    elems, slices, cells, width = maps_ref.shape
    lane = lax.broadcasted_iota(jnp.int32, (cells, width), 1)
    there = lax.axis_index("beam") > 0
    scale = -1.0 / total

    def step(z, packs):
        proj, whole = packs
        place = lane - z
        carry = jnp.where(there, carry_ref[pl.ds(skip + z, 1)], 0.0)
        att = jnp.exp((inside_ref[z] + carry) * scale)
        for e in range(elems):
            weight = att * local_ref[e, z]
            weight_ref[e, z] = weight
            here = place == e * slices
            proj = jnp.where(here, jnp.sum(weight * maps_ref[e, z], axis=1, keepdims=True), proj)
            whole = jnp.where(here, jnp.sum(weight, axis=1, keepdims=True), whole)
        return proj, whole

    zero = jnp.zeros((cells, width), F32)
    proj, whole = lax.fori_loop(0, slices, step, (zero, zero), unroll=UNROLL)
    out_ref[0] = proj
    out_ref[1] = whole
    out_ref[2] = pack_ref[0]
    out_ref[3] = pack_ref[1]
    out_ref[4] = pack_ref[2]


def dual_step(field, ahead, dual, last):
    step = 0.5 * (ahead - field)
    return jnp.where(last, 0.0, clip(step if dual is None else dual + step))


def tile_duals(tile, dual_x, dual_y, sub, lane, shape):
    cells, width = shape
    new_x = dual_step(tile, pltpu.roll(tile, cells - 1, axis=0), dual_x, sub == cells - 1)
    new_y = dual_step(tile, pltpu.roll(tile, width - 1, axis=1), dual_y, lane == width - 1)
    spread = pltpu.roll(new_x, 1, axis=0) - new_x + (pltpu.roll(new_y, 1, axis=1) - new_y)
    return new_x, new_y, spread


def first_dual_kernel(maps_ref, zone_ref, ztwo_ref, *refs):
    elems, slices, cells, width = maps_ref.shape
    sides = beam_sides(cells)
    own_refs, refs = refs[: len(sides)], refs[len(sides) :]
    other_refs, refs = refs[: len(sides)], refs[len(sides) :]
    dual_z_ref, dual_x_ref, dual_y_ref, behind_ref, adj_ref, *edge_refs, ahead_ref = refs
    count, rank = lax.axis_size("gz"), lax.axis_index("gz")
    sub = lax.broadcasted_iota(jnp.int32, (cells, width), 0)
    lane = lax.broadcasted_iota(jnp.int32, (cells, width), 1)
    for (row, sign, there), own, other, edge in zip(sides, own_refs, other_refs, edge_refs):
        rows = pl.ds(0, elems * slices)
        edge[...] = clip(0.5 * face(own[rows], other[rows], sign, there))
    for e in range(elems):
        ahead, behind = pair_order(zone_ref[e], ztwo_ref[e])
        ahead_ref[e] = ahead
        behind_ref[e] = jnp.where(rank > 0, clip(0.5 * (maps_ref[e, 0] - behind)), 0.0)

    def step(z, behind):
        at_end = z == slices - 1
        zero_end = jnp.logical_and(at_end, rank == count - 1)
        duals = []
        for e in range(elems):
            tile = maps_ref[e, z]
            inner = maps_ref[e, jnp.minimum(z + 1, slices - 1)]
            ahead = jnp.where(at_end, ahead_ref[e], inner)
            dual_z = jnp.where(zero_end, 0.0, clip(0.5 * (ahead - tile)))
            dual_x, dual_y, spread = tile_duals(tile, None, None, sub, lane, (cells, width))
            dual_z_ref[e, z] = dual_z
            dual_x_ref[e, z] = dual_x
            dual_y_ref[e, z] = dual_y
            spread = spread + (behind[e] - dual_z)
            for (row, sign, there), edge in zip(sides, edge_refs):
                spread = spread + jnp.where(sub == row, sign * edge[pl.ds(e * slices + z, 1)], 0.0)
            adj_ref[e, z] = spread
            duals.append(dual_z)
        return tuple(duals)

    lax.fori_loop(0, slices, step, tuple(behind_ref[e] for e in range(elems)), unroll=UNROLL)


def join(ref, width):
    elems, cells, slices = ref.shape
    parts = [ref[e] for e in range(elems)]
    if elems * slices < width:
        parts.append(jnp.zeros((cells, width - elems * slices), F32))
    return jnp.concatenate(parts, axis=1)


def part(ref, pack):
    slices = ref.shape[2]
    for e in range(ref.shape[0]):
        ref[e] = pack[:, e * slices : (e + 1) * slices]


def first_update_kernel(total, size, maps_ref, weight_ref, adj_ref, coef_ref, measured_ref, *refs):
    elems, slices, cells, width = maps_ref.shape
    pack_refs, refs = refs[: halves(size)], refs[halves(size) :]
    own_ref, *refs = refs
    full_ref, cur_ref, ext_ref, dd_ref, yedge_ref, out_ref, emission_ref, zone_ref, ztwo_ref, *face_refs = refs
    mine = lax.axis_index("path")
    pack_shape = (cells, width)
    lane = lax.broadcasted_iota(jnp.int32, pack_shape, 1)
    rim = (lane == 0) | (lane == width - 1)
    pick = by_rank(pack_refs, size, 5)
    proj, whole, strip = [[pick(r, i) for r in range(size)] for i in range(3)]
    far = jnp.zeros(pack_shape, jnp.bool_)
    for e in range(elems):
        inside = (lane >= e * slices) & (lane < (e + 1) * slices)
        far = far | (inside & (coef_ref[elems * elems + e : elems * elems + e + 1][:, 0:1] != 0.0))
    below = [jnp.zeros(pack_shape, F32)]
    above = [jnp.zeros(pack_shape, F32)]
    for r in range(1, size):
        below.append(below[-1] + strip[r - 1])
        above.append(above[-1] + strip[size - r])
    factor = [jnp.exp(jnp.where(far, above[size - 1 - r], below[r]) * (-1.0 / total)) for r in range(size)]
    image = factor[0] * proj[0]
    weights = factor[0] * whole[0]
    own = factor[0]
    for r in range(1, size):
        image = image + factor[r] * proj[r]
        weights = weights + factor[r] * whole[r]
        own = jnp.where(mine == r, factor[r], own)
    sig = 1.0 / weights
    data_dual = sig * (image - join(measured_ref, width)) / (1.0 + sig)
    dd_ref[0] = data_dual
    dd_ref[1] = sig
    part(emission_ref, image * (1.0 / total))
    ahead, behind = neighbours(pick, size, 3, 4)
    y_ahead = jnp.where(mine < size - 1, clip(0.5 * (ahead - own_ref[4])), 0.0)
    y_behind = jnp.where(mine > 0, clip(0.5 * (own_ref[3] - behind)), 0.0)
    joined = join_edges(y_behind, -y_ahead, lane)
    yedge_ref[0] = y_ahead
    yedge_ref[1] = y_behind

    def weigh(z, offset, none):
        for e in range(elems):
            weight = weight_ref[e, z] * spread(own, lane, e * slices + z)
            full_ref[e, z] = weight
            ext_ref[e, z] = weight * spread(data_dual, lane, e * slices + z) + adj_ref[e, z]
        return none

    def update(z, offset, edges):
        edges = list(edges)
        for e in range(elems):
            k, odd = e * slices + z, (e * slices + offset) % 2
            tile = maps_ref[e, z]
            new = tile - (ext_ref[e, z] + edge_columns(joined[odd], rim, k)) / (full_ref[e, z] + 6.0)
            new = jnp.maximum(new, 0.0)
            ext = 2.0 * new - tile
            cur_ref[e, z] = new
            ext_ref[e, z] = ext
            edges[odd] = gather_edges(edges[odd], ext, lane, k)
        return tuple(edges)

    def project(z, offset, image):
        for e in range(elems):
            row = jnp.sum(full_ref[e, z] * ext_ref[e, z], axis=1, keepdims=True)
            image = jnp.where(lane == e * slices + z, row, image)
        return image

    zero = jnp.zeros(pack_shape, F32)
    sweep(slices, weigh, 0)
    edges = sweep(slices, update, (zero, zero))
    out_ref[0] = sweep(slices, project, zero)
    out_ref[1], out_ref[2] = packed_edges(edges, lane)
    for e in range(elems):
        for z in range(slices):
            rows = beam_rows(ext_ref[e, z, 0:1], ext_ref[e, z, cells - 1 : cells])
            for ref, row in zip(face_refs, rows):
                ref[e * slices + z : e * slices + z + 1] = row
    for e in range(elems):
        zone_ref[e], ztwo_ref[e] = pair_order(ext_ref[e, slices - 1], ext_ref[e, 0])


def second_dual_kernel(ext_ref, dual_z_ref, dual_x_ref, dual_y_ref, adj_ref):
    elems, slices, cells, width = ext_ref.shape
    sub = lax.broadcasted_iota(jnp.int32, (cells, width), 0)
    lane = lax.broadcasted_iota(jnp.int32, (cells, width), 1)

    def step(z, behind):
        at_end = z == slices - 1
        duals = []
        for e in range(elems):
            tile = ext_ref[e, z]
            ahead = ext_ref[e, jnp.minimum(z + 1, slices - 1)]
            dual_z = jnp.where(at_end, 0.0, clip(dual_z_ref[e, z] + 0.5 * (ahead - tile)))
            _, _, spread = tile_duals(tile, dual_x_ref[e, z], dual_y_ref[e, z], sub, lane, (cells, width))
            adj_ref[e, z] = spread + (behind[e] - dual_z)
            duals.append(dual_z)
        return tuple(duals)

    zero = jnp.zeros((cells, width), F32)
    lax.fori_loop(0, slices, step, (zero,) * elems, unroll=UNROLL)


def last_update_kernel(size, cur_ref, ext_ref, weight_ref, adj_ref, measured_ref, dd_ref, yedge_ref, zedge_ref,
                       zbehind_ref, zone_ref, ztwo_ref, *refs):
    elems, slices, cells, width = cur_ref.shape
    sides = beam_sides(cells)
    pack_refs, refs = refs[: halves(size)], refs[halves(size) :]
    own_pack_ref, *refs = refs
    edge_refs, refs = refs[: len(sides)], refs[len(sides) :]
    own_refs, refs = refs[: len(sides)], refs[len(sides) :]
    other_refs, refs = refs[: len(sides)], refs[len(sides) :]
    new_ref, dual_ref, zface_ref, *face_refs = refs
    mine = lax.axis_index("path")
    count, rank = lax.axis_size("gz"), lax.axis_index("gz")
    pick = by_rank(pack_refs, size, 3)
    image = pick(0, 0)
    for r in range(1, size):
        image = image + pick(r, 0)
    sig = dd_ref[1]
    data_dual = (dd_ref[0] + sig * (image - join(measured_ref, width))) / (1.0 + sig)
    part(dual_ref, data_dual)
    ahead, behind = neighbours(pick, size, 1, 2)
    y_ahead = jnp.where(mine < size - 1, clip(yedge_ref[0] + 0.5 * (ahead - own_pack_ref[2])), 0.0)
    y_behind = jnp.where(mine > 0, clip(yedge_ref[1] + 0.5 * (own_pack_ref[1] - behind)), 0.0)
    for (row, sign, there), edge, own, other, out in zip(sides, edge_refs, own_refs, other_refs, face_refs):
        out[...] = clip(edge[...] + 0.5 * face(own[...], other[...], sign, there)) * sign
    sub = lax.broadcasted_iota(jnp.int32, (cells, width), 0)
    lane = lax.broadcasted_iota(jnp.int32, (cells, width), 1)
    rim = (lane == 0) | (lane == width - 1)
    joined = join_edges(y_behind, -y_ahead, lane)
    for e in range(elems):
        other_ahead, other_behind = pair_order(zone_ref[e], ztwo_ref[e])
        z_behind = clip(zbehind_ref[e] + 0.5 * (ext_ref[e, 0] - other_behind))
        z_ahead = clip(zedge_ref[e, slices - 1] + 0.5 * (other_ahead - ext_ref[e, slices - 1]))
        zface_ref[0, e] = jnp.where(rank > 0, z_behind, 0.0)
        zface_ref[1, e] = jnp.where(rank < count - 1, z_ahead, 0.0)

    def weigh(z, offset, none):
        for e in range(elems):
            new_ref[e, z] = weight_ref[e, z] * spread(data_dual, lane, e * slices + z) + adj_ref[e, z]
        return none

    def update(z, offset, none):
        for e in range(elems):
            k, odd = e * slices + z, (e * slices + offset) % 2
            step = new_ref[e, z] + edge_columns(joined[odd], rim, k)
            for (row, sign, there), out in zip(sides, face_refs):
                step = step + jnp.where(sub == row, out[pl.ds(k, 1)], 0.0)
            new_ref[e, z] = jnp.maximum(cur_ref[e, z] - step / (weight_ref[e, z] + 6.0), 0.0)
        return none

    sweep(slices, weigh, 0)
    for e in range(elems):
        new_ref[e, 0] = new_ref[e, 0] + zface_ref[0, e]
        new_ref[e, slices - 1] = new_ref[e, slices - 1] - zface_ref[1, e]
    sweep(slices, update, 0)


def shards(maps, measured, beta_table, view, kappa, line_of, side):
    elems, slices, cells, width = maps.shape
    total_x = cells * lax.axis_size("beam")
    total_y = width * lax.axis_size("path")
    size = lax.axis_size("path")
    block = f32(elems, slices, cells, width)
    plane = f32(elems, cells, width)
    rows = f32(elems * slices, width)
    faces = len(beam_sides(cells))
    measured = measured.transpose(0, 2, 1)
    kappa = kappa.T

    tall = f32((elems + 1) * slices, width)
    maps, inside, coef, zone, ztwo, *own = call(
        functools.partial(open_kernel, total_x),
        [view] + [pltpu.with_memory_space_constraint(a, pltpu.HBM) for a in (maps, beta_table, kappa, line_of, side)],
        [block, f32(slices, cells, width), f32(elems * elems + elems, width), plane, plane, tall] + [rows] * (faces - 1),
        [SMEM] + [pltpu.HBM] * 5,
        [
            pltpu.SMEM(beta_table.shape, F32),
            pltpu.SMEM(kappa.shape, F32),
            pltpu.SMEM(line_of.shape, jnp.int32),
            pltpu.SMEM(side.shape, jnp.int32),
            pltpu.SemaphoreType.DMA((5,)),
        ],
    )
    other = exchange_beam(own)
    carry, skip = other[-1], elems * slices
    beams = lax.axis_size("beam")
    if beams > 2:
        carry, skip = carry[skip:], 0
        reach = 1
        while reach < beams - 1:
            far = lax.axis_index("beam") > reach
            carry = carry + jnp.where(far, shifted(carry, "beam", reach), 0.0)
            reach *= 2
    local, pack = call(
        functools.partial(depth_kernel, total_y),
        [maps, coef],
        [block, f32(3, cells, width)],
        [VMEM] * 2,
        [
            pltpu.VMEM(maps.shape, F32),
            pltpu.VMEM((elems * slices * cells, 2 * width), jnp.bfloat16),
            pltpu.VMEM((elems * slices * cells, 2 * width), F32),
        ],
    )
    weight, pack = call(
        functools.partial(weight_kernel, total_x, skip),
        [maps, inside, carry, local, pack],
        [block, f32(5, cells, width)],
        [VMEM] * 5,
    )
    packs, joined = around(pack, "path")
    zone, ztwo = swapped(after(zone, pack), "gz", 0), swapped(after(ztwo, joined), "gz", 1)
    dual_z, dual_x, dual_y, zdual, adj, *edge = call(
        first_dual_kernel,
        [maps, zone, ztwo, *own, *other],
        [block, block, block, plane, block] + [rows] * faces,
        [VMEM] * (3 + 2 * faces),
        [pltpu.VMEM(plane.shape, F32)],
    )
    weight, current, extrap, dd, yedge, pack, emission, zone, ztwo, *own = call(
        functools.partial(first_update_kernel, total_y, size),
        [maps, weight, adj, coef, measured, *packs, pack],
        [block, block, block, f32(2, cells, width), f32(2, cells, width),
         f32(3, cells, width), f32(elems, cells, slices), plane, plane] + [rows] * faces,
        [VMEM] * (6 + len(packs)),
    )
    packs, joined = around(pack, "path")
    zone, ztwo = swapped(zone, "gz", 0), swapped(after(ztwo, joined), "gz", 1)
    other = exchange_beam(own)
    (adj,) = call(second_dual_kernel, [extrap, dual_z, dual_x, dual_y], [block], [VMEM] * 4)
    current, data_dual = call(
        functools.partial(last_update_kernel, size),
        [current, extrap, weight, adj, measured, dd, yedge, dual_z, zdual, zone, ztwo, *packs, pack, *edge, *own, *other],
        [block, f32(elems, cells, slices)],
        [VMEM] * (12 + len(packs) + 3 * faces),
        [pltpu.VMEM((2, elems, cells, width), F32)] + [pltpu.VMEM((elems * slices, width), F32)] * faces,
    )
    return emission.transpose(0, 2, 1), current, data_dual.transpose(0, 2, 1)


def solution(mesh):
    return jax.shard_map(
        shards,
        mesh=mesh,
        in_specs=(P(None, "gz", "beam", "path"), P(None, "gz", "beam"), P(), P(), P(), P(), P()),
        out_specs=(P(None, "gz", "beam"), P(None, "gz", "beam", "path"), P(None, "gz", "beam")),
        check_vma=False,
    )
```

```python
import functools

import jax
import jax.numpy as jnp
from jax import lax
from jax.experimental import pallas as pl
from jax.experimental.pallas import tpu as pltpu
from jax.sharding import PartitionSpec as P

ITERS = 2
LAM = 0.1
F32 = jnp.float32
VMEM = pltpu.VMEM
SMEM = pltpu.SMEM
UNROLL = 4
VMEM_LIMIT = 32 * 1024 * 1024


def clip(value):
    return jnp.clip(value, -LAM, LAM)


def call(body, ins, outs, spaces, scratch=(), out_spaces=None, flops=1_000_000):
    specs = [pl.BlockSpec(memory_space=space) for space in spaces]
    moved = sum(a.size * 4 for a in ins) + sum(o.size * 4 for o in outs)
    return pl.pallas_call(
        body,
        out_shape=outs,
        in_specs=specs,
        out_specs=[pl.BlockSpec(memory_space=space) for space in out_spaces or [VMEM] * len(outs)],
        scratch_shapes=list(scratch),
        compiler_params=pltpu.CompilerParams(vmem_limit_bytes=VMEM_LIMIT),
        cost_estimate=pl.CostEstimate(flops=flops, bytes_accessed=moved, transcendentals=0),
    )(*ins)


def f32(*shape):
    return jax.ShapeDtypeStruct(shape, F32)


def shifted(block, axis, distance):
    n = lax.axis_size(axis)
    return lax.ppermute(block, axis, [((i - distance) % n, i) for i in range(n)])


def swapped(block, axis, start):
    n = lax.axis_size(axis)
    route = {i: i for i in range(n)}
    for i in range(start, n - 1, 2):
        route[i], route[i + 1] = i + 1, i
    if start and n % 2 == 0:
        route[0], route[n - 1] = n - 1, 0
    return lax.ppermute(block, axis, sorted(route.items()))


def pair_order(ahead, behind):
    even = lax.rem(lax.axis_index("gz"), 2) == 0
    return jnp.where(even, ahead, behind), jnp.where(even, behind, ahead)


def after(value, other):
    return lax.optimization_barrier((value, other))[0]


def around_direct(block, axis):
    return [block] + [shifted(block, axis, s) for s in range(1, lax.axis_size(axis))]


def by_distance(refs, size):
    mine = lax.axis_index("path")

    def pick(rank, i):
        value = refs[0][i]
        for s in range(1, size):
            value = jnp.where(lax.rem(mine - s + size, size) == rank, refs[s][i], value)
        return value

    return pick


def halves(size):
    return 2 if size > 1 and size & (size - 1) == 0 else 1


def join_kernel(bit, axis, mine_ref, other_ref, out_ref):
    upper = (lax.axis_index(axis) & bit) != 0
    count = mine_ref.shape[0]
    for i in range(count):
        out_ref[i] = jnp.where(upper, other_ref[i], mine_ref[i])
        out_ref[count + i] = jnp.where(upper, mine_ref[i], other_ref[i])


def around(block, axis):
    n = lax.axis_size(axis)
    if halves(n) == 1:
        return [lax.all_gather(block, axis, axis=0, tiled=True)], block
    bit = 1
    while True:
        other = lax.ppermute(block, axis, [(i, i ^ bit) for i in range(n)])
        if 2 * bit == n:
            return [block, other], block
        count, *shape = block.shape
        (block,) = call(
            functools.partial(join_kernel, bit, axis), [block, other], [f32(2 * count, *shape)], [VMEM] * 2
        )
        bit *= 2


def by_rank(refs, size, count):
    if len(refs) == 1:
        return lambda rank, i: refs[0][rank * count + i]
    upper = (lax.axis_index("path") & (size // 2)) != 0

    def pick(rank, i):
        at = rank % (size // 2) * count + i
        mine, other = refs[0][at], refs[1][at]
        return jnp.where(upper, mine, other) if rank >= size // 2 else jnp.where(upper, other, mine)

    return pick


def neighbours(pick, size, first, last):
    mine = lax.axis_index("path")
    ahead, behind = pick(size - 1, first), pick(0, last)
    for rank in range(1, size):
        ahead = jnp.where(mine + 1 == rank, pick(rank, first), ahead)
        behind = jnp.where(mine - 1 == rank, pick(rank, last), behind)
    return ahead, behind


def spread(pack, lane, k):
    return jnp.sum(jnp.where(lane == k, pack, 0.0), axis=1, keepdims=True)


def gather_edges(pack, tile, lane, k):
    width = tile.shape[1]
    here = (lane == k) | (lane == lax.rem(k + width - 1, width))
    return jnp.where(here, pltpu.roll(tile, k, axis=1), pack)


def packed_edges(edges, lane):
    even = lane % 2 == 0
    first = jnp.where(even, edges[0], edges[1])
    return first, pltpu.roll(jnp.where(even, edges[1], edges[0]), 1, axis=1)


def join_edges(first, last, lane):
    width = first.shape[1]
    last = pltpu.roll(last, width - 1, axis=1)
    even = lane % 2 == 0
    return jnp.where(even, first, last), jnp.where(even, last, first)


def edge_columns(pack, rim, k):
    width = pack.shape[1]
    return jnp.where(rim, pltpu.roll(pack, lax.rem(width - k, width), axis=1), 0.0)


def slice_group(slices):
    return UNROLL if slices % UNROLL == 0 else slices


def sweep(slices, body, carry):
    group = slice_group(slices)

    def step(i, carry):
        for offset in range(group):
            carry = body(group * i + offset, offset, carry)
        return carry

    return lax.fori_loop(0, slices // group, step, carry)


def beam_sides(cells):
    count, rank = lax.axis_size("beam"), lax.axis_index("beam")
    if count == 2:
        return [
            (
                jnp.where(rank == 0, cells - 1, 0),
                jnp.where(rank == 0, F32(-1.0), F32(1.0)),
                None,
            )
        ]
    return [(cells - 1, F32(-1.0), rank < count - 1), (0, F32(1.0), rank > 0)]


def beam_rows(first, last):
    count, rank = lax.axis_size("beam"), lax.axis_index("beam")
    if count == 2:
        return [jnp.where(rank == 0, last, first)]
    return [last, first]


def face(own, other, sign, there):
    step = (own - other) * sign
    return step if there is None else jnp.where(there, step, 0.0)


def exchange_beam(rows):
    if lax.axis_size("beam") == 2:
        return [lax.ppermute(rows[0], "beam", [(0, 1), (1, 0)])]
    return [shifted(rows[1], "beam", -1), shifted(rows[0], "beam", 1)]


def open_kernel(total, view_ref, source_ref, *refs):
    small, refs = refs[:4], refs[4:]
    maps_ref, inside_ref, coef_ref, zone_ref, ztwo_ref, *refs = refs
    elems, slices, cells, width = maps_ref.shape
    faces = len(beam_sides(cells))
    face_refs, refs = refs[:faces], refs[faces:]
    beta_ref, kappa_ref, line_ref, side_ref, sems = refs
    half = slices // 2
    parts = [pl.ds(0, half), pl.ds(half, slices - half)] if half else [pl.ds(0, slices)]
    fetch = []
    for i, (ref, kept) in enumerate(zip(small, (beta_ref, kappa_ref, line_ref, side_ref))):
        fetch.append(pltpu.make_async_copy(ref, kept, sems.at[i]))
    large = []
    for i, at in enumerate(parts):
        large.append(pltpu.make_async_copy(source_ref.at[:, at], maps_ref.at[:, at], sems.at[len(small) + i]))
    for copy in large[:1] + fetch + large[1:]:
        copy.start()
    for copy in fetch:
        copy.wait()
    for e in range(elems):
        line = line_ref[e]
        for f in range(elems):
            coef_ref[e * elems + f : e * elems + f + 1] = jnp.full((1, width), kappa_ref[f, line])
        coef_ref[elems * elems + e : elems * elems + e + 1] = jnp.full((1, width), side_ref[e].astype(F32))
    view = view_ref[0]
    beta = [beta_ref[view, e] for e in range(elems)]
    sub = lax.broadcasted_iota(jnp.int32, maps_ref.shape[2:], 0)
    for z in range(slices):
        if z == 0 or z == half:
            large[1 if z else 0].wait()
        tiles = [maps_ref[e, z] for e in range(elems)]
        mu = beta[0] * tiles[0]
        for e in range(1, elems):
            mu = mu + beta[e] * tiles[e]
        run = mu
        reach = 1
        while reach < cells:
            run = run + jnp.where(sub >= reach, pltpu.roll(run, reach, axis=0), 0.0)
            reach *= 2
        inside_ref[z] = jnp.where(sub >= 1, pltpu.roll(run, 1, axis=0), 0.0)
        face_refs[0][elems * slices + z : elems * slices + z + 1] = run[cells - 1 : cells]
        for e in range(elems):
            rows = beam_rows(tiles[e][0:1], tiles[e][cells - 1 : cells])
            for ref, row in zip(face_refs, rows):
                ref[e * slices + z : e * slices + z + 1] = row
    for e in range(elems):
        zone_ref[e], ztwo_ref[e] = pair_order(maps_ref[e, slices - 1], maps_ref[e, 0])


def depth_kernel(total, maps_ref, coef_ref, local_ref, pack_ref, mu_ref, parts_ref, sums_ref):
    elems, slices, cells, width = maps_ref.shape
    rows = slices * cells
    row = lax.broadcasted_iota(jnp.int32, (2 * width, 2 * width), 0)
    col = lax.broadcasted_iota(jnp.int32, (2 * width, 2 * width), 1)
    row = jnp.where(row >= width, row - width, row)
    table = jnp.where((row < col) | (col >= width), 1.0, 0.0).astype(jnp.bfloat16)
    for e in range(elems):
        mu = coef_ref[e * elems : e * elems + 1][None] * maps_ref[0]
        for f in range(1, elems):
            mu = mu + coef_ref[e * elems + f : e * elems + f + 1][None] * maps_ref[f]
        mu_ref[e] = mu
        flat = mu.reshape(rows, width)
        high = flat.astype(jnp.bfloat16)
        low = (flat - high.astype(F32)).astype(jnp.bfloat16)
        parts_ref[e * rows : (e + 1) * rows, 0:width] = high
        parts_ref[e * rows : (e + 1) * rows, width:] = low
    sums_ref[...] = jnp.dot(parts_ref[...], table, preferred_element_type=F32)
    lane = lax.broadcasted_iota(jnp.int32, (cells, width), 1)
    scale = -1.0 / total
    strip = jnp.zeros((cells, width), F32)
    edges = [strip, strip]
    for e in range(elems):
        forward = coef_ref[elems * elems + e : elems * elems + e + 1] == 0.0
        for z in range(slices):
            k = e * slices + z
            before = sums_ref[k * cells : (k + 1) * cells, 0:width]
            whole = sums_ref[k * cells : (k + 1) * cells, width:]
            after = whole - before - mu_ref[e, z]
            local_ref[e, z] = jnp.exp(jnp.where(forward, before, after) * scale)
            strip = jnp.where(lane == k, whole, strip)
            edges[k % 2] = gather_edges(edges[k % 2], maps_ref[e, z], lane, k)
    pack_ref[0] = strip
    pack_ref[1], pack_ref[2] = packed_edges(edges, lane)


def weight_kernel(total, skip, maps_ref, inside_ref, carry_ref, local_ref, pack_ref, weight_ref, out_ref):
    elems, slices, cells, width = maps_ref.shape
    lane = lax.broadcasted_iota(jnp.int32, (cells, width), 1)
    there = lax.axis_index("beam") > 0
    scale = -1.0 / total

    def step(z, packs):
        proj, whole = packs
        place = lane - z
        carry = jnp.where(there, carry_ref[pl.ds(skip + z, 1)], 0.0)
        att = jnp.exp((inside_ref[z] + carry) * scale)
        for e in range(elems):
            weight = att * local_ref[e, z]
            weight_ref[e, z] = weight
            here = place == e * slices
            proj = jnp.where(here, jnp.sum(weight * maps_ref[e, z], axis=1, keepdims=True), proj)
            whole = jnp.where(here, jnp.sum(weight, axis=1, keepdims=True), whole)
        return proj, whole

    zero = jnp.zeros((cells, width), F32)
    proj, whole = lax.fori_loop(0, slices, step, (zero, zero), unroll=UNROLL)
    out_ref[0] = proj
    out_ref[1] = whole
    out_ref[2] = pack_ref[0]
    out_ref[3] = pack_ref[1]
    out_ref[4] = pack_ref[2]


def dual_step(field, ahead, dual, last):
    step = 0.5 * (ahead - field)
    return jnp.where(last, 0.0, clip(step if dual is None else dual + step))


def tile_duals(tile, dual_x, dual_y, sub, lane, shape):
    cells, width = shape
    new_x = dual_step(tile, pltpu.roll(tile, cells - 1, axis=0), dual_x, sub == cells - 1)
    new_y = dual_step(tile, pltpu.roll(tile, width - 1, axis=1), dual_y, lane == width - 1)
    spread = pltpu.roll(new_x, 1, axis=0) - new_x + (pltpu.roll(new_y, 1, axis=1) - new_y)
    return new_x, new_y, spread


def join(ref, width):
    elems, cells, slices = ref.shape
    parts = [ref[e] for e in range(elems)]
    if elems * slices < width:
        parts.append(jnp.zeros((cells, width - elems * slices), F32))
    return jnp.concatenate(parts, axis=1)


def first_dual_kernel(maps_ref, zone_ref, ztwo_ref, measured_ref, coef_ref, *refs):
    elems, slices, cells, width = maps_ref.shape
    sides = beam_sides(cells)
    own_refs, refs = refs[: len(sides)], refs[len(sides) :]
    other_refs, refs = refs[: len(sides)], refs[len(sides) :]
    dual_z_ref, dual_x_ref, dual_y_ref, behind_ref, adj_ref, still_ref, *edge_refs, ahead_ref = refs
    count, rank = lax.axis_size("gz"), lax.axis_index("gz")
    sub = lax.broadcasted_iota(jnp.int32, (cells, width), 0)
    lane = lax.broadcasted_iota(jnp.int32, (cells, width), 1)
    still_ref[0] = join(measured_ref, width)
    far = jnp.zeros((cells, width), F32)
    for e in range(elems):
        inside = (lane >= e * slices) & (lane < (e + 1) * slices)
        far = jnp.where(inside, coef_ref[elems * elems + e : elems * elems + e + 1][:, 0:1], far)
    still_ref[1] = far
    for (row, sign, there), own, other, edge in zip(sides, own_refs, other_refs, edge_refs):
        rows = pl.ds(0, elems * slices)
        edge[...] = clip(0.5 * face(own[rows], other[rows], sign, there))
    for e in range(elems):
        ahead, behind = pair_order(zone_ref[e], ztwo_ref[e])
        ahead_ref[e] = ahead
        behind_ref[e] = jnp.where(rank > 0, clip(0.5 * (maps_ref[e, 0] - behind)), 0.0)

    def step(z, behind):
        at_end = z == slices - 1
        zero_end = jnp.logical_and(at_end, rank == count - 1)
        duals = []
        for e in range(elems):
            tile = maps_ref[e, z]
            inner = maps_ref[e, jnp.minimum(z + 1, slices - 1)]
            ahead = jnp.where(at_end, ahead_ref[e], inner)
            dual_z = jnp.where(zero_end, 0.0, clip(0.5 * (ahead - tile)))
            dual_x, dual_y, spread = tile_duals(tile, None, None, sub, lane, (cells, width))
            dual_z_ref[e, z] = dual_z
            dual_x_ref[e, z] = dual_x
            dual_y_ref[e, z] = dual_y
            spread = spread + (behind[e] - dual_z)
            for (row, sign, there), edge in zip(sides, edge_refs):
                spread = spread + jnp.where(sub == row, sign * edge[pl.ds(e * slices + z, 1)], 0.0)
            adj_ref[e, z] = spread
            duals.append(dual_z)
        return tuple(duals)

    lax.fori_loop(0, slices, step, tuple(behind_ref[e] for e in range(elems)), unroll=UNROLL)


def part(ref, pack):
    slices = ref.shape[2]
    for e in range(ref.shape[0]):
        ref[e] = pack[:, e * slices : (e + 1) * slices]


def first_update_kernel(total, size, maps_ref, weight_ref, adj_ref, still_ref, *refs):
    elems, slices, cells, width = maps_ref.shape
    pack_refs, refs = refs[:size], refs[size:]
    full_ref, cur_ref, ext_ref, dd_ref, yedge_ref, out_ref, emission_ref = refs
    own_ref = pack_refs[0]
    mine = lax.axis_index("path")
    pack_shape = (cells, width)
    lane = lax.broadcasted_iota(jnp.int32, pack_shape, 1)
    rim = (lane == 0) | (lane == width - 1)
    pick = by_distance(pack_refs, size)
    proj, whole, strip = [[pick(r, i) for r in range(size)] for i in range(3)]
    far = still_ref[1] != 0.0
    below = [jnp.zeros(pack_shape, F32)]
    above = [jnp.zeros(pack_shape, F32)]
    for r in range(1, size):
        below.append(below[-1] + strip[r - 1])
        above.append(above[-1] + strip[size - r])
    factor = [jnp.exp(jnp.where(far, above[size - 1 - r], below[r]) * (-1.0 / total)) for r in range(size)]
    image = factor[0] * proj[0]
    weights = factor[0] * whole[0]
    own = factor[0]
    for r in range(1, size):
        image = image + factor[r] * proj[r]
        weights = weights + factor[r] * whole[r]
        own = jnp.where(mine == r, factor[r], own)
    sig = 1.0 / weights
    data_dual = sig * (image - still_ref[0]) / (1.0 + sig)
    dd_ref[0] = data_dual
    dd_ref[1] = sig
    part(emission_ref, image * (1.0 / total))
    ahead, behind = neighbours(pick, size, 3, 4)
    y_ahead = jnp.where(mine < size - 1, clip(0.5 * (ahead - own_ref[4])), 0.0)
    y_behind = jnp.where(mine > 0, clip(0.5 * (own_ref[3] - behind)), 0.0)
    joined = join_edges(y_behind, -y_ahead, lane)
    yedge_ref[0] = y_ahead
    yedge_ref[1] = y_behind

    def weigh(z, offset, none):
        for e in range(elems):
            weight = weight_ref[e, z] * spread(own, lane, e * slices + z)
            full_ref[e, z] = weight
            ext_ref[e, z] = weight * spread(data_dual, lane, e * slices + z) + adj_ref[e, z]
        return none

    def update(z, offset, edges):
        edges = list(edges)
        for e in range(elems):
            k, odd = e * slices + z, (e * slices + offset) % 2
            tile = maps_ref[e, z]
            new = tile - (ext_ref[e, z] + edge_columns(joined[odd], rim, k)) / (full_ref[e, z] + 6.0)
            new = jnp.maximum(new, 0.0)
            ext = 2.0 * new - tile
            cur_ref[e, z] = new
            ext_ref[e, z] = ext
            edges[odd] = gather_edges(edges[odd], ext, lane, k)
        return tuple(edges)

    def project(z, offset, image):
        for e in range(elems):
            row = jnp.sum(full_ref[e, z] * ext_ref[e, z], axis=1, keepdims=True)
            image = jnp.where(lane == e * slices + z, row, image)
        return image

    zero = jnp.zeros(pack_shape, F32)
    sweep(slices, weigh, 0)
    edges = sweep(slices, update, (zero, zero))
    out_ref[0] = sweep(slices, project, zero)
    out_ref[1], out_ref[2] = packed_edges(edges, lane)


def face_kernel(ext_ref, zone_ref, ztwo_ref, *face_refs):
    elems, slices, cells, width = ext_ref.shape
    for e in range(elems):
        for z in range(slices):
            rows = beam_rows(ext_ref[e, z, 0:1], ext_ref[e, z, cells - 1 : cells])
            for ref, row in zip(face_refs, rows):
                ref[e * slices + z : e * slices + z + 1] = row
    for e in range(elems):
        zone_ref[e], ztwo_ref[e] = pair_order(ext_ref[e, slices - 1], ext_ref[e, 0])


def second_dual_kernel(ext_ref, dual_z_ref, dual_x_ref, dual_y_ref, adj_ref):
    elems, slices, cells, width = ext_ref.shape
    sub = lax.broadcasted_iota(jnp.int32, (cells, width), 0)
    lane = lax.broadcasted_iota(jnp.int32, (cells, width), 1)

    def step(z, behind):
        at_end = z == slices - 1
        duals = []
        for e in range(elems):
            tile = ext_ref[e, z]
            ahead = ext_ref[e, jnp.minimum(z + 1, slices - 1)]
            dual_z = jnp.where(at_end, 0.0, clip(dual_z_ref[e, z] + 0.5 * (ahead - tile)))
            _, _, spread = tile_duals(tile, dual_x_ref[e, z], dual_y_ref[e, z], sub, lane, (cells, width))
            adj_ref[e, z] = spread + (behind[e] - dual_z)
            duals.append(dual_z)
        return tuple(duals)

    zero = jnp.zeros((cells, width), F32)
    lax.fori_loop(0, slices, step, (zero,) * elems, unroll=UNROLL)


def last_update_kernel(size, cur_ref, ext_ref, weight_ref, adj_ref, still_ref, dd_ref, yedge_ref, zedge_ref,
                       zbehind_ref, zone_ref, ztwo_ref, *refs):
    elems, slices, cells, width = cur_ref.shape
    sides = beam_sides(cells)
    pack_refs, refs = refs[: halves(size)], refs[halves(size) :]
    own_pack_ref, *refs = refs
    edge_refs, refs = refs[: len(sides)], refs[len(sides) :]
    own_refs, refs = refs[: len(sides)], refs[len(sides) :]
    other_refs, refs = refs[: len(sides)], refs[len(sides) :]
    result_ref, dual_ref, new_ref, zface_ref, *face_refs, sems = refs
    mine = lax.axis_index("path")
    count, rank = lax.axis_size("gz"), lax.axis_index("gz")
    pick = by_rank(pack_refs, size, 3)
    image = pick(0, 0)
    for r in range(1, size):
        image = image + pick(r, 0)
    sig = dd_ref[1]
    data_dual = (dd_ref[0] + sig * (image - still_ref[0])) / (1.0 + sig)
    part(dual_ref, data_dual)
    ahead, behind = neighbours(pick, size, 1, 2)
    y_ahead = jnp.where(mine < size - 1, clip(yedge_ref[0] + 0.5 * (ahead - own_pack_ref[2])), 0.0)
    y_behind = jnp.where(mine > 0, clip(yedge_ref[1] + 0.5 * (own_pack_ref[1] - behind)), 0.0)
    for (row, sign, there), edge, own, other, out in zip(sides, edge_refs, own_refs, other_refs, face_refs):
        out[...] = clip(edge[...] + 0.5 * face(own[...], other[...], sign, there)) * sign
    sub = lax.broadcasted_iota(jnp.int32, (cells, width), 0)
    lane = lax.broadcasted_iota(jnp.int32, (cells, width), 1)
    rim = (lane == 0) | (lane == width - 1)
    joined = join_edges(y_behind, -y_ahead, lane)
    for e in range(elems):
        other_ahead, other_behind = pair_order(zone_ref[e], ztwo_ref[e])
        z_behind = clip(zbehind_ref[e] + 0.5 * (ext_ref[e, 0] - other_behind))
        z_ahead = clip(zedge_ref[e, slices - 1] + 0.5 * (other_ahead - ext_ref[e, slices - 1]))
        zface_ref[0, e] = jnp.where(rank > 0, z_behind, 0.0)
        zface_ref[1, e] = jnp.where(rank < count - 1, z_ahead, 0.0)

    def weigh(z, offset, none):
        for e in range(elems):
            new_ref[e, z] = weight_ref[e, z] * spread(data_dual, lane, e * slices + z) + adj_ref[e, z]
        return none

    group = slice_group(slices)

    def written(i):
        at = pl.ds(group * i, group)
        return pltpu.make_async_copy(new_ref.at[:, at], result_ref.at[:, at], sems.at[i])

    def update(z, offset, none):
        for e in range(elems):
            k, odd = e * slices + z, (e * slices + offset) % 2
            step = new_ref[e, z] + edge_columns(joined[odd], rim, k)
            for (row, sign, there), out in zip(sides, face_refs):
                step = step + jnp.where(sub == row, out[pl.ds(k, 1)], 0.0)
            new_ref[e, z] = jnp.maximum(cur_ref[e, z] - step / (weight_ref[e, z] + 6.0), 0.0)
        if offset == group - 1:
            written(z // group).start()
        return none

    sweep(slices, weigh, 0)
    for e in range(elems):
        new_ref[e, 0] = new_ref[e, 0] + zface_ref[0, e]
        new_ref[e, slices - 1] = new_ref[e, slices - 1] - zface_ref[1, e]
    sweep(slices, update, 0)
    for i in range(slices // group):
        written(i).wait()


def shards(maps, measured, beta_table, view, kappa, line_of, side):
    elems, slices, cells, width = maps.shape
    total_x = cells * lax.axis_size("beam")
    total_y = width * lax.axis_size("path")
    size = lax.axis_size("path")
    block = f32(elems, slices, cells, width)
    plane = f32(elems, cells, width)
    rows = f32(elems * slices, width)
    faces = len(beam_sides(cells))
    measured = measured.transpose(0, 2, 1)
    kappa = kappa.T

    tall = f32((elems + 1) * slices, width)
    maps, inside, coef, zone, ztwo, *own = call(
        functools.partial(open_kernel, total_x),
        [view] + [pltpu.with_memory_space_constraint(a, pltpu.HBM) for a in (maps, beta_table, kappa, line_of, side)],
        [block, f32(slices, cells, width), f32(elems * elems + elems, width), plane, plane, tall] + [rows] * (faces - 1),
        [SMEM] + [pltpu.HBM] * 5,
        [
            pltpu.SMEM(beta_table.shape, F32),
            pltpu.SMEM(kappa.shape, F32),
            pltpu.SMEM(line_of.shape, jnp.int32),
            pltpu.SMEM(side.shape, jnp.int32),
            pltpu.SemaphoreType.DMA((6,)),
        ],
    )
    other = exchange_beam(own)
    carry, skip = other[-1], elems * slices
    beams = lax.axis_size("beam")
    if beams > 2:
        carry, skip = carry[skip:], 0
        reach = 1
        while reach < beams - 1:
            far = lax.axis_index("beam") > reach
            carry = carry + jnp.where(far, shifted(carry, "beam", reach), 0.0)
            reach *= 2
    local, pack = call(
        functools.partial(depth_kernel, total_y),
        [maps, coef],
        [block, f32(3, cells, width)],
        [VMEM] * 2,
        [
            pltpu.VMEM(maps.shape, F32),
            pltpu.VMEM((elems * slices * cells, 2 * width), jnp.bfloat16),
            pltpu.VMEM((elems * slices * cells, 2 * width), F32),
        ],
    )
    weight, pack = call(
        functools.partial(weight_kernel, total_x, skip),
        [maps, inside, carry, local, pack],
        [block, f32(5, cells, width)],
        [VMEM] * 5,
    )
    packs = around_direct(pack, "path")
    zone, ztwo = swapped(zone, "gz", 0), swapped(ztwo, "gz", 1)
    dual_z, dual_x, dual_y, zdual, adj, still, *edge = call(
        first_dual_kernel,
        [maps, zone, ztwo, measured, coef, *own, *other],
        [block, block, block, plane, block, f32(2, cells, width)] + [rows] * faces,
        [VMEM] * (5 + 2 * faces),
        [pltpu.VMEM(plane.shape, F32)],
    )
    weight, current, extrap, dd, yedge, pack, emission = call(
        functools.partial(first_update_kernel, total_y, size),
        [maps, weight, adj, still, *packs],
        [block, block, block, f32(2, cells, width), f32(2, cells, width),
         f32(3, cells, width), f32(elems, cells, slices)],
        [VMEM] * (4 + size),
    )
    packs, joined = around(pack, "path")
    zone, ztwo, *own = call(face_kernel, [extrap], [plane, plane] + [rows] * faces, [VMEM])
    zone, ztwo = swapped(zone, "gz", 0), swapped(after(ztwo, joined), "gz", 1)
    other = exchange_beam(own)
    (adj,) = call(second_dual_kernel, [extrap, dual_z, dual_x, dual_y], [block], [VMEM] * 4)
    groups = slices // slice_group(slices)
    current, data_dual = call(
        functools.partial(last_update_kernel, size),
        [current, extrap, weight, adj, still, dd, yedge, dual_z, zdual, zone, ztwo, *packs, pack, *edge, *own, *other],
        [block, f32(elems, cells, slices)],
        [VMEM] * (12 + len(packs) + 3 * faces),
        [pltpu.VMEM(maps.shape, F32), pltpu.VMEM((2, elems, cells, width), F32)]
        + [pltpu.VMEM((elems * slices, width), F32)] * faces
        + [pltpu.SemaphoreType.DMA((groups,))],
        [pl.ANY, VMEM],
    )
    return emission.transpose(0, 2, 1), current, data_dual.transpose(0, 2, 1)


def solution(mesh):
    return jax.shard_map(
        shards,
        mesh=mesh,
        in_specs=(P(None, "gz", "beam", "path"), P(None, "gz", "beam"), P(), P(), P(), P(), P()),
        out_specs=(P(None, "gz", "beam"), P(None, "gz", "beam", "path"), P(None, "gz", "beam")),
        check_vma=False,
    )
```

```python
import functools

import jax
import jax.numpy as jnp
from jax import lax
from jax.experimental import pallas as pl
from jax.experimental.pallas import tpu as pltpu
from jax.sharding import PartitionSpec as P

ITERS = 2
LAM = 0.1
F32 = jnp.float32
VMEM = pltpu.VMEM
SMEM = pltpu.SMEM
UNROLL = 4
VMEM_LIMIT = 32 * 1024 * 1024


def clip(value):
    return jnp.clip(value, -LAM, LAM)


def call(body, ins, outs, spaces, scratch=(), flops=1_000_000):
    specs = [pl.BlockSpec(memory_space=space) for space in spaces]
    moved = sum(a.size * 4 for a in ins) + sum(o.size * 4 for o in outs)
    return pl.pallas_call(
        body,
        out_shape=outs,
        in_specs=specs,
        out_specs=[pl.BlockSpec(memory_space=VMEM)] * len(outs),
        scratch_shapes=list(scratch),
        compiler_params=pltpu.CompilerParams(vmem_limit_bytes=VMEM_LIMIT),
        cost_estimate=pl.CostEstimate(flops=flops, bytes_accessed=moved, transcendentals=0),
    )(*ins)


def f32(*shape):
    return jax.ShapeDtypeStruct(shape, F32)


def shifted(block, axis, distance):
    n = lax.axis_size(axis)
    return lax.ppermute(block, axis, [((i - distance) % n, i) for i in range(n)])


def swapped(block, axis, start):
    n = lax.axis_size(axis)
    route = {i: i for i in range(n)}
    for i in range(start, n - 1, 2):
        route[i], route[i + 1] = i + 1, i
    if start and n % 2 == 0:
        route[0], route[n - 1] = n - 1, 0
    return lax.ppermute(block, axis, sorted(route.items()))


def pair_order(ahead, behind):
    even = lax.rem(lax.axis_index("gz"), 2) == 0
    return jnp.where(even, ahead, behind), jnp.where(even, behind, ahead)


def merged(mine, other, far, scale, bit):
    upper = (lax.axis_index("path") & bit) != 0
    low = [jnp.where(upper, o, m) for m, o in zip(mine, other)]
    high = [jnp.where(upper, m, o) for m, o in zip(mine, other)]
    if far is None:
        return [low[0], high[1]] + [a + b for a, b in zip(low[2:], high[2:])]
    low_factor = jnp.where(far, jnp.exp(high[2] * scale), 1.0)
    high_factor = jnp.where(far, 1.0, jnp.exp(low[2] * scale))
    sums = [low_factor * a + high_factor * b for a, b in zip(low[3:], high[3:])]
    return [low[0], high[1], low[2] + high[2]] + sums


def passed(state, other, far, bit):
    mine = lax.axis_index("path")
    ahead = jnp.where(mine & (2 * bit - 1) == bit - 1, other[0], state[0])
    behind = jnp.where(mine & (2 * bit - 1) == bit, other[1], state[1])
    if far is None:
        return [ahead, behind]
    upper = (mine & bit) != 0
    in_way = jnp.where(upper, jnp.where(far, 0.0, other[2]), jnp.where(far, other[2], 0.0))
    return [ahead, behind, state[2] + in_way]


def rows_of(ref):
    return [ref[i] for i in range(ref.shape[0])]


def merge_all(bit, scale, refs, far, kept):
    mine_ref, other_ref, *state_refs = refs
    state = rows_of(state_refs[0]) if state_refs else [jnp.zeros(mine_ref.shape[1:], F32)] * kept
    mine, other = rows_of(mine_ref), rows_of(other_ref)
    return merged(mine, other, far, scale, bit), passed(state, other, far, bit)


def merge_kernel(bit, scale, kept, *refs):
    *refs, out_ref, state_ref = refs
    far = None
    if kept == 3:
        far_ref, *refs = refs
        far = far_ref[3] != 0.0
    packs, state = merge_all(bit, scale, refs, far, kept)
    for ref, values in ((out_ref, packs), (state_ref, state)):
        for i, value in enumerate(values):
            ref[i] = value


def around(block, axis, scale, far=None):
    n = lax.axis_size(axis)
    if n < 2 or n & (n - 1):
        raise ValueError("path size")
    kept = 2 if far is None else 3
    state = []
    bit = 1
    while True:
        other = lax.ppermute(block, axis, [(i, i ^ bit) for i in range(n)])
        if 2 * bit == n:
            return [block, other] + state
        ins = ([] if far is None else [far]) + [block, other] + state
        block, *state = call(
            functools.partial(merge_kernel, bit, scale, kept),
            ins,
            [f32(*block.shape), f32(kept, *block.shape[1:])],
            [VMEM] * len(ins),
        )
        bit *= 2


def spread(pack, lane, k):
    return jnp.sum(jnp.where(lane == k, pack, 0.0), axis=1, keepdims=True)


def gather_edges(pack, tile, lane, k):
    width = tile.shape[1]
    here = (lane == k) | (lane == (k - 1) % width)
    return jnp.where(here, pltpu.roll(tile, k, axis=1) if k else tile, pack)


def packed_edges(edges, lane):
    even = lane % 2 == 0
    first = jnp.where(even, edges[0], edges[1])
    return first, pltpu.roll(jnp.where(even, edges[1], edges[0]), 1, axis=1)


def join_edges(first, last, lane):
    width = first.shape[1]
    last = pltpu.roll(last, width - 1, axis=1)
    even = lane % 2 == 0
    return jnp.where(even, first, last), jnp.where(even, last, first)


def edge_columns(pack, rim, k):
    return jnp.where(rim, pltpu.roll(pack, pack.shape[1] - k, axis=1) if k else pack, 0.0)


def reciprocal(value):
    guess = pl.reciprocal(value, approx=True)
    return guess * (2.0 - value * guess)


def sweep(slices, body, carry):
    group = UNROLL if slices % UNROLL == 0 else slices

    def step(i, carry):
        for offset in range(group):
            carry = body(group * i + offset, offset, carry)
        return carry

    return lax.fori_loop(0, slices // group, step, carry)


def beam_sides(cells):
    count, rank = lax.axis_size("beam"), lax.axis_index("beam")
    if count == 2:
        return [
            (
                jnp.where(rank == 0, cells - 1, 0),
                jnp.where(rank == 0, F32(-1.0), F32(1.0)),
                None,
            )
        ]
    return [(cells - 1, F32(-1.0), rank < count - 1), (0, F32(1.0), rank > 0)]


def beam_rows(first, last):
    count, rank = lax.axis_size("beam"), lax.axis_index("beam")
    if count == 2:
        return [jnp.where(rank == 0, last, first)]
    return [last, first]


def face(own, other, sign, there):
    step = (own - other) * sign
    return step if there is None else jnp.where(there, step, 0.0)


def exchange_beam(rows):
    if lax.axis_size("beam") == 2:
        return [lax.ppermute(rows[0], "beam", [(0, 1), (1, 0)])]
    return [shifted(rows[1], "beam", -1), shifted(rows[0], "beam", 1)]


def open_kernel(total, view_ref, source_ref, *refs):
    small, refs = refs[:4], refs[4:]
    maps_ref, inside_ref, coef_ref, *refs = refs
    elems, slices, cells, width = maps_ref.shape
    faces = len(beam_sides(cells))
    face_refs, refs = refs[:faces], refs[faces:]
    beta_ref, kappa_ref, line_ref, side_ref, sems = refs
    half = slices // 2
    parts = [pl.ds(0, half), pl.ds(half, slices - half)] if half else [pl.ds(0, slices)]
    fetch = []
    for i, (ref, kept) in enumerate(zip(small, (beta_ref, kappa_ref, line_ref, side_ref))):
        fetch.append(pltpu.make_async_copy(ref, kept, sems.at[i]))
    large = []
    for i, at in enumerate(parts):
        large.append(pltpu.make_async_copy(source_ref.at[:, at], maps_ref.at[:, at], sems.at[len(small) + i]))
    for copy in large[:1] + fetch + large[1:]:
        copy.start()
    for copy in fetch:
        copy.wait()
    for e in range(elems):
        line = line_ref[e]
        for f in range(elems):
            coef_ref[e * elems + f : e * elems + f + 1] = jnp.full((1, width), kappa_ref[f, line])
        coef_ref[elems * elems + e : elems * elems + e + 1] = jnp.full((1, width), side_ref[e].astype(F32))
    view = view_ref[0]
    beta = [beta_ref[view, e] for e in range(elems)]
    sub = lax.broadcasted_iota(jnp.int32, maps_ref.shape[2:], 0)
    for z in range(slices):
        if z == 0 or z == half:
            large[1 if z else 0].wait()
        tiles = [maps_ref[e, z] for e in range(elems)]
        mu = beta[0] * tiles[0]
        for e in range(1, elems):
            mu = mu + beta[e] * tiles[e]
        run = mu
        reach = 1
        while reach < cells:
            run = run + jnp.where(sub >= reach, pltpu.roll(run, reach, axis=0), 0.0)
            reach *= 2
        inside_ref[z] = jnp.where(sub >= 1, pltpu.roll(run, 1, axis=0), 0.0)
        face_refs[0][elems * slices + z : elems * slices + z + 1] = run[cells - 1 : cells]
        for e in range(elems):
            rows = beam_rows(tiles[e][0:1], tiles[e][cells - 1 : cells])
            for ref, row in zip(face_refs, rows):
                ref[e * slices + z : e * slices + z + 1] = row


def depth_kernel(total, maps_ref, coef_ref, local_ref, pack_ref, mu_ref, parts_ref, sums_ref):
    elems, slices, cells, width = maps_ref.shape
    rows = slices * cells
    row = lax.broadcasted_iota(jnp.int32, (2 * width, 2 * width), 0)
    col = lax.broadcasted_iota(jnp.int32, (2 * width, 2 * width), 1)
    row = jnp.where(row >= width, row - width, row)
    table = jnp.where((row < col) | (col >= width), 1.0, 0.0).astype(jnp.bfloat16)
    for e in range(elems):
        mu = coef_ref[e * elems : e * elems + 1][None] * maps_ref[0]
        for f in range(1, elems):
            mu = mu + coef_ref[e * elems + f : e * elems + f + 1][None] * maps_ref[f]
        mu_ref[e] = mu
        flat = mu.reshape(rows, width)
        high = flat.astype(jnp.bfloat16)
        low = (flat - high.astype(F32)).astype(jnp.bfloat16)
        parts_ref[e * rows : (e + 1) * rows, 0:width] = high
        parts_ref[e * rows : (e + 1) * rows, width:] = low
    sums_ref[...] = jnp.dot(parts_ref[...], table, preferred_element_type=F32)
    lane = lax.broadcasted_iota(jnp.int32, (cells, width), 1)
    scale = -1.0 / total
    strip = jnp.zeros((cells, width), F32)
    edges = [strip, strip]
    for e in range(elems):
        forward = coef_ref[elems * elems + e : elems * elems + e + 1] == 0.0
        for z in range(slices):
            k = e * slices + z
            before = sums_ref[k * cells : (k + 1) * cells, 0:width]
            whole = sums_ref[k * cells : (k + 1) * cells, width:]
            after = whole - before - mu_ref[e, z]
            local_ref[e, z] = jnp.exp(jnp.where(forward, before, after) * scale)
            strip = jnp.where(lane == k, whole, strip)
            edges[k % 2] = gather_edges(edges[k % 2], maps_ref[e, z], lane, k)
    pack_ref[0], pack_ref[1] = packed_edges(edges, lane)
    pack_ref[2] = strip
    far = jnp.zeros((cells, width), F32)
    for e in range(elems):
        inside = (lane >= e * slices) & (lane < (e + 1) * slices)
        far = jnp.where(inside, coef_ref[elems * elems + e : elems * elems + e + 1][:, 0:1], far)
    pack_ref[3] = far


def weight_kernel(total, skip, maps_ref, inside_ref, carry_ref, local_ref, pack_ref, weight_ref, out_ref, zone_ref, ztwo_ref):
    elems, slices, cells, width = maps_ref.shape
    lane = lax.broadcasted_iota(jnp.int32, (cells, width), 1)
    there = lax.axis_index("beam") > 0
    scale = -1.0 / total

    def step(z, packs):
        proj, whole = packs
        place = lane - z
        carry = jnp.where(there, carry_ref[pl.ds(skip + z, 1)], 0.0)
        att = jnp.exp((inside_ref[z] + carry) * scale)
        for e in range(elems):
            weight = att * local_ref[e, z]
            weight_ref[e, z] = weight
            here = place == e * slices
            proj = jnp.where(here, jnp.sum(weight * maps_ref[e, z], axis=1, keepdims=True), proj)
            whole = jnp.where(here, jnp.sum(weight, axis=1, keepdims=True), whole)
        return proj, whole

    zero = jnp.zeros((cells, width), F32)
    proj, whole = lax.fori_loop(0, slices, step, (zero, zero), unroll=UNROLL)
    out_ref[0] = pack_ref[0]
    out_ref[1] = pack_ref[1]
    out_ref[2] = pack_ref[2]
    out_ref[3] = proj
    out_ref[4] = whole
    for e in range(elems):
        zone_ref[e], ztwo_ref[e] = pair_order(maps_ref[e, slices - 1], maps_ref[e, 0])


def dual_step(field, ahead, dual, last):
    step = 0.5 * (ahead - field)
    return jnp.where(last, 0.0, clip(step if dual is None else dual + step))


def tile_duals(tile, dual_x, dual_y, sub, lane, shape):
    cells, width = shape
    new_x = dual_step(tile, pltpu.roll(tile, cells - 1, axis=0), dual_x, sub == cells - 1)
    new_y = dual_step(tile, pltpu.roll(tile, width - 1, axis=1), dual_y, lane == width - 1)
    spread = pltpu.roll(new_x, 1, axis=0) - new_x + (pltpu.roll(new_y, 1, axis=1) - new_y)
    return new_x, new_y, spread


def join(ref, width):
    elems, cells, slices = ref.shape
    parts = [ref[e] for e in range(elems)]
    if elems * slices < width:
        parts.append(jnp.zeros((cells, width - elems * slices), F32))
    return jnp.concatenate(parts, axis=1)


def first_dual_kernel(maps_ref, measured_ref, *refs):
    elems, slices, cells, width = maps_ref.shape
    sides = beam_sides(cells)
    own_refs, refs = refs[: len(sides)], refs[len(sides) :]
    other_refs, refs = refs[: len(sides)], refs[len(sides) :]
    dual_z_ref, dual_x_ref, dual_y_ref, adj_ref, still_ref, *edge_refs = refs
    sub = lax.broadcasted_iota(jnp.int32, (cells, width), 0)
    lane = lax.broadcasted_iota(jnp.int32, (cells, width), 1)
    still_ref[...] = join(measured_ref, width)
    for (row, sign, there), own, other, edge in zip(sides, own_refs, other_refs, edge_refs):
        rows = pl.ds(0, elems * slices)
        edge[...] = clip(0.5 * face(own[rows], other[rows], sign, there))
    def step(z, behind):
        at_end = z == slices - 1
        duals = []
        for e in range(elems):
            tile = maps_ref[e, z]
            ahead = maps_ref[e, jnp.minimum(z + 1, slices - 1)]
            dual_z = jnp.where(at_end, 0.0, clip(0.5 * (ahead - tile)))
            dual_x, dual_y, spread = tile_duals(tile, None, None, sub, lane, (cells, width))
            dual_z_ref[e, z] = dual_z
            dual_x_ref[e, z] = dual_x
            dual_y_ref[e, z] = dual_y
            spread = spread + (behind[e] - dual_z)
            for (row, sign, there), edge in zip(sides, edge_refs):
                spread = spread + jnp.where(sub == row, sign * edge[pl.ds(e * slices + z, 1)], 0.0)
            adj_ref[e, z] = spread
            duals.append(dual_z)
        return tuple(duals)

    zero = jnp.zeros((cells, width), F32)
    lax.fori_loop(0, slices, step, (zero,) * elems, unroll=UNROLL)


def part(ref, pack):
    slices = ref.shape[2]
    for e in range(ref.shape[0]):
        ref[e] = pack[:, e * slices : (e + 1) * slices]


def first_update_kernel(total, size, maps_ref, weight_ref, adj_ref, still_ref, far_ref, own_ref, zone_ref, ztwo_ref,
                        *refs):
    elems, slices, cells, width = maps_ref.shape
    pack_refs, refs = refs[:-9], refs[-9:]
    full_ref, tau_ref, cur_ref, ext_ref, dd_ref, yedge_ref, zdual_ref, out_ref, emission_ref = refs
    count, rank = lax.axis_size("gz"), lax.axis_index("gz")
    mine = lax.axis_index("path")
    pack_shape = (cells, width)
    lane = lax.broadcasted_iota(jnp.int32, pack_shape, 1)
    rim = (lane == 0) | (lane == width - 1)
    packs, state = merge_all(size // 2, -1.0 / total, pack_refs, far_ref[3] != 0.0, 3)
    image, weights = packs[3], packs[4]
    ahead, behind, base = state
    own = jnp.exp(base * (-1.0 / total))
    sig = 1.0 / weights
    data_dual = sig * (image - still_ref[...]) / (1.0 + sig)
    dd_ref[0] = data_dual
    dd_ref[1] = sig
    part(emission_ref, image * (1.0 / total))
    y_ahead = jnp.where(mine < size - 1, clip(0.5 * (ahead - own_ref[1])), 0.0)
    y_behind = jnp.where(mine > 0, clip(0.5 * (own_ref[0] - behind)), 0.0)
    joined = join_edges(y_behind, -y_ahead, lane)
    yedge_ref[0] = y_ahead
    yedge_ref[1] = y_behind

    def weigh(z, offset, none):
        for e in range(elems):
            weight = weight_ref[e, z] * spread(own, lane, e * slices + z)
            full_ref[e, z] = weight
            tau_ref[e, z] = reciprocal(weight + 6.0)
            ext_ref[e, z] = weight * spread(data_dual, lane, e * slices + z) + adj_ref[e, z]
        return none

    def project(z, offset, image):
        for e in range(elems):
            row = jnp.sum(full_ref[e, z] * ext_ref[e, z], axis=1, keepdims=True)
            image = jnp.where(lane == e * slices + z, row, image)
        return image

    zero = jnp.zeros(pack_shape, F32)
    sweep(slices, weigh, 0)
    for e in range(elems):
        ahead, behind = pair_order(zone_ref[e], ztwo_ref[e])
        behind = jnp.where(rank > 0, clip(0.5 * (maps_ref[e, 0] - behind)), 0.0)
        ahead = jnp.where(rank < count - 1, clip(0.5 * (ahead - maps_ref[e, slices - 1])), 0.0)
        zdual_ref[0, e] = behind
        zdual_ref[1, e] = ahead
        ext_ref[e, 0] = ext_ref[e, 0] + behind
        ext_ref[e, slices - 1] = ext_ref[e, slices - 1] - ahead
    edges = [zero, zero]
    for z in range(slices):
        for e in range(elems):
            k = e * slices + z
            tile = maps_ref[e, z]
            step = (ext_ref[e, z] + edge_columns(joined[k % 2], rim, k)) * tau_ref[e, z]
            new = jnp.maximum(tile - step, 0.0)
            ext = 2.0 * new - tile
            cur_ref[e, z] = new
            ext_ref[e, z] = ext
            edges[k % 2] = gather_edges(edges[k % 2], ext, lane, k)
    out_ref[0], out_ref[1] = packed_edges(edges, lane)
    out_ref[2] = sweep(slices, project, zero)
    for i in range(3, out_ref.shape[0]):
        out_ref[i] = zero


def face_kernel(ext_ref, zone_ref, ztwo_ref, *face_refs):
    elems, slices, cells, width = ext_ref.shape
    for e in range(elems):
        for z in range(slices):
            rows = beam_rows(ext_ref[e, z, 0:1], ext_ref[e, z, cells - 1 : cells])
            for ref, row in zip(face_refs, rows):
                ref[e * slices + z : e * slices + z + 1] = row
    for e in range(elems):
        zone_ref[e], ztwo_ref[e] = pair_order(ext_ref[e, slices - 1], ext_ref[e, 0])


def second_dual_kernel(ext_ref, dual_z_ref, dual_x_ref, dual_y_ref, adj_ref):
    elems, slices, cells, width = ext_ref.shape
    sub = lax.broadcasted_iota(jnp.int32, (cells, width), 0)
    lane = lax.broadcasted_iota(jnp.int32, (cells, width), 1)

    def step(z, behind):
        at_end = z == slices - 1
        duals = []
        for e in range(elems):
            tile = ext_ref[e, z]
            ahead = ext_ref[e, jnp.minimum(z + 1, slices - 1)]
            dual_z = jnp.where(at_end, 0.0, clip(dual_z_ref[e, z] + 0.5 * (ahead - tile)))
            _, _, spread = tile_duals(tile, dual_x_ref[e, z], dual_y_ref[e, z], sub, lane, (cells, width))
            adj_ref[e, z] = spread + (behind[e] - dual_z)
            duals.append(dual_z)
        return tuple(duals)

    zero = jnp.zeros((cells, width), F32)
    lax.fori_loop(0, slices, step, (zero,) * elems, unroll=UNROLL)


def last_update_kernel(size, cur_ref, ext_ref, weight_ref, tau_ref, adj_ref, still_ref, dd_ref, yedge_ref, zdual_ref,
                       own_pack_ref, zone_ref, ztwo_ref, *refs):
    elems, slices, cells, width = cur_ref.shape
    sides = beam_sides(cells)
    kept = 2 if size == 2 else 3
    pack_refs, refs = refs[:kept], refs[kept:]
    edge_refs, refs = refs[: len(sides)], refs[len(sides) :]
    own_refs, refs = refs[: len(sides)], refs[len(sides) :]
    other_refs, refs = refs[: len(sides)], refs[len(sides) :]
    new_ref, dual_ref, zface_ref, *face_refs = refs
    mine = lax.axis_index("path")
    count, rank = lax.axis_size("gz"), lax.axis_index("gz")
    packs, (ahead, behind) = merge_all(size // 2, None, pack_refs, None, 2)
    image = packs[2]
    sig = dd_ref[1]
    data_dual = (dd_ref[0] + sig * (image - still_ref[...])) / (1.0 + sig)
    part(dual_ref, data_dual)
    y_ahead = jnp.where(mine < size - 1, clip(yedge_ref[0] + 0.5 * (ahead - own_pack_ref[1])), 0.0)
    y_behind = jnp.where(mine > 0, clip(yedge_ref[1] + 0.5 * (own_pack_ref[0] - behind)), 0.0)
    for (row, sign, there), edge, own, other, out in zip(sides, edge_refs, own_refs, other_refs, face_refs):
        out[...] = clip(edge[...] + 0.5 * face(own[...], other[...], sign, there)) * sign
    sub = lax.broadcasted_iota(jnp.int32, (cells, width), 0)
    lane = lax.broadcasted_iota(jnp.int32, (cells, width), 1)
    rim = (lane == 0) | (lane == width - 1)
    joined = join_edges(y_behind, -y_ahead, lane)
    for e in range(elems):
        other_ahead, other_behind = pair_order(zone_ref[e], ztwo_ref[e])
        z_behind = clip(zdual_ref[0, e] + 0.5 * (ext_ref[e, 0] - other_behind))
        z_ahead = clip(zdual_ref[1, e] + 0.5 * (other_ahead - ext_ref[e, slices - 1]))
        zface_ref[0, e] = jnp.where(rank > 0, z_behind, 0.0)
        zface_ref[1, e] = jnp.where(rank < count - 1, z_ahead, 0.0)

    def weigh(z, offset, none):
        for e in range(elems):
            new_ref[e, z] = weight_ref[e, z] * spread(data_dual, lane, e * slices + z) + adj_ref[e, z]
        return none

    sweep(slices, weigh, 0)
    for e in range(elems):
        new_ref[e, 0] = new_ref[e, 0] + zface_ref[0, e]
        new_ref[e, slices - 1] = new_ref[e, slices - 1] - zface_ref[1, e]
    for z in range(slices):
        for e in range(elems):
            k = e * slices + z
            step = new_ref[e, z] + edge_columns(joined[k % 2], rim, k)
            for (row, sign, there), out in zip(sides, face_refs):
                step = step + jnp.where(sub == row, out[k : k + 1], 0.0)
            new_ref[e, z] = jnp.maximum(cur_ref[e, z] - step * tau_ref[e, z], 0.0)


def shards(maps, measured, beta_table, view, kappa, line_of, side):
    elems, slices, cells, width = maps.shape
    total_x = cells * lax.axis_size("beam")
    total_y = width * lax.axis_size("path")
    size = lax.axis_size("path")
    block = f32(elems, slices, cells, width)
    plane = f32(elems, cells, width)
    rows = f32(elems * slices, width)
    faces = len(beam_sides(cells))
    measured = measured.transpose(0, 2, 1)
    kappa = kappa.T

    tall = f32((elems + 1) * slices, width)
    maps, inside, coef, *own = call(
        functools.partial(open_kernel, total_x),
        [view] + [pltpu.with_memory_space_constraint(a, pltpu.HBM) for a in (maps, beta_table, kappa, line_of, side)],
        [block, f32(slices, cells, width), f32(elems * elems + elems, width), tall] + [rows] * (faces - 1),
        [SMEM] + [pltpu.HBM] * 5,
        [
            pltpu.SMEM(beta_table.shape, F32),
            pltpu.SMEM(kappa.shape, F32),
            pltpu.SMEM(line_of.shape, jnp.int32),
            pltpu.SMEM(side.shape, jnp.int32),
            pltpu.SemaphoreType.DMA((6,)),
        ],
    )
    other = exchange_beam(own)
    carry, skip = other[-1], elems * slices
    beams = lax.axis_size("beam")
    if beams > 2:
        carry, skip = carry[skip:], 0
        reach = 1
        while reach < beams - 1:
            far = lax.axis_index("beam") > reach
            carry = carry + jnp.where(far, shifted(carry, "beam", reach), 0.0)
            reach *= 2
    local, still = call(
        functools.partial(depth_kernel, total_y),
        [maps, coef],
        [block, f32(4, cells, width)],
        [VMEM] * 2,
        [
            pltpu.VMEM(maps.shape, F32),
            pltpu.VMEM((elems * slices * cells, 2 * width), jnp.bfloat16),
            pltpu.VMEM((elems * slices * cells, 2 * width), F32),
        ],
    )
    weight, pack, zone, ztwo = call(
        functools.partial(weight_kernel, total_x, skip),
        [maps, inside, carry, local, still],
        [block, f32(5, cells, width), plane, plane],
        [VMEM] * 5,
    )
    packs = around(pack, "path", -1.0 / total_y, still)
    zone, ztwo = swapped(zone, "gz", 0), swapped(ztwo, "gz", 1)
    dual_z, dual_x, dual_y, adj, counts, *edge = call(
        first_dual_kernel,
        [maps, measured, *own, *other],
        [block, block, block, block, f32(cells, width)] + [rows] * faces,
        [VMEM] * (2 + 2 * faces),
    )
    weight, tau, current, extrap, dd, yedge, zdual, pack, emission = call(
        functools.partial(first_update_kernel, total_y, size),
        [maps, weight, adj, counts, still, pack, zone, ztwo, *packs],
        [block, block, block, block, f32(2, cells, width), f32(2, cells, width), f32(2, elems, cells, width),
         f32(4, cells, width), f32(elems, cells, slices)],
        [VMEM] * (8 + len(packs)),
    )
    packs = around(pack, "path", None)
    zone, ztwo, *own = call(face_kernel, [extrap], [plane, plane] + [rows] * faces, [VMEM])
    zone, ztwo = swapped(zone, "gz", 0), swapped(ztwo, "gz", 1)
    other = exchange_beam(own)
    (adj,) = call(second_dual_kernel, [extrap, dual_z, dual_x, dual_y], [block], [VMEM] * 4)
    current, data_dual = call(
        functools.partial(last_update_kernel, size),
        [current, extrap, weight, tau, adj, counts, dd, yedge, zdual, pack, zone, ztwo, *packs, *edge, *own, *other],
        [block, f32(elems, cells, slices)],
        [VMEM] * (12 + len(packs) + 3 * faces),
        [pltpu.VMEM((2, elems, cells, width), F32)] + [pltpu.VMEM((elems * slices, width), F32)] * faces,
    )
    return emission.transpose(0, 2, 1), current, data_dual.transpose(0, 2, 1)


def solution(mesh):
    return jax.shard_map(
        shards,
        mesh=mesh,
        in_specs=(P(None, "gz", "beam", "path"), P(None, "gz", "beam"), P(), P(), P(), P(), P()),
        out_specs=(P(None, "gz", "beam"), P(None, "gz", "beam", "path"), P(None, "gz", "beam")),
        check_vma=False,
    )
```

```python
import functools

import jax
import jax.numpy as jnp
from jax import lax
from jax.experimental import pallas as pl
from jax.experimental.pallas import tpu as pltpu
from jax.sharding import PartitionSpec as P

ITERS = 2
LAM = 0.1
F32 = jnp.float32
VMEM = pltpu.VMEM
SMEM = pltpu.SMEM
UNROLL = 4
VMEM_LIMIT = 32 * 1024 * 1024


def clip(value):
    return jnp.clip(value, -LAM, LAM)


def call(body, ins, outs, spaces, scratch=(), flops=1_000_000):
    specs = [pl.BlockSpec(memory_space=space) for space in spaces]
    moved = sum(a.size * 4 for a in ins) + sum(o.size * 4 for o in outs)
    return pl.pallas_call(
        body,
        out_shape=outs,
        in_specs=specs,
        out_specs=[pl.BlockSpec(memory_space=VMEM)] * len(outs),
        scratch_shapes=list(scratch),
        compiler_params=pltpu.CompilerParams(vmem_limit_bytes=VMEM_LIMIT),
        cost_estimate=pl.CostEstimate(flops=flops, bytes_accessed=moved, transcendentals=0),
    )(*ins)


def f32(*shape):
    return jax.ShapeDtypeStruct(shape, F32)


def shifted(block, axis, distance):
    n = lax.axis_size(axis)
    return lax.ppermute(block, axis, [((i - distance) % n, i) for i in range(n)])


def swapped(block, start):
    n, paths = lax.axis_size("gz"), lax.axis_size("path")
    route = []
    for p in range(paths):
        for z in range(n):
            other = z + 1 if (z - start) % 2 == 0 else z - 1
            there = (p, other) if 0 <= other < n else (p ^ 1, z)
            route.append((p * n + z, there[0] * n + there[1]))
    return lax.ppermute(block, ("path", "gz"), route)


def pair_order(ahead, behind):
    even = lax.rem(lax.axis_index("gz"), 2) == 0
    return jnp.where(even, ahead, behind), jnp.where(even, behind, ahead)


def merged(mine, other, far, scale, bit):
    upper = (lax.axis_index("path") & bit) != 0
    low = [jnp.where(upper, o, m) for m, o in zip(mine, other)]
    high = [jnp.where(upper, m, o) for m, o in zip(mine, other)]
    if far is None:
        return [low[0], high[1]] + [a + b for a, b in zip(low[2:], high[2:])]
    low_factor = jnp.where(far, jnp.exp(high[2] * scale), 1.0)
    high_factor = jnp.where(far, 1.0, jnp.exp(low[2] * scale))
    sums = [low_factor * a + high_factor * b for a, b in zip(low[3:], high[3:])]
    return [low[0], high[1], low[2] + high[2]] + sums


def passed(state, other, far, bit):
    mine = lax.axis_index("path")
    ahead = jnp.where(mine & (2 * bit - 1) == bit - 1, other[0], state[0])
    behind = jnp.where(mine & (2 * bit - 1) == bit, other[1], state[1])
    if far is None:
        return [ahead, behind]
    upper = (mine & bit) != 0
    in_way = jnp.where(upper, jnp.where(far, 0.0, other[2]), jnp.where(far, other[2], 0.0))
    return [ahead, behind, state[2] + in_way]


def rows_of(ref):
    return [ref[i] for i in range(ref.shape[0])]


def merge_all(bit, scale, refs, far, kept):
    mine_ref, other_ref, *state_refs = refs
    state = rows_of(state_refs[0]) if state_refs else [jnp.zeros(mine_ref.shape[1:], F32)] * kept
    mine, other = rows_of(mine_ref), rows_of(other_ref)
    return merged(mine, other, far, scale, bit), passed(state, other, far, bit)


def merge_kernel(bit, scale, kept, *refs):
    *refs, out_ref, state_ref = refs
    far = None
    if kept == 3:
        far_ref, *refs = refs
        far = far_ref[3] != 0.0
    packs, state = merge_all(bit, scale, refs, far, kept)
    for ref, values in ((out_ref, packs), (state_ref, state)):
        for i, value in enumerate(values):
            ref[i] = value


def around(block, axis, scale, far=None):
    n = lax.axis_size(axis)
    if n < 2 or n & (n - 1):
        raise ValueError("path size")
    kept = 2 if far is None else 3
    state = []
    bit = 1
    while True:
        other = lax.ppermute(block, axis, [(i, i ^ bit) for i in range(n)])
        if 2 * bit == n:
            return [block, other] + state
        ins = ([] if far is None else [far]) + [block, other] + state
        block, *state = call(
            functools.partial(merge_kernel, bit, scale, kept),
            ins,
            [f32(*block.shape), f32(kept, *block.shape[1:])],
            [VMEM] * len(ins),
        )
        bit *= 2


def spread(pack, lane, k):
    return jnp.sum(jnp.where(lane == k, pack, 0.0), axis=1, keepdims=True)


def gather_edges(pack, tile, lane, k):
    width = tile.shape[1]
    here = (lane == k) | (lane == (k - 1) % width)
    return jnp.where(here, pltpu.roll(tile, k, axis=1) if k else tile, pack)


def packed_edges(edges, lane):
    even = lane % 2 == 0
    first = jnp.where(even, edges[0], edges[1])
    return first, pltpu.roll(jnp.where(even, edges[1], edges[0]), 1, axis=1)


def join_edges(first, last, lane):
    width = first.shape[1]
    last = pltpu.roll(last, width - 1, axis=1)
    even = lane % 2 == 0
    return jnp.where(even, first, last), jnp.where(even, last, first)


def edge_columns(pack, rim, k):
    return jnp.where(rim, pltpu.roll(pack, pack.shape[1] - k, axis=1) if k else pack, 0.0)


def reciprocal(value):
    guess = pl.reciprocal(value, approx=True)
    return guess * (2.0 - value * guess)


def sweep(slices, body, carry):
    group = UNROLL if slices % UNROLL == 0 else slices

    def step(i, carry):
        for offset in range(group):
            carry = body(group * i + offset, offset, carry)
        return carry

    return lax.fori_loop(0, slices // group, step, carry)


def beam_sides(cells):
    count, rank = lax.axis_size("beam"), lax.axis_index("beam")
    if count == 2:
        return [
            (
                jnp.where(rank == 0, cells - 1, 0),
                jnp.where(rank == 0, F32(-1.0), F32(1.0)),
                None,
            )
        ]
    return [(cells - 1, F32(-1.0), rank < count - 1), (0, F32(1.0), rank > 0)]


def beam_rows(first, last):
    count, rank = lax.axis_size("beam"), lax.axis_index("beam")
    if count == 2:
        return [jnp.where(rank == 0, last, first)]
    return [last, first]


def face(own, other, sign, there):
    step = (own - other) * sign
    return step if there is None else jnp.where(there, step, 0.0)


def exchange_beam(rows):
    if lax.axis_size("beam") == 2:
        return [lax.ppermute(rows[0], "beam", [(0, 1), (1, 0)])]
    return [shifted(rows[1], "beam", -1), shifted(rows[0], "beam", 1)]


def open_kernel(total, view_ref, source_ref, *refs):
    small, refs = refs[:4], refs[4:]
    maps_ref, inside_ref, coef_ref, *refs = refs
    elems, slices, cells, width = maps_ref.shape
    faces = len(beam_sides(cells))
    face_refs, refs = refs[:faces], refs[faces:]
    beta_ref, kappa_ref, line_ref, side_ref, sems = refs
    half = slices // 2
    parts = [pl.ds(0, half), pl.ds(half, slices - half)] if half else [pl.ds(0, slices)]
    fetch = []
    for i, (ref, kept) in enumerate(zip(small, (beta_ref, kappa_ref, line_ref, side_ref))):
        fetch.append(pltpu.make_async_copy(ref, kept, sems.at[i]))
    large = []
    for i, at in enumerate(parts):
        large.append(pltpu.make_async_copy(source_ref.at[:, at], maps_ref.at[:, at], sems.at[len(small) + i]))
    for copy in large[:1] + fetch + large[1:]:
        copy.start()
    for copy in fetch:
        copy.wait()
    for e in range(elems):
        line = line_ref[e]
        for f in range(elems):
            coef_ref[e * elems + f : e * elems + f + 1] = jnp.full((1, width), kappa_ref[f, line])
        coef_ref[elems * elems + e : elems * elems + e + 1] = jnp.full((1, width), side_ref[e].astype(F32))
    view = view_ref[0, 0]
    beta = [beta_ref[view, e] for e in range(elems)]
    sub = lax.broadcasted_iota(jnp.int32, maps_ref.shape[2:], 0)
    for z in range(slices):
        if z == 0 or z == half:
            large[1 if z else 0].wait()
        tiles = [maps_ref[e, z] for e in range(elems)]
        mu = beta[0] * tiles[0]
        for e in range(1, elems):
            mu = mu + beta[e] * tiles[e]
        run = mu
        reach = 1
        while reach < cells:
            run = run + jnp.where(sub >= reach, pltpu.roll(run, reach, axis=0), 0.0)
            reach *= 2
        inside_ref[z] = jnp.where(sub >= 1, pltpu.roll(run, 1, axis=0), 0.0)
        face_refs[0][elems * slices + z : elems * slices + z + 1] = run[cells - 1 : cells]
        for e in range(elems):
            rows = beam_rows(tiles[e][0:1], tiles[e][cells - 1 : cells])
            for ref, row in zip(face_refs, rows):
                ref[e * slices + z : e * slices + z + 1] = row


def depth_kernel(total, maps_ref, coef_ref, local_ref, pack_ref, mu_ref, parts_ref, sums_ref):
    elems, slices, cells, width = maps_ref.shape
    rows = slices * cells
    row = lax.broadcasted_iota(jnp.int32, (2 * width, 2 * width), 0)
    col = lax.broadcasted_iota(jnp.int32, (2 * width, 2 * width), 1)
    row = jnp.where(row >= width, row - width, row)
    table = jnp.where((row < col) | (col >= width), 1.0, 0.0).astype(jnp.bfloat16)
    for e in range(elems):
        mu = coef_ref[e * elems : e * elems + 1][None] * maps_ref[0]
        for f in range(1, elems):
            mu = mu + coef_ref[e * elems + f : e * elems + f + 1][None] * maps_ref[f]
        mu_ref[e] = mu
        flat = mu.reshape(rows, width)
        high = flat.astype(jnp.bfloat16)
        low = (flat - high.astype(F32)).astype(jnp.bfloat16)
        parts_ref[e * rows : (e + 1) * rows, 0:width] = high
        parts_ref[e * rows : (e + 1) * rows, width:] = low
    sums_ref[...] = jnp.dot(parts_ref[...], table, preferred_element_type=F32)
    lane = lax.broadcasted_iota(jnp.int32, (cells, width), 1)
    scale = -1.0 / total
    strip = jnp.zeros((cells, width), F32)
    edges = [strip, strip]
    for e in range(elems):
        forward = coef_ref[elems * elems + e : elems * elems + e + 1] == 0.0
        for z in range(slices):
            k = e * slices + z
            before = sums_ref[k * cells : (k + 1) * cells, 0:width]
            whole = sums_ref[k * cells : (k + 1) * cells, width:]
            after = whole - before - mu_ref[e, z]
            local_ref[e, z] = jnp.exp(jnp.where(forward, before, after) * scale)
            strip = jnp.where(lane == k, whole, strip)
            edges[k % 2] = gather_edges(edges[k % 2], maps_ref[e, z], lane, k)
    pack_ref[0], pack_ref[1] = packed_edges(edges, lane)
    pack_ref[2] = strip
    far = jnp.zeros((cells, width), F32)
    for e in range(elems):
        inside = (lane >= e * slices) & (lane < (e + 1) * slices)
        far = jnp.where(inside, coef_ref[elems * elems + e : elems * elems + e + 1][:, 0:1], far)
    pack_ref[3] = far


def weight_kernel(total, skip, maps_ref, inside_ref, carry_ref, local_ref, pack_ref, weight_ref, out_ref, zone_ref, ztwo_ref):
    elems, slices, cells, width = maps_ref.shape
    lane = lax.broadcasted_iota(jnp.int32, (cells, width), 1)
    there = lax.axis_index("beam") > 0
    scale = -1.0 / total

    def step(z, packs):
        proj, whole = packs
        place = lane - z
        carry = jnp.where(there, carry_ref[pl.ds(skip + z, 1)], 0.0)
        att = jnp.exp((inside_ref[z] + carry) * scale)
        for e in range(elems):
            weight = att * local_ref[e, z]
            weight_ref[e, z] = weight
            here = place == e * slices
            proj = jnp.where(here, jnp.sum(weight * maps_ref[e, z], axis=1, keepdims=True), proj)
            whole = jnp.where(here, jnp.sum(weight, axis=1, keepdims=True), whole)
        return proj, whole

    zero = jnp.zeros((cells, width), F32)
    proj, whole = lax.fori_loop(0, slices, step, (zero, zero), unroll=UNROLL)
    out_ref[0] = pack_ref[0]
    out_ref[1] = pack_ref[1]
    out_ref[2] = pack_ref[2]
    out_ref[3] = proj
    out_ref[4] = whole
    for e in range(elems):
        zone_ref[e], ztwo_ref[e] = pair_order(maps_ref[e, slices - 1], maps_ref[e, 0])


def dual_step(field, ahead, dual, last):
    step = 0.5 * (ahead - field)
    return jnp.where(last, 0.0, clip(step if dual is None else dual + step))


def tile_duals(tile, dual_x, dual_y, sub, lane, shape):
    cells, width = shape
    new_x = dual_step(tile, pltpu.roll(tile, cells - 1, axis=0), dual_x, sub == cells - 1)
    new_y = dual_step(tile, pltpu.roll(tile, width - 1, axis=1), dual_y, lane == width - 1)
    spread = pltpu.roll(new_x, 1, axis=0) - new_x + (pltpu.roll(new_y, 1, axis=1) - new_y)
    return new_x, new_y, spread


def join(ref, width):
    elems, cells, slices = ref.shape
    parts = [ref[e] for e in range(elems)]
    if elems * slices < width:
        parts.append(jnp.zeros((cells, width - elems * slices), F32))
    return jnp.concatenate(parts, axis=1)


def first_dual_kernel(maps_ref, measured_ref, *refs):
    elems, slices, cells, width = maps_ref.shape
    sides = beam_sides(cells)
    own_refs, refs = refs[: len(sides)], refs[len(sides) :]
    other_refs, refs = refs[: len(sides)], refs[len(sides) :]
    dual_z_ref, dual_x_ref, dual_y_ref, adj_ref, still_ref, *edge_refs = refs
    sub = lax.broadcasted_iota(jnp.int32, (cells, width), 0)
    lane = lax.broadcasted_iota(jnp.int32, (cells, width), 1)
    still_ref[...] = join(measured_ref, width)
    for (row, sign, there), own, other, edge in zip(sides, own_refs, other_refs, edge_refs):
        rows = pl.ds(0, elems * slices)
        edge[...] = clip(0.5 * face(own[rows], other[rows], sign, there))
    def step(z, behind):
        at_end = z == slices - 1
        duals = []
        for e in range(elems):
            tile = maps_ref[e, z]
            ahead = maps_ref[e, jnp.minimum(z + 1, slices - 1)]
            dual_z = jnp.where(at_end, 0.0, clip(0.5 * (ahead - tile)))
            dual_x, dual_y, spread = tile_duals(tile, None, None, sub, lane, (cells, width))
            dual_z_ref[e, z] = dual_z
            dual_x_ref[e, z] = dual_x
            dual_y_ref[e, z] = dual_y
            spread = spread + (behind[e] - dual_z)
            for (row, sign, there), edge in zip(sides, edge_refs):
                spread = spread + jnp.where(sub == row, sign * edge[pl.ds(e * slices + z, 1)], 0.0)
            adj_ref[e, z] = spread
            duals.append(dual_z)
        return tuple(duals)

    zero = jnp.zeros((cells, width), F32)
    lax.fori_loop(0, slices, step, (zero,) * elems, unroll=UNROLL)


def part(ref, pack):
    slices = ref.shape[2]
    for e in range(ref.shape[0]):
        ref[e] = pack[:, e * slices : (e + 1) * slices]


def first_update_kernel(total, size, maps_ref, weight_ref, adj_ref, still_ref, far_ref, own_ref, zone_ref, ztwo_ref,
                        *refs):
    elems, slices, cells, width = maps_ref.shape
    pack_refs, refs = refs[:-9], refs[-9:]
    full_ref, tau_ref, cur_ref, ext_ref, dd_ref, yedge_ref, zdual_ref, out_ref, emission_ref = refs
    count, rank = lax.axis_size("gz"), lax.axis_index("gz")
    mine = lax.axis_index("path")
    pack_shape = (cells, width)
    lane = lax.broadcasted_iota(jnp.int32, pack_shape, 1)
    rim = (lane == 0) | (lane == width - 1)
    packs, state = merge_all(size // 2, -1.0 / total, pack_refs, far_ref[3] != 0.0, 3)
    image, weights = packs[3], packs[4]
    ahead, behind, base = state
    own = jnp.exp(base * (-1.0 / total))
    sig = 1.0 / weights
    data_dual = sig * (image - still_ref[...]) / (1.0 + sig)
    dd_ref[0] = data_dual
    dd_ref[1] = sig
    part(emission_ref, image * (1.0 / total))
    y_ahead = jnp.where(mine < size - 1, clip(0.5 * (ahead - own_ref[1])), 0.0)
    y_behind = jnp.where(mine > 0, clip(0.5 * (own_ref[0] - behind)), 0.0)
    joined = join_edges(y_behind, -y_ahead, lane)
    yedge_ref[0] = y_ahead
    yedge_ref[1] = y_behind

    def weigh(z, offset, none):
        for e in range(elems):
            weight = weight_ref[e, z] * spread(own, lane, e * slices + z)
            full_ref[e, z] = weight
            tau_ref[e, z] = reciprocal(weight + 6.0)
            ext_ref[e, z] = weight * spread(data_dual, lane, e * slices + z) + adj_ref[e, z]
        return none

    def project(z, offset, image):
        for e in range(elems):
            row = jnp.sum(full_ref[e, z] * ext_ref[e, z], axis=1, keepdims=True)
            image = jnp.where(lane == e * slices + z, row, image)
        return image

    zero = jnp.zeros(pack_shape, F32)
    sweep(slices, weigh, 0)
    for e in range(elems):
        ahead, behind = pair_order(zone_ref[e], ztwo_ref[e])
        behind = jnp.where(rank > 0, clip(0.5 * (maps_ref[e, 0] - behind)), 0.0)
        ahead = jnp.where(rank < count - 1, clip(0.5 * (ahead - maps_ref[e, slices - 1])), 0.0)
        zdual_ref[0, e] = behind
        zdual_ref[1, e] = ahead
        ext_ref[e, 0] = ext_ref[e, 0] + behind
        ext_ref[e, slices - 1] = ext_ref[e, slices - 1] - ahead
    edges = [zero, zero]
    for z in range(slices):
        for e in range(elems):
            k = e * slices + z
            tile = maps_ref[e, z]
            step = (ext_ref[e, z] + edge_columns(joined[k % 2], rim, k)) * tau_ref[e, z]
            new = jnp.maximum(tile - step, 0.0)
            ext = 2.0 * new - tile
            cur_ref[e, z] = new
            ext_ref[e, z] = ext
            edges[k % 2] = gather_edges(edges[k % 2], ext, lane, k)
    out_ref[0], out_ref[1] = packed_edges(edges, lane)
    out_ref[2] = sweep(slices, project, zero)
    for i in range(3, out_ref.shape[0]):
        out_ref[i] = zero


def face_kernel(ext_ref, zone_ref, ztwo_ref, *face_refs):
    elems, slices, cells, width = ext_ref.shape
    for e in range(elems):
        for z in range(slices):
            rows = beam_rows(ext_ref[e, z, 0:1], ext_ref[e, z, cells - 1 : cells])
            for ref, row in zip(face_refs, rows):
                ref[e * slices + z : e * slices + z + 1] = row
    for e in range(elems):
        zone_ref[e], ztwo_ref[e] = pair_order(ext_ref[e, slices - 1], ext_ref[e, 0])


def second_dual_kernel(ext_ref, dual_z_ref, dual_x_ref, dual_y_ref, adj_ref):
    elems, slices, cells, width = ext_ref.shape
    sub = lax.broadcasted_iota(jnp.int32, (cells, width), 0)
    lane = lax.broadcasted_iota(jnp.int32, (cells, width), 1)

    def step(z, behind):
        at_end = z == slices - 1
        duals = []
        for e in range(elems):
            tile = ext_ref[e, z]
            ahead = ext_ref[e, jnp.minimum(z + 1, slices - 1)]
            dual_z = jnp.where(at_end, 0.0, clip(dual_z_ref[e, z] + 0.5 * (ahead - tile)))
            _, _, spread = tile_duals(tile, dual_x_ref[e, z], dual_y_ref[e, z], sub, lane, (cells, width))
            adj_ref[e, z] = spread + (behind[e] - dual_z)
            duals.append(dual_z)
        return tuple(duals)

    zero = jnp.zeros((cells, width), F32)
    lax.fori_loop(0, slices, step, (zero,) * elems, unroll=UNROLL)


def second_face_kernel(cur_ref, ext_ref, weight_ref, tau_ref, adj_ref, zdual_ref, zone_ref, ztwo_ref, *refs):
    elems, slices, cells, width = cur_ref.shape
    sides = beam_sides(cells)
    edge_refs, refs = refs[: len(sides)], refs[len(sides) :]
    own_refs, refs = refs[: len(sides)], refs[len(sides) :]
    other_refs, refs = refs[: len(sides)], refs[len(sides) :]
    base_ref, pull_ref, *face_refs = refs
    count, rank = lax.axis_size("gz"), lax.axis_index("gz")
    sub = lax.broadcasted_iota(jnp.int32, (cells, width), 0)
    for (row, sign, there), edge, own, other, out in zip(sides, edge_refs, own_refs, other_refs, face_refs):
        out[...] = clip(edge[...] + 0.5 * face(own[...], other[...], sign, there)) * sign
    for e in range(elems):
        ahead, behind = pair_order(zone_ref[e], ztwo_ref[e])
        behind = jnp.where(rank > 0, clip(zdual_ref[0, e] + 0.5 * (ext_ref[e, 0] - behind)), 0.0)
        ahead = clip(zdual_ref[1, e] + 0.5 * (ahead - ext_ref[e, slices - 1]))
        ahead = jnp.where(rank < count - 1, ahead, 0.0)
        for z in range(slices):
            k = e * slices + z
            adj = adj_ref[e, z]
            if z == 0:
                adj = adj + behind
            if z == slices - 1:
                adj = adj - ahead
            for (row, sign, there), out in zip(sides, face_refs):
                adj = adj + jnp.where(sub == row, out[k : k + 1], 0.0)
            tau = tau_ref[e, z]
            base_ref[e, z] = cur_ref[e, z] - tau * adj
            pull_ref[e, z] = tau * weight_ref[e, z]


def last_update_kernel(size, base_ref, pull_ref, tau_ref, still_ref, dd_ref, yedge_ref, own_pack_ref, *refs):
    elems, slices, cells, width = base_ref.shape
    *pack_refs, new_ref, dual_ref = refs
    mine = lax.axis_index("path")
    packs, (ahead, behind) = merge_all(size // 2, None, pack_refs, None, 2)
    image = packs[2]
    sig = dd_ref[1]
    data_dual = (dd_ref[0] + sig * (image - still_ref[...])) / (1.0 + sig)
    part(dual_ref, data_dual)
    y_ahead = jnp.where(mine < size - 1, clip(yedge_ref[0] + 0.5 * (ahead - own_pack_ref[1])), 0.0)
    y_behind = jnp.where(mine > 0, clip(yedge_ref[1] + 0.5 * (own_pack_ref[0] - behind)), 0.0)
    lane = lax.broadcasted_iota(jnp.int32, (cells, width), 1)
    rim = (lane == 0) | (lane == width - 1)
    joined = join_edges(y_behind, -y_ahead, lane)

    def weigh(z, offset, none):
        for e in range(elems):
            new_ref[e, z] = base_ref[e, z] - pull_ref[e, z] * spread(data_dual, lane, e * slices + z)
        return none

    sweep(slices, weigh, 0)
    for z in range(slices):
        for e in range(elems):
            k = e * slices + z
            edge = edge_columns(joined[k % 2], rim, k)
            new_ref[e, z] = jnp.maximum(new_ref[e, z] - edge * tau_ref[e, z], 0.0)


def shards(maps, measured, beta_table, view, kappa, line_of, side):
    elems, slices, cells, width = maps.shape
    total_x = cells * lax.axis_size("beam")
    total_y = width * lax.axis_size("path")
    size = lax.axis_size("path")
    block = f32(elems, slices, cells, width)
    plane = f32(elems, cells, width)
    rows = f32(elems * slices, width)
    faces = len(beam_sides(cells))
    measured = measured.transpose(0, 2, 1)
    kappa = kappa.T
    view = view.reshape(1, 1)

    tall = f32((elems + 1) * slices, width)
    maps, inside, coef, *own = call(
        functools.partial(open_kernel, total_x),
        [view] + [pltpu.with_memory_space_constraint(a, pltpu.HBM) for a in (maps, beta_table, kappa, line_of, side)],
        [block, f32(slices, cells, width), f32(elems * elems + elems, width), tall] + [rows] * (faces - 1),
        [SMEM] + [pltpu.HBM] * 5,
        [
            pltpu.SMEM(beta_table.shape, F32),
            pltpu.SMEM(kappa.shape, F32),
            pltpu.SMEM(line_of.shape, jnp.int32),
            pltpu.SMEM(side.shape, jnp.int32),
            pltpu.SemaphoreType.DMA((6,)),
        ],
    )
    other = exchange_beam(own)
    carry, skip = other[-1], elems * slices
    beams = lax.axis_size("beam")
    if beams > 2:
        carry, skip = carry[skip:], 0
        reach = 1
        while reach < beams - 1:
            far = lax.axis_index("beam") > reach
            carry = carry + jnp.where(far, shifted(carry, "beam", reach), 0.0)
            reach *= 2
    local, still = call(
        functools.partial(depth_kernel, total_y),
        [maps, coef],
        [block, f32(4, cells, width)],
        [VMEM] * 2,
        [
            pltpu.VMEM(maps.shape, F32),
            pltpu.VMEM((elems * slices * cells, 2 * width), jnp.bfloat16),
            pltpu.VMEM((elems * slices * cells, 2 * width), F32),
        ],
    )
    weight, pack, zone, ztwo = call(
        functools.partial(weight_kernel, total_x, skip),
        [maps, inside, carry, local, still],
        [block, f32(5, cells, width), plane, plane],
        [VMEM] * 5,
    )
    packs = around(pack, "path", -1.0 / total_y, still)
    zone, ztwo = swapped(zone, 0), swapped(ztwo, 1)
    dual_z, dual_x, dual_y, adj, counts, *edge = call(
        first_dual_kernel,
        [maps, measured, *own, *other],
        [block, block, block, block, f32(cells, width)] + [rows] * faces,
        [VMEM] * (2 + 2 * faces),
    )
    weight, tau, current, extrap, dd, yedge, zdual, pack, emission = call(
        functools.partial(first_update_kernel, total_y, size),
        [maps, weight, adj, counts, still, pack, zone, ztwo, *packs],
        [block, block, block, block, f32(2, cells, width), f32(2, cells, width), f32(2, elems, cells, width),
         f32(5, cells, width), f32(elems, cells, slices)],
        [VMEM] * (8 + len(packs)),
    )
    packs = around(pack, "path", None)
    zone, ztwo, *own = call(face_kernel, [extrap], [plane, plane] + [rows] * faces, [VMEM])
    zone, ztwo = swapped(zone, 0), swapped(ztwo, 1)
    other = exchange_beam(own)
    (adj,) = call(second_dual_kernel, [extrap, dual_z, dual_x, dual_y], [block], [VMEM] * 4)
    base, pull = call(
        second_face_kernel,
        [current, extrap, weight, tau, adj, zdual, zone, ztwo, *edge, *own, *other],
        [block, block],
        [VMEM] * (8 + 3 * faces),
        [pltpu.VMEM((elems * slices, width), F32)] * faces,
    )
    current, data_dual = call(
        functools.partial(last_update_kernel, size),
        [base, pull, tau, counts, dd, yedge, pack, *packs],
        [block, f32(elems, cells, slices)],
        [VMEM] * (7 + len(packs)),
    )
    return emission.transpose(0, 2, 1), current, data_dual.transpose(0, 2, 1)


def solution(mesh):
    return jax.shard_map(
        shards,
        mesh=mesh,
        in_specs=(P(None, "gz", "beam", "path"), P(None, "gz", "beam"), P(), P(), P(), P(), P()),
        out_specs=(P(None, "gz", "beam"), P(None, "gz", "beam", "path"), P(None, "gz", "beam")),
        check_vma=False,
    )
```

```python
import functools

import jax
import jax.numpy as jnp
from jax import lax
from jax.experimental import pallas as pl
from jax.experimental.pallas import tpu as pltpu
from jax.sharding import PartitionSpec as P

ITERS = 2
LAM = 0.1
F32 = jnp.float32
VMEM = pltpu.VMEM
SMEM = pltpu.SMEM
UNROLL = 4
VMEM_LIMIT = 32 * 1024 * 1024


def clip(value):
    return jnp.clip(value, -LAM, LAM)


def call(body, ins, outs, spaces, scratch=(), flops=1_000_000):
    specs = [pl.BlockSpec(memory_space=space) for space in spaces]
    moved = sum(a.size * 4 for a in ins) + sum(o.size * 4 for o in outs)
    return pl.pallas_call(
        body,
        out_shape=outs,
        in_specs=specs,
        out_specs=[pl.BlockSpec(memory_space=VMEM)] * len(outs),
        scratch_shapes=list(scratch),
        compiler_params=pltpu.CompilerParams(vmem_limit_bytes=VMEM_LIMIT),
        cost_estimate=pl.CostEstimate(flops=flops, bytes_accessed=moved, transcendentals=0),
    )(*ins)


def f32(*shape):
    return jax.ShapeDtypeStruct(shape, F32)


def shifted(block, axis, distance):
    n = lax.axis_size(axis)
    return lax.ppermute(block, axis, [((i - distance) % n, i) for i in range(n)])


def swapped(block, start):
    n, paths = lax.axis_size("gz"), lax.axis_size("path")
    route = []
    for p in range(paths):
        for z in range(n):
            other = z + 1 if (z - start) % 2 == 0 else z - 1
            there = (p, other) if 0 <= other < n else (p ^ 1, z)
            route.append((p * n + z, there[0] * n + there[1]))
    return lax.ppermute(block, ("path", "gz"), route)


def pair_order(ahead, behind):
    even = lax.rem(lax.axis_index("gz"), 2) == 0
    return jnp.where(even, ahead, behind), jnp.where(even, behind, ahead)


def merged(mine, other, far, scale, bit):
    upper = (lax.axis_index("path") & bit) != 0
    low = [jnp.where(upper, o, m) for m, o in zip(mine, other)]
    high = [jnp.where(upper, m, o) for m, o in zip(mine, other)]
    if far is None:
        return [low[0], high[1]] + [a + b for a, b in zip(low[2:], high[2:])]
    low_factor = jnp.where(far, jnp.exp(high[2] * scale), 1.0)
    high_factor = jnp.where(far, 1.0, jnp.exp(low[2] * scale))
    sums = [low_factor * a + high_factor * b for a, b in zip(low[3:], high[3:])]
    return [low[0], high[1], low[2] + high[2]] + sums


def passed(state, other, far, bit):
    mine = lax.axis_index("path")
    ahead = jnp.where(mine & (2 * bit - 1) == bit - 1, other[0], state[0])
    behind = jnp.where(mine & (2 * bit - 1) == bit, other[1], state[1])
    if far is None:
        return [ahead, behind]
    upper = (mine & bit) != 0
    in_way = jnp.where(upper, jnp.where(far, 0.0, other[2]), jnp.where(far, other[2], 0.0))
    return [ahead, behind, state[2] + in_way]


def rows_of(ref):
    return [ref[i] for i in range(ref.shape[0])]


def merge_all(bit, scale, refs, far, kept):
    mine_ref, other_ref, *state_refs = refs
    state = rows_of(state_refs[0]) if state_refs else [jnp.zeros(mine_ref.shape[1:], F32)] * kept
    mine, other = rows_of(mine_ref), rows_of(other_ref)
    return merged(mine, other, far, scale, bit), passed(state, other, far, bit)


def merge_kernel(bit, scale, kept, *refs):
    *refs, out_ref, state_ref = refs
    far = None
    if kept == 3:
        far_ref, *refs = refs
        far = far_ref[3] != 0.0
    packs, state = merge_all(bit, scale, refs, far, kept)
    for ref, values in ((out_ref, packs), (state_ref, state)):
        for i, value in enumerate(values):
            ref[i] = value


def around(block, axis, scale, far=None):
    n = lax.axis_size(axis)
    if n < 2 or n & (n - 1):
        raise ValueError("path size")
    kept = 2 if far is None else 3
    state = []
    bit = 1
    while True:
        other = lax.ppermute(block, axis, [(i, i ^ bit) for i in range(n)])
        if 2 * bit == n:
            return [block, other] + state
        ins = ([] if far is None else [far]) + [block, other] + state
        block, *state = call(
            functools.partial(merge_kernel, bit, scale, kept),
            ins,
            [f32(*block.shape), f32(kept, *block.shape[1:])],
            [VMEM] * len(ins),
        )
        bit *= 2


def split(flat):
    high = flat.astype(jnp.bfloat16)
    return high, (flat - high.astype(F32)).astype(jnp.bfloat16)


def put_rows(parts_ref, e, tiles):
    slices, cells, width = tiles.shape
    at = slice(e * slices * cells, (e + 1) * slices * cells)
    parts_ref[at, 0:width], parts_ref[at, width:] = split(tiles.reshape(slices * cells, width))


def row_sums(parts_ref, sums_ref):
    depth, width = parts_ref.shape[1], sums_ref.shape[1]
    ones = jnp.ones((depth, width), jnp.bfloat16)
    sums_ref[...] = jnp.dot(parts_ref[...], ones, preferred_element_type=F32)


def packed_sums(sums_ref, lane):
    cells, width = lane.shape
    pack = jnp.zeros((cells, width), F32)
    for k in range(sums_ref.shape[0] // cells):
        pack = jnp.where(lane == k, sums_ref[k * cells : (k + 1) * cells], pack)
    return pack


def spread(pack, lane, elems, slices, parts_ref, sums_ref):
    for e in range(elems):
        put_rows(parts_ref, e, jnp.stack([jnp.where(lane == e * slices + z, pack, 0.0) for z in range(slices)]))
    row_sums(parts_ref, sums_ref)


def tile_of(ref, k, cells):
    return ref[pl.ds(pl.multiple_of(k * cells, cells), cells)]


def gather_edges(pack, tile, lane, k):
    width = tile.shape[1]
    here = (lane == k) | (lane == (k - 1) % width)
    return jnp.where(here, pltpu.roll(tile, k, axis=1) if k else tile, pack)


def packed_edges(edges, lane):
    even = lane % 2 == 0
    first = jnp.where(even, edges[0], edges[1])
    return first, pltpu.roll(jnp.where(even, edges[1], edges[0]), 1, axis=1)


def join_edges(first, last, lane):
    width = first.shape[1]
    last = pltpu.roll(last, width - 1, axis=1)
    even = lane % 2 == 0
    return jnp.where(even, first, last), jnp.where(even, last, first)


def edge_columns(pack, rim, k):
    return jnp.where(rim, pltpu.roll(pack, pack.shape[1] - k, axis=1) if k else pack, 0.0)


def reciprocal(value):
    guess = pl.reciprocal(value, approx=True)
    return guess * (2.0 - value * guess)


def sweep(slices, body, carry):
    group = UNROLL if slices % UNROLL == 0 else slices

    def step(i, carry):
        for offset in range(group):
            carry = body(group * i + offset, offset, carry)
        return carry

    return lax.fori_loop(0, slices // group, step, carry)


def beam_sides(cells):
    count, rank = lax.axis_size("beam"), lax.axis_index("beam")
    if count == 2:
        return [
            (
                jnp.where(rank == 0, cells - 1, 0),
                jnp.where(rank == 0, F32(-1.0), F32(1.0)),
                None,
            )
        ]
    return [(cells - 1, F32(-1.0), rank < count - 1), (0, F32(1.0), rank > 0)]


def beam_rows(first, last):
    count, rank = lax.axis_size("beam"), lax.axis_index("beam")
    if count == 2:
        return [jnp.where(rank == 0, last, first)]
    return [last, first]


def face(own, other, sign, there):
    step = (own - other) * sign
    return step if there is None else jnp.where(there, step, 0.0)


def exchange_beam(rows):
    if lax.axis_size("beam") == 2:
        return [lax.ppermute(rows[0], "beam", [(0, 1), (1, 0)])]
    return [shifted(rows[1], "beam", -1), shifted(rows[0], "beam", 1)]


def open_kernel(total, view_ref, source_ref, *refs):
    small, refs = refs[:4], refs[4:]
    maps_ref, inside_ref, coef_ref, *refs = refs
    elems, slices, cells, width = maps_ref.shape
    faces = len(beam_sides(cells))
    face_refs, refs = refs[:faces], refs[faces:]
    beta_ref, kappa_ref, line_ref, side_ref, sems = refs
    half = slices // 2
    parts = [pl.ds(0, half), pl.ds(half, slices - half)] if half else [pl.ds(0, slices)]
    fetch = []
    for i, (ref, kept) in enumerate(zip(small, (beta_ref, kappa_ref, line_ref, side_ref))):
        fetch.append(pltpu.make_async_copy(ref, kept, sems.at[i]))
    large = []
    for i, at in enumerate(parts):
        large.append(pltpu.make_async_copy(source_ref.at[:, at], maps_ref.at[:, at], sems.at[len(small) + i]))
    for copy in large[:1] + fetch + large[1:]:
        copy.start()
    for copy in fetch:
        copy.wait()
    for e in range(elems):
        line = line_ref[e]
        for f in range(elems):
            coef_ref[e * elems + f : e * elems + f + 1] = jnp.full((1, width), kappa_ref[f, line])
        coef_ref[elems * elems + e : elems * elems + e + 1] = jnp.full((1, width), side_ref[e].astype(F32))
    view = view_ref[0, 0]
    beta = [beta_ref[view, e] for e in range(elems)]
    sub = lax.broadcasted_iota(jnp.int32, maps_ref.shape[2:], 0)
    for z in range(slices):
        if z == 0 or z == half:
            large[1 if z else 0].wait()
        tiles = [maps_ref[e, z] for e in range(elems)]
        mu = beta[0] * tiles[0]
        for e in range(1, elems):
            mu = mu + beta[e] * tiles[e]
        run = mu
        reach = 1
        while reach < cells:
            run = run + jnp.where(sub >= reach, pltpu.roll(run, reach, axis=0), 0.0)
            reach *= 2
        inside_ref[z] = jnp.where(sub >= 1, pltpu.roll(run, 1, axis=0), 0.0)
        face_refs[0][elems * slices + z : elems * slices + z + 1] = run[cells - 1 : cells]
        for e in range(elems):
            rows = beam_rows(tiles[e][0:1], tiles[e][cells - 1 : cells])
            for ref, row in zip(face_refs, rows):
                ref[e * slices + z : e * slices + z + 1] = row


def depth_kernel(total, maps_ref, coef_ref, local_ref, pack_ref, mu_ref, parts_ref, sums_ref):
    elems, slices, cells, width = maps_ref.shape
    rows = slices * cells
    row = lax.broadcasted_iota(jnp.int32, (2 * width, 2 * width), 0)
    col = lax.broadcasted_iota(jnp.int32, (2 * width, 2 * width), 1)
    row = jnp.where(row >= width, row - width, row)
    table = jnp.where((row < col) | (col >= width), 1.0, 0.0).astype(jnp.bfloat16)
    for e in range(elems):
        mu = coef_ref[e * elems : e * elems + 1][None] * maps_ref[0]
        for f in range(1, elems):
            mu = mu + coef_ref[e * elems + f : e * elems + f + 1][None] * maps_ref[f]
        mu_ref[e] = mu
        put_rows(parts_ref, e, mu)
    sums_ref[...] = jnp.dot(parts_ref[...], table, preferred_element_type=F32)
    lane = lax.broadcasted_iota(jnp.int32, (cells, width), 1)
    scale = -1.0 / total
    strip = jnp.zeros((cells, width), F32)
    edges = [strip, strip]
    for e in range(elems):
        forward = coef_ref[elems * elems + e : elems * elems + e + 1] == 0.0
        for z in range(slices):
            k = e * slices + z
            before = sums_ref[k * cells : (k + 1) * cells, 0:width]
            whole = sums_ref[k * cells : (k + 1) * cells, width:]
            after = whole - before - mu_ref[e, z]
            local_ref[e, z] = jnp.exp(jnp.where(forward, before, after) * scale)
            strip = jnp.where(lane == k, whole, strip)
            edges[k % 2] = gather_edges(edges[k % 2], maps_ref[e, z], lane, k)
    pack_ref[0], pack_ref[1] = packed_edges(edges, lane)
    pack_ref[2] = strip
    far = jnp.zeros((cells, width), F32)
    for e in range(elems):
        inside = (lane >= e * slices) & (lane < (e + 1) * slices)
        far = jnp.where(inside, coef_ref[elems * elems + e : elems * elems + e + 1][:, 0:1], far)
    pack_ref[3] = far


def weight_kernel(total, skip, maps_ref, inside_ref, carry_ref, local_ref, pack_ref, weight_ref, out_ref, zone_ref,
                  ztwo_ref, proj_ref, whole_ref, sums_ref):
    elems, slices, cells, width = maps_ref.shape
    lane = lax.broadcasted_iota(jnp.int32, (cells, width), 1)
    there = lax.axis_index("beam") > 0
    carry = jnp.where(there, carry_ref[skip : skip + slices], 0.0)
    att = jnp.exp((inside_ref[...] + carry[:, None]) * (-1.0 / total))
    for e in range(elems):
        weight = att * local_ref[e]
        weight_ref[e] = weight
        put_rows(whole_ref, e, weight)
        put_rows(proj_ref, e, weight * maps_ref[e])
    row_sums(proj_ref, sums_ref)
    out_ref[3] = packed_sums(sums_ref, lane)
    row_sums(whole_ref, sums_ref)
    out_ref[4] = packed_sums(sums_ref, lane)
    for i in range(3):
        out_ref[i] = pack_ref[i]
    for e in range(elems):
        zone_ref[e], ztwo_ref[e] = pair_order(maps_ref[e, slices - 1], maps_ref[e, 0])


def dual_step(field, ahead, dual, last):
    step = 0.5 * (ahead - field)
    return jnp.where(last, 0.0, clip(step if dual is None else dual + step))


def tile_duals(tile, dual_x, dual_y, sub, lane, shape):
    cells, width = shape
    new_x = dual_step(tile, pltpu.roll(tile, cells - 1, axis=0), dual_x, sub == cells - 1)
    new_y = dual_step(tile, pltpu.roll(tile, width - 1, axis=1), dual_y, lane == width - 1)
    spread = pltpu.roll(new_x, 1, axis=0) - new_x + (pltpu.roll(new_y, 1, axis=1) - new_y)
    return new_x, new_y, spread


def join(ref, width):
    elems, cells, slices = ref.shape
    parts = [ref[e] for e in range(elems)]
    if elems * slices < width:
        parts.append(jnp.zeros((cells, width - elems * slices), F32))
    return jnp.concatenate(parts, axis=1)


def first_dual_kernel(maps_ref, measured_ref, *refs):
    elems, slices, cells, width = maps_ref.shape
    sides = beam_sides(cells)
    own_refs, refs = refs[: len(sides)], refs[len(sides) :]
    other_refs, refs = refs[: len(sides)], refs[len(sides) :]
    dual_z_ref, dual_x_ref, dual_y_ref, adj_ref, still_ref, *edge_refs = refs
    sub = lax.broadcasted_iota(jnp.int32, (cells, width), 0)
    lane = lax.broadcasted_iota(jnp.int32, (cells, width), 1)
    still_ref[...] = join(measured_ref, width)
    for (row, sign, there), own, other, edge in zip(sides, own_refs, other_refs, edge_refs):
        rows = pl.ds(0, elems * slices)
        edge[...] = clip(0.5 * face(own[rows], other[rows], sign, there))
    def step(z, behind):
        at_end = z == slices - 1
        duals = []
        for e in range(elems):
            tile = maps_ref[e, z]
            ahead = maps_ref[e, jnp.minimum(z + 1, slices - 1)]
            dual_z = jnp.where(at_end, 0.0, clip(0.5 * (ahead - tile)))
            dual_x, dual_y, spread = tile_duals(tile, None, None, sub, lane, (cells, width))
            dual_z_ref[e, z] = dual_z
            dual_x_ref[e, z] = dual_x
            dual_y_ref[e, z] = dual_y
            spread = spread + (behind[e] - dual_z)
            for (row, sign, there), edge in zip(sides, edge_refs):
                spread = spread + jnp.where(sub == row, sign * edge[pl.ds(e * slices + z, 1)], 0.0)
            adj_ref[e, z] = spread
            duals.append(dual_z)
        return tuple(duals)

    zero = jnp.zeros((cells, width), F32)
    lax.fori_loop(0, slices, step, (zero,) * elems, unroll=UNROLL)


def part(ref, pack):
    slices = ref.shape[2]
    for e in range(ref.shape[0]):
        ref[e] = pack[:, e * slices : (e + 1) * slices]


def first_update_kernel(total, size, maps_ref, weight_ref, adj_ref, still_ref, far_ref, pack_ref, zone_ref, ztwo_ref,
                        *refs):
    elems, slices, cells, width = maps_ref.shape
    pack_refs, refs = refs[:-12], refs[-12:]
    full_ref, tau_ref, cur_ref, ext_ref, dd_ref, yedge_ref, zdual_ref, out_ref, emission_ref, *refs = refs
    parts_ref, own_ref, dual_ref = refs
    count, rank = lax.axis_size("gz"), lax.axis_index("gz")
    mine = lax.axis_index("path")
    pack_shape = (cells, width)
    lane = lax.broadcasted_iota(jnp.int32, pack_shape, 1)
    rim = (lane == 0) | (lane == width - 1)
    packs, state = merge_all(size // 2, -1.0 / total, pack_refs, far_ref[3] != 0.0, 3)
    image, weights = packs[3], packs[4]
    ahead, behind, base = state
    own = jnp.exp(base * (-1.0 / total))
    sig = 1.0 / weights
    data_dual = sig * (image - still_ref[...]) / (1.0 + sig)
    dd_ref[0] = data_dual
    dd_ref[1] = sig
    part(emission_ref, image * (1.0 / total))
    y_ahead = jnp.where(mine < size - 1, clip(0.5 * (ahead - pack_ref[1])), 0.0)
    y_behind = jnp.where(mine > 0, clip(0.5 * (pack_ref[0] - behind)), 0.0)
    joined = join_edges(y_behind, -y_ahead, lane)
    yedge_ref[0] = y_ahead
    yedge_ref[1] = y_behind

    def weigh(z, offset, none):
        for e in range(elems):
            k = e * slices + z
            weight = weight_ref[e, z] * tile_of(own_ref, k, cells)
            full_ref[e, z] = weight
            tau_ref[e, z] = reciprocal(weight + 6.0)
            ext_ref[e, z] = weight * tile_of(dual_ref, k, cells) + adj_ref[e, z]
        return none

    zero = jnp.zeros(pack_shape, F32)
    spread(own, lane, elems, slices, parts_ref, own_ref)
    spread(data_dual, lane, elems, slices, parts_ref, dual_ref)
    sweep(slices, weigh, 0)
    for e in range(elems):
        ahead, behind = pair_order(zone_ref[e], ztwo_ref[e])
        behind = jnp.where(rank > 0, clip(0.5 * (maps_ref[e, 0] - behind)), 0.0)
        ahead = jnp.where(rank < count - 1, clip(0.5 * (ahead - maps_ref[e, slices - 1])), 0.0)
        zdual_ref[0, e] = behind
        zdual_ref[1, e] = ahead
        ext_ref[e, 0] = ext_ref[e, 0] + behind
        ext_ref[e, slices - 1] = ext_ref[e, slices - 1] - ahead
    edges = [zero, zero]
    for z in range(slices):
        for e in range(elems):
            k = e * slices + z
            tile = maps_ref[e, z]
            step = (ext_ref[e, z] + edge_columns(joined[k % 2], rim, k)) * tau_ref[e, z]
            new = jnp.maximum(tile - step, 0.0)
            ext = 2.0 * new - tile
            cur_ref[e, z] = new
            ext_ref[e, z] = ext
            edges[k % 2] = gather_edges(edges[k % 2], ext, lane, k)
    out_ref[0], out_ref[1] = packed_edges(edges, lane)
    for e in range(elems):
        put_rows(parts_ref, e, full_ref[e] * ext_ref[e])
    row_sums(parts_ref, own_ref)
    out_ref[2] = packed_sums(own_ref, lane)
    for i in range(3, out_ref.shape[0]):
        out_ref[i] = zero


def face_kernel(ext_ref, zone_ref, ztwo_ref, *face_refs):
    elems, slices, cells, _ = ext_ref.shape
    for e in range(elems):
        for z in range(slices):
            rows = beam_rows(ext_ref[e, z, 0:1], ext_ref[e, z, cells - 1 : cells])
            for ref, row in zip(face_refs, rows):
                ref[e * slices + z : e * slices + z + 1] = row
        zone_ref[e], ztwo_ref[e] = pair_order(ext_ref[e, slices - 1], ext_ref[e, 0])


def second_dual_kernel(ext_ref, dual_z_ref, dual_x_ref, dual_y_ref, adj_ref):
    elems, slices, cells, width = ext_ref.shape
    sub = lax.broadcasted_iota(jnp.int32, (cells, width), 0)
    lane = lax.broadcasted_iota(jnp.int32, (cells, width), 1)

    def step(z, behind):
        at_end = z == slices - 1
        duals = []
        for e in range(elems):
            tile = ext_ref[e, z]
            ahead = ext_ref[e, jnp.minimum(z + 1, slices - 1)]
            dual_z = jnp.where(at_end, 0.0, clip(dual_z_ref[e, z] + 0.5 * (ahead - tile)))
            _, _, spread = tile_duals(tile, dual_x_ref[e, z], dual_y_ref[e, z], sub, lane, (cells, width))
            adj_ref[e, z] = spread + (behind[e] - dual_z)
            duals.append(dual_z)
        return tuple(duals)

    zero = jnp.zeros((cells, width), F32)
    lax.fori_loop(0, slices, step, (zero,) * elems, unroll=UNROLL)


def second_face_kernel(cur_ref, ext_ref, weight_ref, tau_ref, adj_ref, zdual_ref, zone_ref, ztwo_ref, *refs):
    elems, slices, cells, width = cur_ref.shape
    sides = beam_sides(cells)
    edge_refs, refs = refs[: len(sides)], refs[len(sides) :]
    own_refs, refs = refs[: len(sides)], refs[len(sides) :]
    other_refs, refs = refs[: len(sides)], refs[len(sides) :]
    base_ref, pull_ref, *face_refs = refs
    count, rank = lax.axis_size("gz"), lax.axis_index("gz")
    sub = lax.broadcasted_iota(jnp.int32, (cells, width), 0)
    for (row, sign, there), edge, own, other, out in zip(sides, edge_refs, own_refs, other_refs, face_refs):
        out[...] = clip(edge[...] + 0.5 * face(own[...], other[...], sign, there)) * sign
    for e in range(elems):
        ahead, behind = pair_order(zone_ref[e], ztwo_ref[e])
        behind = jnp.where(rank > 0, clip(zdual_ref[0, e] + 0.5 * (ext_ref[e, 0] - behind)), 0.0)
        ahead = clip(zdual_ref[1, e] + 0.5 * (ahead - ext_ref[e, slices - 1]))
        ahead = jnp.where(rank < count - 1, ahead, 0.0)
        for z in range(slices):
            k = e * slices + z
            adj = adj_ref[e, z]
            if z == 0:
                adj = adj + behind
            if z == slices - 1:
                adj = adj - ahead
            for (row, sign, there), out in zip(sides, face_refs):
                adj = adj + jnp.where(sub == row, out[k : k + 1], 0.0)
            tau = tau_ref[e, z]
            base_ref[e, z] = cur_ref[e, z] - tau * adj
            pull_ref[e, z] = tau * weight_ref[e, z]


def last_update_kernel(size, base_ref, pull_ref, tau_ref, still_ref, dd_ref, yedge_ref, own_pack_ref, *refs):
    elems, slices, cells, width = base_ref.shape
    *pack_refs, new_ref, dual_ref, parts_ref, sums_ref = refs
    mine = lax.axis_index("path")
    packs, (ahead, behind) = merge_all(size // 2, None, pack_refs, None, 2)
    image = packs[2]
    sig = dd_ref[1]
    data_dual = (dd_ref[0] + sig * (image - still_ref[...])) / (1.0 + sig)
    part(dual_ref, data_dual)
    y_ahead = jnp.where(mine < size - 1, clip(yedge_ref[0] + 0.5 * (ahead - own_pack_ref[1])), 0.0)
    y_behind = jnp.where(mine > 0, clip(yedge_ref[1] + 0.5 * (own_pack_ref[0] - behind)), 0.0)
    lane = lax.broadcasted_iota(jnp.int32, (cells, width), 1)
    rim = (lane == 0) | (lane == width - 1)
    joined = join_edges(y_behind, -y_ahead, lane)

    def weigh(z, offset, none):
        for e in range(elems):
            new_ref[e, z] = base_ref[e, z] - pull_ref[e, z] * tile_of(sums_ref, e * slices + z, cells)
        return none

    spread(data_dual, lane, elems, slices, parts_ref, sums_ref)
    sweep(slices, weigh, 0)
    for z in range(slices):
        for e in range(elems):
            k = e * slices + z
            edge = edge_columns(joined[k % 2], rim, k)
            new_ref[e, z] = jnp.maximum(new_ref[e, z] - edge * tau_ref[e, z], 0.0)


def shards(maps, measured, beta_table, view, kappa, line_of, side):
    elems, slices, cells, width = maps.shape
    total_x = cells * lax.axis_size("beam")
    total_y = width * lax.axis_size("path")
    size = lax.axis_size("path")
    block = f32(elems, slices, cells, width)
    plane = f32(elems, cells, width)
    rows = f32(elems * slices, width)
    faces = len(beam_sides(cells))
    measured = measured.transpose(0, 2, 1)
    kappa = kappa.T
    view = view.reshape(1, 1)

    tall = f32((elems + 1) * slices, width)
    parts = pltpu.VMEM((elems * slices * cells, 2 * width), jnp.bfloat16)
    sums = pltpu.VMEM((elems * slices * cells, width), F32)
    maps, inside, coef, *own = call(
        functools.partial(open_kernel, total_x),
        [view] + [pltpu.with_memory_space_constraint(a, pltpu.HBM) for a in (maps, beta_table, kappa, line_of, side)],
        [block, f32(slices, cells, width), f32(elems * elems + elems, width), tall] + [rows] * (faces - 1),
        [SMEM] + [pltpu.HBM] * 5,
        [
            pltpu.SMEM(beta_table.shape, F32),
            pltpu.SMEM(kappa.shape, F32),
            pltpu.SMEM(line_of.shape, jnp.int32),
            pltpu.SMEM(side.shape, jnp.int32),
            pltpu.SemaphoreType.DMA((6,)),
        ],
    )
    other = exchange_beam(own)
    carry, skip = other[-1], elems * slices
    beams = lax.axis_size("beam")
    if beams > 2:
        carry, skip = carry[skip:], 0
        reach = 1
        while reach < beams - 1:
            far = lax.axis_index("beam") > reach
            carry = carry + jnp.where(far, shifted(carry, "beam", reach), 0.0)
            reach *= 2
    local, still = call(
        functools.partial(depth_kernel, total_y),
        [maps, coef],
        [block, f32(4, cells, width)],
        [VMEM] * 2,
        [
            pltpu.VMEM(maps.shape, F32),
            parts,
            pltpu.VMEM((elems * slices * cells, 2 * width), F32),
        ],
    )
    weight, pack, zone, ztwo = call(
        functools.partial(weight_kernel, total_x, skip),
        [maps, inside, carry, local, still],
        [block, f32(5, cells, width), plane, plane],
        [VMEM] * 5,
        [parts, parts, sums],
    )
    packs = around(pack, "path", -1.0 / total_y, still)
    zone, ztwo = swapped(zone, 0), swapped(ztwo, 1)
    dual_z, dual_x, dual_y, adj, counts, *edge = call(
        first_dual_kernel,
        [maps, measured, *own, *other],
        [block, block, block, block, f32(cells, width)] + [rows] * faces,
        [VMEM] * (2 + 2 * faces),
    )
    weight, tau, current, extrap, dd, yedge, zdual, pack, emission = call(
        functools.partial(first_update_kernel, total_y, size),
        [maps, weight, adj, counts, still, pack, zone, ztwo, *packs],
        [block, block, block, block, f32(2, cells, width), f32(2, cells, width), f32(2, elems, cells, width),
         f32(5, cells, width), f32(elems, cells, slices)],
        [VMEM] * (8 + len(packs)),
        [parts, sums, sums],
    )
    packs = around(pack, "path", None)
    zone, ztwo, *own = call(face_kernel, [extrap], [plane, plane] + [rows] * faces, [VMEM])
    zone, ztwo = swapped(zone, 0), swapped(ztwo, 1)
    other = exchange_beam(own)
    (adj,) = call(second_dual_kernel, [extrap, dual_z, dual_x, dual_y], [block], [VMEM] * 4)
    base, pull = call(
        second_face_kernel,
        [current, extrap, weight, tau, adj, zdual, zone, ztwo, *edge, *own, *other],
        [block, block],
        [VMEM] * (8 + 3 * faces),
        [pltpu.VMEM((elems * slices, width), F32)] * faces,
    )
    current, data_dual = call(
        functools.partial(last_update_kernel, size),
        [base, pull, tau, counts, dd, yedge, pack, *packs],
        [block, f32(elems, cells, slices)],
        [VMEM] * (7 + len(packs)),
        [parts, sums],
    )
    return emission.transpose(0, 2, 1), current, data_dual.transpose(0, 2, 1)


def solution(mesh):
    return jax.shard_map(
        shards,
        mesh=mesh,
        in_specs=(P(None, "gz", "beam", "path"), P(None, "gz", "beam"), P(), P(), P(), P(), P()),
        out_specs=(P(None, "gz", "beam"), P(None, "gz", "beam", "path"), P(None, "gz", "beam")),
        check_vma=False,
    )
```

```python
import functools

import jax
import jax.numpy as jnp
from jax import lax
from jax.experimental import pallas as pl
from jax.experimental.pallas import tpu as pltpu
from jax.sharding import PartitionSpec as P

ITERS = 2
LAM = 0.1
F32 = jnp.float32
VMEM = pltpu.VMEM
SMEM = pltpu.SMEM
UNROLL = 4
VMEM_LIMIT = 32 * 1024 * 1024


def clip(value):
    return jnp.clip(value, -LAM, LAM)


def call(body, ins, outs, spaces, scratch=(), flops=1_000_000):
    specs = [pl.BlockSpec(memory_space=space) for space in spaces]
    moved = sum(a.size * 4 for a in ins) + sum(o.size * 4 for o in outs)
    return pl.pallas_call(
        body,
        out_shape=outs,
        in_specs=specs,
        out_specs=[pl.BlockSpec(memory_space=VMEM)] * len(outs),
        scratch_shapes=list(scratch),
        compiler_params=pltpu.CompilerParams(vmem_limit_bytes=VMEM_LIMIT),
        cost_estimate=pl.CostEstimate(flops=flops, bytes_accessed=moved, transcendentals=0),
    )(*ins)


def f32(*shape):
    return jax.ShapeDtypeStruct(shape, F32)


def shifted(block, axis, distance):
    n = lax.axis_size(axis)
    return lax.ppermute(block, axis, [((i - distance) % n, i) for i in range(n)])


def swapped(block, start):
    n, paths = lax.axis_size("gz"), lax.axis_size("path")
    route = []
    for p in range(paths):
        for z in range(n):
            other = z + 1 if (z - start) % 2 == 0 else z - 1
            there = (p, other) if 0 <= other < n else (p ^ 1, z)
            route.append((p * n + z, there[0] * n + there[1]))
    return lax.ppermute(block, ("path", "gz"), route)


def pair_order(ahead, behind):
    even = lax.rem(lax.axis_index("gz"), 2) == 0
    return jnp.where(even, ahead, behind), jnp.where(even, behind, ahead)


def merged(mine, other, far, scale, bit):
    upper = (lax.axis_index("path") & bit) != 0
    low = [jnp.where(upper, o, m) for m, o in zip(mine, other)]
    high = [jnp.where(upper, m, o) for m, o in zip(mine, other)]
    if far is None:
        return [low[0], high[1]] + [a + b for a, b in zip(low[2:], high[2:])]
    low_factor = jnp.where(far, jnp.exp(high[2] * scale), 1.0)
    high_factor = jnp.where(far, 1.0, jnp.exp(low[2] * scale))
    sums = [low_factor * a + high_factor * b for a, b in zip(low[3:], high[3:])]
    return [low[0], high[1], low[2] + high[2]] + sums


def passed(state, other, far, bit):
    mine = lax.axis_index("path")
    ahead = jnp.where(mine & (2 * bit - 1) == bit - 1, other[0], state[0])
    behind = jnp.where(mine & (2 * bit - 1) == bit, other[1], state[1])
    if far is None:
        return [ahead, behind]
    upper = (mine & bit) != 0
    in_way = jnp.where(upper, jnp.where(far, 0.0, other[2]), jnp.where(far, other[2], 0.0))
    return [ahead, behind, state[2] + in_way]


def rows_of(ref):
    return [ref[i] for i in range(ref.shape[0])]


def merge_all(bit, scale, refs, far, kept):
    mine_ref, other_ref, *state_refs = refs
    state = rows_of(state_refs[0]) if state_refs else [jnp.zeros(mine_ref.shape[1:], F32)] * kept
    mine, other = rows_of(mine_ref), rows_of(other_ref)
    return merged(mine, other, far, scale, bit), passed(state, other, far, bit)


def merge_kernel(bit, scale, kept, *refs):
    *refs, out_ref, state_ref = refs
    far = None
    if kept == 3:
        far_ref, *refs = refs
        far = far_ref[3] != 0.0
    packs, state = merge_all(bit, scale, refs, far, kept)
    for ref, values in ((out_ref, packs), (state_ref, state)):
        for i, value in enumerate(values):
            ref[i] = value


def around(block, axis, scale, far=None):
    n = lax.axis_size(axis)
    if n < 2 or n & (n - 1):
        raise ValueError("path size")
    kept = 2 if far is None else 3
    state = []
    bit = 1
    while True:
        other = lax.ppermute(block, axis, [(i, i ^ bit) for i in range(n)])
        if 2 * bit == n:
            return [block, other] + state
        ins = ([] if far is None else [far]) + [block, other] + state
        block, *state = call(
            functools.partial(merge_kernel, bit, scale, kept),
            ins,
            [f32(*block.shape), f32(kept, *block.shape[1:])],
            [VMEM] * len(ins),
        )
        bit *= 2


def split(flat):
    high = flat.astype(jnp.bfloat16)
    return high, (flat - high.astype(F32)).astype(jnp.bfloat16)


def put_rows(parts_ref, e, tiles):
    slices, cells, width = tiles.shape
    at = slice(e * slices * cells, (e + 1) * slices * cells)
    parts_ref[at, 0:width], parts_ref[at, width:] = split(tiles.reshape(slices * cells, width))


def row_sums(parts_ref, sums_ref):
    depth, width = parts_ref.shape[1], sums_ref.shape[1]
    ones = jnp.ones((depth, width), jnp.bfloat16)
    sums_ref[...] = jnp.dot(parts_ref[...], ones, preferred_element_type=F32)


def packed_sums(sums_ref, lane):
    cells, width = lane.shape
    pack = jnp.zeros((cells, width), F32)
    for k in range(sums_ref.shape[0] // cells):
        pack = jnp.where(lane == k, sums_ref[k * cells : (k + 1) * cells], pack)
    return pack


def spread(pack, lane, elems, slices, parts_ref, sums_ref):
    for e in range(elems):
        put_rows(parts_ref, e, jnp.stack([jnp.where(lane == e * slices + z, pack, 0.0) for z in range(slices)]))
    row_sums(parts_ref, sums_ref)


def gather_edges(pack, tile, lane, k):
    width = tile.shape[1]
    here = (lane == k) | (lane == (k - 1) % width)
    return jnp.where(here, pltpu.roll(tile, k, axis=1) if k else tile, pack)


def packed_edges(edges, lane):
    even = lane % 2 == 0
    first = jnp.where(even, edges[0], edges[1])
    return first, pltpu.roll(jnp.where(even, edges[1], edges[0]), 1, axis=1)


def join_edges(first, last, lane):
    width = first.shape[1]
    last = pltpu.roll(last, width - 1, axis=1)
    even = lane % 2 == 0
    return jnp.where(even, first, last), jnp.where(even, last, first)


def edge_columns(pack, rim, k):
    return jnp.where(rim, pltpu.roll(pack, pack.shape[1] - k, axis=1) if k else pack, 0.0)


def reciprocal(value):
    guess = pl.reciprocal(value, approx=True)
    return guess * (2.0 - value * guess)


def beam_sides(cells):
    count, rank = lax.axis_size("beam"), lax.axis_index("beam")
    if count == 2:
        return [
            (
                jnp.where(rank == 0, cells - 1, 0),
                jnp.where(rank == 0, F32(-1.0), F32(1.0)),
                None,
            )
        ]
    return [(cells - 1, F32(-1.0), rank < count - 1), (0, F32(1.0), rank > 0)]


def beam_rows(first, last):
    count, rank = lax.axis_size("beam"), lax.axis_index("beam")
    if count == 2:
        return [jnp.where(rank == 0, last, first)]
    return [last, first]


def face(own, other, sign, there):
    step = (own - other) * sign
    return step if there is None else jnp.where(there, step, 0.0)


def exchange_beam(rows):
    if lax.axis_size("beam") == 2:
        return [lax.ppermute(rows[0], "beam", [(0, 1), (1, 0)])]
    return [shifted(rows[1], "beam", -1), shifted(rows[0], "beam", 1)]


def open_kernel(total, view_ref, source_ref, *refs):
    small, refs = refs[:4], refs[4:]
    maps_ref, inside_ref, coef_ref, *refs = refs
    elems, slices, cells, width = maps_ref.shape
    faces = len(beam_sides(cells))
    face_refs, refs = refs[:faces], refs[faces:]
    beta_ref, kappa_ref, line_ref, side_ref, sems = refs
    half = slices // 2
    parts = [pl.ds(0, half), pl.ds(half, slices - half)] if half else [pl.ds(0, slices)]
    fetch = []
    for i, (ref, kept) in enumerate(zip(small, (beta_ref, kappa_ref, line_ref, side_ref))):
        fetch.append(pltpu.make_async_copy(ref, kept, sems.at[i]))
    large = []
    for i, at in enumerate(parts):
        large.append(pltpu.make_async_copy(source_ref.at[:, at], maps_ref.at[:, at], sems.at[len(small) + i]))
    for copy in large[:1] + fetch + large[1:]:
        copy.start()
    for copy in fetch:
        copy.wait()
    for e in range(elems):
        line = line_ref[e]
        for f in range(elems):
            coef_ref[e * elems + f : e * elems + f + 1] = jnp.full((1, width), kappa_ref[f, line])
        coef_ref[elems * elems + e : elems * elems + e + 1] = jnp.full((1, width), side_ref[e].astype(F32))
    view = view_ref[0, 0]
    beta = [beta_ref[view, e] for e in range(elems)]
    sub = lax.broadcasted_iota(jnp.int32, maps_ref.shape[2:], 0)
    for z in range(slices):
        if z == 0 or z == half:
            large[1 if z else 0].wait()
        tiles = [maps_ref[e, z] for e in range(elems)]
        mu = beta[0] * tiles[0]
        for e in range(1, elems):
            mu = mu + beta[e] * tiles[e]
        run = mu
        reach = 1
        while reach < cells:
            run = run + jnp.where(sub >= reach, pltpu.roll(run, reach, axis=0), 0.0)
            reach *= 2
        inside_ref[z] = jnp.where(sub >= 1, pltpu.roll(run, 1, axis=0), 0.0)
        face_refs[0][elems * slices + z : elems * slices + z + 1] = run[cells - 1 : cells]
        for e in range(elems):
            rows = beam_rows(tiles[e][0:1], tiles[e][cells - 1 : cells])
            for ref, row in zip(face_refs, rows):
                ref[e * slices + z : e * slices + z + 1] = row


def depth_kernel(total, maps_ref, coef_ref, local_ref, pack_ref, mu_ref, parts_ref, sums_ref):
    elems, slices, cells, width = maps_ref.shape
    rows = slices * cells
    row = lax.broadcasted_iota(jnp.int32, (2 * width, 2 * width), 0)
    col = lax.broadcasted_iota(jnp.int32, (2 * width, 2 * width), 1)
    row = jnp.where(row >= width, row - width, row)
    table = jnp.where((row < col) | (col >= width), 1.0, 0.0).astype(jnp.bfloat16)
    for e in range(elems):
        mu = coef_ref[e * elems : e * elems + 1][None] * maps_ref[0]
        for f in range(1, elems):
            mu = mu + coef_ref[e * elems + f : e * elems + f + 1][None] * maps_ref[f]
        mu_ref[e] = mu
        put_rows(parts_ref, e, mu)
    sums_ref[...] = jnp.dot(parts_ref[...], table, preferred_element_type=F32)
    lane = lax.broadcasted_iota(jnp.int32, (cells, width), 1)
    scale = -1.0 / total
    strip = jnp.zeros((cells, width), F32)
    edges = [strip, strip]
    for e in range(elems):
        forward = coef_ref[elems * elems + e : elems * elems + e + 1] == 0.0
        for z in range(slices):
            k = e * slices + z
            before = sums_ref[k * cells : (k + 1) * cells, 0:width]
            whole = sums_ref[k * cells : (k + 1) * cells, width:]
            after = whole - before - mu_ref[e, z]
            local_ref[e, z] = jnp.exp(jnp.where(forward, before, after) * scale)
            strip = jnp.where(lane == k, whole, strip)
            edges[k % 2] = gather_edges(edges[k % 2], maps_ref[e, z], lane, k)
    pack_ref[0], pack_ref[1] = packed_edges(edges, lane)
    pack_ref[2] = strip
    far = jnp.zeros((cells, width), F32)
    for e in range(elems):
        inside = (lane >= e * slices) & (lane < (e + 1) * slices)
        far = jnp.where(inside, coef_ref[elems * elems + e : elems * elems + e + 1][:, 0:1], far)
    pack_ref[3] = far


def weight_kernel(total, skip, maps_ref, inside_ref, carry_ref, local_ref, pack_ref, weight_ref, out_ref, zone_ref,
                  ztwo_ref, proj_ref, whole_ref, sums_ref):
    elems, slices, cells, width = maps_ref.shape
    lane = lax.broadcasted_iota(jnp.int32, (cells, width), 1)
    there = lax.axis_index("beam") > 0
    carry = jnp.where(there, carry_ref[skip : skip + slices], 0.0)
    att = jnp.exp((inside_ref[...] + carry[:, None]) * (-1.0 / total))
    for e in range(elems):
        weight = att * local_ref[e]
        weight_ref[e] = weight
        put_rows(whole_ref, e, weight)
        put_rows(proj_ref, e, weight * maps_ref[e])
    row_sums(proj_ref, sums_ref)
    out_ref[3] = packed_sums(sums_ref, lane)
    row_sums(whole_ref, sums_ref)
    out_ref[4] = packed_sums(sums_ref, lane)
    for i in range(3):
        out_ref[i] = pack_ref[i]
    for e in range(elems):
        zone_ref[e], ztwo_ref[e] = pair_order(maps_ref[e, slices - 1], maps_ref[e, 0])


def dual_step(field, ahead, dual, last):
    step = 0.5 * (ahead - field)
    return jnp.where(last, 0.0, clip(step if dual is None else dual + step))


def tile_duals(tile, dual_x, dual_y, sub, lane, shape):
    cells, width = shape
    new_x = dual_step(tile, pltpu.roll(tile, cells - 1, axis=0), dual_x, sub == cells - 1)
    new_y = dual_step(tile, pltpu.roll(tile, width - 1, axis=1), dual_y, lane == width - 1)
    spread = pltpu.roll(new_x, 1, axis=0) - new_x + (pltpu.roll(new_y, 1, axis=1) - new_y)
    return new_x, new_y, spread


def join(ref, width):
    elems, cells, slices = ref.shape
    parts = [ref[e] for e in range(elems)]
    if elems * slices < width:
        parts.append(jnp.zeros((cells, width - elems * slices), F32))
    return jnp.concatenate(parts, axis=1)


def first_dual_kernel(maps_ref, measured_ref, *refs):
    elems, slices, cells, width = maps_ref.shape
    sides = beam_sides(cells)
    own_refs, refs = refs[: len(sides)], refs[len(sides) :]
    other_refs, refs = refs[: len(sides)], refs[len(sides) :]
    dual_z_ref, dual_x_ref, dual_y_ref, adj_ref, still_ref, *edge_refs = refs
    sub = lax.broadcasted_iota(jnp.int32, (cells, width), 0)
    lane = lax.broadcasted_iota(jnp.int32, (cells, width), 1)
    still_ref[...] = join(measured_ref, width)
    for (row, sign, there), own, other, edge in zip(sides, own_refs, other_refs, edge_refs):
        rows = pl.ds(0, elems * slices)
        edge[...] = clip(0.5 * face(own[rows], other[rows], sign, there))
    def step(z, behind):
        at_end = z == slices - 1
        duals = []
        for e in range(elems):
            tile = maps_ref[e, z]
            ahead = maps_ref[e, jnp.minimum(z + 1, slices - 1)]
            dual_z = jnp.where(at_end, 0.0, clip(0.5 * (ahead - tile)))
            dual_x, dual_y, spread = tile_duals(tile, None, None, sub, lane, (cells, width))
            dual_z_ref[e, z] = dual_z
            dual_x_ref[e, z] = dual_x
            dual_y_ref[e, z] = dual_y
            spread = spread + (behind[e] - dual_z)
            for (row, sign, there), edge in zip(sides, edge_refs):
                spread = spread + jnp.where(sub == row, sign * edge[pl.ds(e * slices + z, 1)], 0.0)
            adj_ref[e, z] = spread
            duals.append(dual_z)
        return tuple(duals)

    zero = jnp.zeros((cells, width), F32)
    lax.fori_loop(0, slices, step, (zero,) * elems, unroll=UNROLL)


def part(ref, pack):
    slices = ref.shape[2]
    for e in range(ref.shape[0]):
        ref[e] = pack[:, e * slices : (e + 1) * slices]


def first_update_kernel(total, size, maps_ref, weight_ref, adj_ref, still_ref, far_ref, pack_ref, zone_ref, ztwo_ref,
                        *refs):
    elems, slices, cells, width = maps_ref.shape
    pack_refs, refs = refs[:-12], refs[-12:]
    pull_ref, tau_ref, cur_ref, ext_ref, dd_ref, yedge_ref, zdual_ref, out_ref, emission_ref, *refs = refs
    parts_ref, own_ref, dual_ref = refs
    count, rank = lax.axis_size("gz"), lax.axis_index("gz")
    mine = lax.axis_index("path")
    pack_shape = (cells, width)
    lane = lax.broadcasted_iota(jnp.int32, pack_shape, 1)
    rim = (lane == 0) | (lane == width - 1)
    packs, state = merge_all(size // 2, -1.0 / total, pack_refs, far_ref[3] != 0.0, 3)
    image, weights = packs[3], packs[4]
    ahead, behind, base = state
    own = jnp.exp(base * (-1.0 / total))
    sig = 1.0 / weights
    data_dual = sig * (image - still_ref[...]) / (1.0 + sig)
    dd_ref[0] = data_dual
    dd_ref[1] = sig
    part(emission_ref, image * (1.0 / total))
    y_ahead = jnp.where(mine < size - 1, clip(0.5 * (ahead - pack_ref[1])), 0.0)
    y_behind = jnp.where(mine > 0, clip(0.5 * (pack_ref[0] - behind)), 0.0)
    joined = join_edges(y_behind, -y_ahead, lane)
    yedge_ref[0] = y_ahead
    yedge_ref[1] = y_behind

    spread(own, lane, elems, slices, parts_ref, own_ref)
    spread(data_dual, lane, elems, slices, parts_ref, dual_ref)
    edges = [jnp.zeros(pack_shape, F32)] * 2
    for e in range(elems):
        ahead, behind = pair_order(zone_ref[e], ztwo_ref[e])
        behind = jnp.where(rank > 0, clip(0.5 * (maps_ref[e, 0] - behind)), 0.0)
        ahead = jnp.where(rank < count - 1, clip(0.5 * (ahead - maps_ref[e, slices - 1])), 0.0)
        zdual_ref[0, e] = behind
        zdual_ref[1, e] = ahead
        rows = []
        for z in range(slices):
            k = e * slices + z
            at = slice(k * cells, (k + 1) * cells)
            tile = maps_ref[e, z]
            weight = weight_ref[e, z] * own_ref[at]
            tau = reciprocal(weight + 6.0)
            step = weight * dual_ref[at] + adj_ref[e, z] + edge_columns(joined[k % 2], rim, k)
            if z == 0:
                step = step + behind
            if z == slices - 1:
                step = step - ahead
            new = jnp.maximum(tile - step * tau, 0.0)
            ext = 2.0 * new - tile
            tau_ref[e, z] = tau
            pull_ref[e, z] = tau * weight
            cur_ref[e, z] = new
            ext_ref[e, z] = ext
            rows.append(weight * ext)
            edges[k % 2] = gather_edges(edges[k % 2], ext, lane, k)
        put_rows(parts_ref, e, jnp.stack(rows))
    out_ref[0], out_ref[1] = packed_edges(edges, lane)
    row_sums(parts_ref, own_ref)
    out_ref[2] = packed_sums(own_ref, lane)
    for i in range(3, out_ref.shape[0]):
        out_ref[i] = jnp.zeros(pack_shape, F32)


def face_kernel(ext_ref, zone_ref, ztwo_ref, *face_refs):
    elems, slices, cells, _ = ext_ref.shape
    for e in range(elems):
        for z in range(slices):
            rows = beam_rows(ext_ref[e, z, 0:1], ext_ref[e, z, cells - 1 : cells])
            for ref, row in zip(face_refs, rows):
                ref[e * slices + z : e * slices + z + 1] = row
        zone_ref[e], ztwo_ref[e] = pair_order(ext_ref[e, slices - 1], ext_ref[e, 0])


def second_dual_kernel(ext_ref, dual_z_ref, dual_x_ref, dual_y_ref, adj_ref):
    elems, slices, cells, width = ext_ref.shape
    sub = lax.broadcasted_iota(jnp.int32, (cells, width), 0)
    lane = lax.broadcasted_iota(jnp.int32, (cells, width), 1)

    def step(z, behind):
        at_end = z == slices - 1
        duals = []
        for e in range(elems):
            tile = ext_ref[e, z]
            ahead = ext_ref[e, jnp.minimum(z + 1, slices - 1)]
            dual_z = jnp.where(at_end, 0.0, clip(dual_z_ref[e, z] + 0.5 * (ahead - tile)))
            _, _, spread = tile_duals(tile, dual_x_ref[e, z], dual_y_ref[e, z], sub, lane, (cells, width))
            adj_ref[e, z] = spread + (behind[e] - dual_z)
            duals.append(dual_z)
        return tuple(duals)

    zero = jnp.zeros((cells, width), F32)
    lax.fori_loop(0, slices, step, (zero,) * elems, unroll=UNROLL)


def second_face_kernel(cur_ref, ext_ref, tau_ref, adj_ref, zdual_ref, zone_ref, ztwo_ref, *refs):
    elems, slices, cells, width = cur_ref.shape
    sides = beam_sides(cells)
    edge_refs, refs = refs[: len(sides)], refs[len(sides) :]
    own_refs, refs = refs[: len(sides)], refs[len(sides) :]
    other_refs, refs = refs[: len(sides)], refs[len(sides) :]
    base_ref, *face_refs = refs
    count, rank = lax.axis_size("gz"), lax.axis_index("gz")
    sub = lax.broadcasted_iota(jnp.int32, (cells, width), 0)
    for (row, sign, there), edge, own, other, out in zip(sides, edge_refs, own_refs, other_refs, face_refs):
        out[...] = clip(edge[...] + 0.5 * face(own[...], other[...], sign, there)) * sign
    for e in range(elems):
        ahead, behind = pair_order(zone_ref[e], ztwo_ref[e])
        behind = jnp.where(rank > 0, clip(zdual_ref[0, e] + 0.5 * (ext_ref[e, 0] - behind)), 0.0)
        ahead = clip(zdual_ref[1, e] + 0.5 * (ahead - ext_ref[e, slices - 1]))
        ahead = jnp.where(rank < count - 1, ahead, 0.0)
        for z in range(slices):
            k = e * slices + z
            adj = adj_ref[e, z]
            if z == 0:
                adj = adj + behind
            if z == slices - 1:
                adj = adj - ahead
            for (row, sign, there), out in zip(sides, face_refs):
                adj = adj + jnp.where(sub == row, out[k : k + 1], 0.0)
            base_ref[e, z] = cur_ref[e, z] - tau_ref[e, z] * adj


def last_update_kernel(size, base_ref, pull_ref, tau_ref, still_ref, dd_ref, yedge_ref, own_pack_ref, *refs):
    elems, slices, cells, width = base_ref.shape
    *pack_refs, new_ref, dual_ref, parts_ref, sums_ref = refs
    mine = lax.axis_index("path")
    packs, (ahead, behind) = merge_all(size // 2, None, pack_refs, None, 2)
    image = packs[2]
    sig = dd_ref[1]
    data_dual = (dd_ref[0] + sig * (image - still_ref[...])) / (1.0 + sig)
    part(dual_ref, data_dual)
    y_ahead = jnp.where(mine < size - 1, clip(yedge_ref[0] + 0.5 * (ahead - own_pack_ref[1])), 0.0)
    y_behind = jnp.where(mine > 0, clip(yedge_ref[1] + 0.5 * (own_pack_ref[0] - behind)), 0.0)
    lane = lax.broadcasted_iota(jnp.int32, (cells, width), 1)
    rim = (lane == 0) | (lane == width - 1)
    joined = join_edges(y_behind, -y_ahead, lane)

    spread(data_dual, lane, elems, slices, parts_ref, sums_ref)
    for e in range(elems):
        for z in range(slices):
            k = e * slices + z
            new = base_ref[e, z] - pull_ref[e, z] * sums_ref[k * cells : (k + 1) * cells]
            new = new - tau_ref[e, z] * edge_columns(joined[k % 2], rim, k)
            new_ref[e, z] = jnp.maximum(new, 0.0)


def shards(maps, measured, beta_table, view, kappa, line_of, side):
    elems, slices, cells, width = maps.shape
    total_x = cells * lax.axis_size("beam")
    total_y = width * lax.axis_size("path")
    size = lax.axis_size("path")
    block = f32(elems, slices, cells, width)
    plane = f32(elems, cells, width)
    rows = f32(elems * slices, width)
    faces = len(beam_sides(cells))
    measured = measured.transpose(0, 2, 1)
    kappa = kappa.T
    view = view.reshape(1, 1)

    tall = f32((elems + 1) * slices, width)
    parts = pltpu.VMEM((elems * slices * cells, 2 * width), jnp.bfloat16)
    sums = pltpu.VMEM((elems * slices * cells, width), F32)
    maps, inside, coef, *own = call(
        functools.partial(open_kernel, total_x),
        [view] + [pltpu.with_memory_space_constraint(a, pltpu.HBM) for a in (maps, beta_table, kappa, line_of, side)],
        [block, f32(slices, cells, width), f32(elems * elems + elems, width), tall] + [rows] * (faces - 1),
        [SMEM] + [pltpu.HBM] * 5,
        [
            pltpu.SMEM(beta_table.shape, F32),
            pltpu.SMEM(kappa.shape, F32),
            pltpu.SMEM(line_of.shape, jnp.int32),
            pltpu.SMEM(side.shape, jnp.int32),
            pltpu.SemaphoreType.DMA((6,)),
        ],
    )
    other = exchange_beam(own)
    carry, skip = other[-1], elems * slices
    beams = lax.axis_size("beam")
    if beams > 2:
        carry, skip = carry[skip:], 0
        reach = 1
        while reach < beams - 1:
            far = lax.axis_index("beam") > reach
            carry = carry + jnp.where(far, shifted(carry, "beam", reach), 0.0)
            reach *= 2
    local, still = call(
        functools.partial(depth_kernel, total_y),
        [maps, coef],
        [block, f32(4, cells, width)],
        [VMEM] * 2,
        [
            pltpu.VMEM(maps.shape, F32),
            parts,
            pltpu.VMEM((elems * slices * cells, 2 * width), F32),
        ],
    )
    weight, pack, zone, ztwo = call(
        functools.partial(weight_kernel, total_x, skip),
        [maps, inside, carry, local, still],
        [block, f32(5, cells, width), plane, plane],
        [VMEM] * 5,
        [parts, parts, sums],
    )
    packs = around(pack, "path", -1.0 / total_y, still)
    zone, ztwo = swapped(zone, 0), swapped(ztwo, 1)
    dual_z, dual_x, dual_y, adj, counts, *edge = call(
        first_dual_kernel,
        [maps, measured, *own, *other],
        [block, block, block, block, f32(cells, width)] + [rows] * faces,
        [VMEM] * (2 + 2 * faces),
    )
    pull, tau, current, extrap, dd, yedge, zdual, pack, emission = call(
        functools.partial(first_update_kernel, total_y, size),
        [maps, weight, adj, counts, still, pack, zone, ztwo, *packs],
        [block, block, block, block, f32(2, cells, width), f32(2, cells, width), f32(2, elems, cells, width),
         f32(5, cells, width), f32(elems, cells, slices)],
        [VMEM] * (8 + len(packs)),
        [parts, sums, sums],
    )
    packs = around(pack, "path", None)
    zone, ztwo, *own = call(face_kernel, [extrap], [plane, plane] + [rows] * faces, [VMEM])
    zone, ztwo = swapped(zone, 0), swapped(ztwo, 1)
    other = exchange_beam(own)
    (adj,) = call(second_dual_kernel, [extrap, dual_z, dual_x, dual_y], [block], [VMEM] * 4)
    (base,) = call(
        second_face_kernel,
        [current, extrap, tau, adj, zdual, zone, ztwo, *edge, *own, *other],
        [block],
        [VMEM] * (7 + 3 * faces),
        [pltpu.VMEM((elems * slices, width), F32)] * faces,
    )
    current, data_dual = call(
        functools.partial(last_update_kernel, size),
        [base, pull, tau, counts, dd, yedge, pack, *packs],
        [block, f32(elems, cells, slices)],
        [VMEM] * (7 + len(packs)),
        [parts, sums],
    )
    return emission.transpose(0, 2, 1), current, data_dual.transpose(0, 2, 1)


def solution(mesh):
    return jax.shard_map(
        shards,
        mesh=mesh,
        in_specs=(P(None, "gz", "beam", "path"), P(None, "gz", "beam"), P(), P(), P(), P(), P()),
        out_specs=(P(None, "gz", "beam"), P(None, "gz", "beam", "path"), P(None, "gz", "beam")),
        check_vma=False,
    )
```

```python
import functools

import jax
import jax.numpy as jnp
from jax import lax
from jax.experimental import pallas as pl
from jax.experimental.pallas import tpu as pltpu
from jax.sharding import PartitionSpec as P

ITERS = 2
LAM = 0.1
F32 = jnp.float32
VMEM = pltpu.VMEM
SMEM = pltpu.SMEM
UNROLL = 4
PARTS = 4
VMEM_LIMIT = 32 * 1024 * 1024


def clip(value):
    return jnp.clip(value, -LAM, LAM)


def call(body, ins, outs, spaces, scratch=(), flops=1_000_000):
    specs = [pl.BlockSpec(memory_space=space) for space in spaces]
    moved = sum(a.size * 4 for a in ins) + sum(o.size * 4 for o in outs)
    return pl.pallas_call(
        body,
        out_shape=outs,
        in_specs=specs,
        out_specs=[pl.BlockSpec(memory_space=VMEM)] * len(outs),
        scratch_shapes=list(scratch),
        compiler_params=pltpu.CompilerParams(vmem_limit_bytes=VMEM_LIMIT),
        cost_estimate=pl.CostEstimate(flops=flops, bytes_accessed=moved, transcendentals=0),
    )(*ins)


def f32(*shape):
    return jax.ShapeDtypeStruct(shape, F32)


def shifted(block, axis, distance):
    n = lax.axis_size(axis)
    return lax.ppermute(block, axis, [((i - distance) % n, i) for i in range(n)])


def swapped(block, start):
    n, paths = lax.axis_size("gz"), lax.axis_size("path")
    route = []
    for p in range(paths):
        for z in range(n):
            other = z + 1 if (z - start) % 2 == 0 else z - 1
            there = (p, other) if 0 <= other < n else (p ^ 1, z)
            route.append((p * n + z, there[0] * n + there[1]))
    return lax.ppermute(block, ("path", "gz"), route)


def pair_order(ahead, behind):
    even = lax.rem(lax.axis_index("gz"), 2) == 0
    return jnp.where(even, ahead, behind), jnp.where(even, behind, ahead)


def merged(mine, other, far, scale, bit):
    upper = (lax.axis_index("path") & bit) != 0
    low = [jnp.where(upper, o, m) for m, o in zip(mine, other)]
    high = [jnp.where(upper, m, o) for m, o in zip(mine, other)]
    if far is None:
        return [low[0], high[1]] + [a + b for a, b in zip(low[2:], high[2:])]
    low_factor = jnp.where(far, jnp.exp(high[2] * scale), 1.0)
    high_factor = jnp.where(far, 1.0, jnp.exp(low[2] * scale))
    sums = [low_factor * a + high_factor * b for a, b in zip(low[3:], high[3:])]
    return [low[0], high[1], low[2] + high[2]] + sums


def passed(state, other, far, bit):
    mine = lax.axis_index("path")
    ahead = jnp.where(mine & (2 * bit - 1) == bit - 1, other[0], state[0])
    behind = jnp.where(mine & (2 * bit - 1) == bit, other[1], state[1])
    if far is None:
        return [ahead, behind]
    upper = (mine & bit) != 0
    in_way = jnp.where(upper, jnp.where(far, 0.0, other[2]), jnp.where(far, other[2], 0.0))
    return [ahead, behind, state[2] + in_way]


def rows_of(ref):
    return [ref[i] for i in range(ref.shape[0])]


def merge_all(bit, scale, refs, far, kept):
    mine_ref, other_ref, *state_refs = refs
    state = rows_of(state_refs[0]) if state_refs else [jnp.zeros(mine_ref.shape[1:], F32)] * kept
    mine, other = rows_of(mine_ref), rows_of(other_ref)
    return merged(mine, other, far, scale, bit), passed(state, other, far, bit)


def merge_kernel(bit, scale, kept, *refs):
    *refs, out_ref, state_ref = refs
    far = None
    if kept == 3:
        far_ref, *refs = refs
        far = far_ref[3] != 0.0
    packs, state = merge_all(bit, scale, refs, far, kept)
    for ref, values in ((out_ref, packs), (state_ref, state)):
        for i, value in enumerate(values):
            ref[i] = value


def around(block, axis, scale, far=None):
    n = lax.axis_size(axis)
    if n < 2 or n & (n - 1):
        raise ValueError("path size")
    kept = 2 if far is None else 3
    state = []
    bit = 1
    while True:
        other = lax.ppermute(block, axis, [(i, i ^ bit) for i in range(n)])
        if 2 * bit == n:
            return [block, other] + state
        ins = ([] if far is None else [far]) + [block, other] + state
        block, *state = call(
            functools.partial(merge_kernel, bit, scale, kept),
            ins,
            [f32(*block.shape), f32(kept, *block.shape[1:])],
            [VMEM] * len(ins),
        )
        bit *= 2


def split(flat):
    high = flat.astype(jnp.bfloat16)
    return high, (flat - high.astype(F32)).astype(jnp.bfloat16)


def put_rows(parts_ref, e, tiles):
    slices, cells, width = tiles.shape
    at = slice(e * slices * cells, (e + 1) * slices * cells)
    parts_ref[at, 0:width], parts_ref[at, width:] = split(tiles.reshape(slices * cells, width))


def row_sums(parts_ref, sums_ref):
    depth, width = parts_ref.shape[1], sums_ref.shape[1]
    ones = jnp.ones((depth, width), jnp.bfloat16)
    sums_ref[...] = jnp.dot(parts_ref[...], ones, preferred_element_type=F32)


def packed_sums(sums_ref, lane):
    cells, width = lane.shape
    pack = jnp.zeros((cells, width), F32)
    for k in range(sums_ref.shape[0] // cells):
        pack = jnp.where(lane == k, sums_ref[k * cells : (k + 1) * cells], pack)
    return pack


def spread(pack, lane, elems, slices, parts_ref, sums_ref):
    for e in range(elems):
        put_rows(parts_ref, e, jnp.stack([jnp.where(lane == e * slices + z, pack, 0.0) for z in range(slices)]))
    row_sums(parts_ref, sums_ref)


def gather_edges(pack, tile, lane, k):
    width = tile.shape[1]
    here = (lane == k) | (lane == (k - 1) % width)
    return jnp.where(here, pltpu.roll(tile, k, axis=1) if k else tile, pack)


def packed_edges(edges, lane):
    even = lane % 2 == 0
    first = jnp.where(even, edges[0], edges[1])
    return first, pltpu.roll(jnp.where(even, edges[1], edges[0]), 1, axis=1)


def join_edges(first, last, lane):
    width = first.shape[1]
    last = pltpu.roll(last, width - 1, axis=1)
    even = lane % 2 == 0
    return jnp.where(even, first, last), jnp.where(even, last, first)


def edge_columns(pack, rim, k):
    return jnp.where(rim, pltpu.roll(pack, pack.shape[1] - k, axis=1) if k else pack, 0.0)


def reciprocal(value):
    guess = pl.reciprocal(value, approx=True)
    return guess * (2.0 - value * guess)


def beam_sides(cells):
    count, rank = lax.axis_size("beam"), lax.axis_index("beam")
    if count == 2:
        return [
            (
                jnp.where(rank == 0, cells - 1, 0),
                jnp.where(rank == 0, F32(-1.0), F32(1.0)),
                None,
            )
        ]
    return [(cells - 1, F32(-1.0), rank < count - 1), (0, F32(1.0), rank > 0)]


def beam_rows(first, last):
    count, rank = lax.axis_size("beam"), lax.axis_index("beam")
    if count == 2:
        return [jnp.where(rank == 0, last, first)]
    return [last, first]


def face(own, other, sign, there):
    step = (own - other) * sign
    return step if there is None else jnp.where(there, step, 0.0)


def exchange_beam(rows):
    if lax.axis_size("beam") == 2:
        return [lax.ppermute(rows[0], "beam", [(0, 1), (1, 0)])]
    return [shifted(rows[1], "beam", -1), shifted(rows[0], "beam", 1)]


def open_kernel(total, view_ref, source_ref, *refs):
    small, refs = refs[:4], refs[4:]
    maps_ref, inside_ref, coef_ref, *refs = refs
    elems, slices, cells, width = maps_ref.shape
    faces = len(beam_sides(cells))
    face_refs, refs = refs[:faces], refs[faces:]
    beta_ref, kappa_ref, line_ref, side_ref, sems = refs
    piece = slices // PARTS if slices % PARTS == 0 else slices
    parts = [pl.ds(z, piece) for z in range(0, slices, piece)]
    fetch = []
    for i, (ref, kept) in enumerate(zip(small, (beta_ref, kappa_ref, line_ref, side_ref))):
        fetch.append(pltpu.make_async_copy(ref, kept, sems.at[i]))
    large = []
    for i, at in enumerate(parts):
        large.append(pltpu.make_async_copy(source_ref.at[:, at], maps_ref.at[:, at], sems.at[len(small) + i]))
    for copy in large[:1] + fetch + large[1:]:
        copy.start()
    for copy in fetch:
        copy.wait()
    for e in range(elems):
        line = line_ref[e]
        for f in range(elems):
            coef_ref[e * elems + f : e * elems + f + 1] = jnp.full((1, width), kappa_ref[f, line])
        coef_ref[elems * elems + e : elems * elems + e + 1] = jnp.full((1, width), side_ref[e].astype(F32))
    view = view_ref[0, 0]
    beta = [beta_ref[view, e] for e in range(elems)]
    sub = lax.broadcasted_iota(jnp.int32, maps_ref.shape[2:], 0)
    for z in range(slices):
        if z % piece == 0:
            large[z // piece].wait()
        tiles = [maps_ref[e, z] for e in range(elems)]
        mu = beta[0] * tiles[0]
        for e in range(1, elems):
            mu = mu + beta[e] * tiles[e]
        run = mu
        reach = 1
        while reach < cells:
            run = run + jnp.where(sub >= reach, pltpu.roll(run, reach, axis=0), 0.0)
            reach *= 2
        inside_ref[z] = jnp.where(sub >= 1, pltpu.roll(run, 1, axis=0), 0.0)
        face_refs[0][elems * slices + z : elems * slices + z + 1] = run[cells - 1 : cells]
        for e in range(elems):
            rows = beam_rows(tiles[e][0:1], tiles[e][cells - 1 : cells])
            for ref, row in zip(face_refs, rows):
                ref[e * slices + z : e * slices + z + 1] = row


def depth_kernel(total, maps_ref, coef_ref, local_ref, pack_ref, mu_ref, parts_ref, sums_ref):
    elems, slices, cells, width = maps_ref.shape
    rows = slices * cells
    row = lax.broadcasted_iota(jnp.int32, (2 * width, 2 * width), 0)
    col = lax.broadcasted_iota(jnp.int32, (2 * width, 2 * width), 1)
    row = jnp.where(row >= width, row - width, row)
    table = jnp.where((row < col) | (col >= width), 1.0, 0.0).astype(jnp.bfloat16)
    for e in range(elems):
        mu = coef_ref[e * elems : e * elems + 1][None] * maps_ref[0]
        for f in range(1, elems):
            mu = mu + coef_ref[e * elems + f : e * elems + f + 1][None] * maps_ref[f]
        mu_ref[e] = mu
        put_rows(parts_ref, e, mu)
    sums_ref[...] = jnp.dot(parts_ref[...], table, preferred_element_type=F32)
    lane = lax.broadcasted_iota(jnp.int32, (cells, width), 1)
    scale = -1.0 / total
    strip = jnp.zeros((cells, width), F32)
    edges = [strip, strip]
    for e in range(elems):
        forward = coef_ref[elems * elems + e : elems * elems + e + 1] == 0.0
        for z in range(slices):
            k = e * slices + z
            before = sums_ref[k * cells : (k + 1) * cells, 0:width]
            whole = sums_ref[k * cells : (k + 1) * cells, width:]
            after = whole - before - mu_ref[e, z]
            local_ref[e, z] = jnp.exp(jnp.where(forward, before, after) * scale)
            strip = jnp.where(lane == k, whole, strip)
            edges[k % 2] = gather_edges(edges[k % 2], maps_ref[e, z], lane, k)
    pack_ref[0], pack_ref[1] = packed_edges(edges, lane)
    pack_ref[2] = strip
    far = jnp.zeros((cells, width), F32)
    for e in range(elems):
        inside = (lane >= e * slices) & (lane < (e + 1) * slices)
        far = jnp.where(inside, coef_ref[elems * elems + e : elems * elems + e + 1][:, 0:1], far)
    pack_ref[3] = far


def weight_kernel(total, skip, maps_ref, inside_ref, carry_ref, local_ref, pack_ref, weight_ref, out_ref, zone_ref,
                  ztwo_ref, proj_ref, whole_ref, sums_ref):
    elems, slices, cells, width = maps_ref.shape
    lane = lax.broadcasted_iota(jnp.int32, (cells, width), 1)
    there = lax.axis_index("beam") > 0
    carry = jnp.where(there, carry_ref[skip : skip + slices], 0.0)
    att = jnp.exp((inside_ref[...] + carry[:, None]) * (-1.0 / total))
    for e in range(elems):
        weight = att * local_ref[e]
        weight_ref[e] = weight
        put_rows(whole_ref, e, weight)
        put_rows(proj_ref, e, weight * maps_ref[e])
    row_sums(proj_ref, sums_ref)
    out_ref[3] = packed_sums(sums_ref, lane)
    row_sums(whole_ref, sums_ref)
    out_ref[4] = packed_sums(sums_ref, lane)
    for i in range(3):
        out_ref[i] = pack_ref[i]
    for e in range(elems):
        zone_ref[e], ztwo_ref[e] = pair_order(maps_ref[e, slices - 1], maps_ref[e, 0])


def dual_step(field, ahead, dual, last):
    step = 0.5 * (ahead - field)
    return jnp.where(last, 0.0, clip(step if dual is None else dual + step))


def tile_duals(tile, dual_x, dual_y, sub, lane, shape):
    cells, width = shape
    new_x = dual_step(tile, pltpu.roll(tile, cells - 1, axis=0), dual_x, sub == cells - 1)
    new_y = dual_step(tile, pltpu.roll(tile, width - 1, axis=1), dual_y, lane == width - 1)
    spread = pltpu.roll(new_x, 1, axis=0) - new_x + (pltpu.roll(new_y, 1, axis=1) - new_y)
    return new_x, new_y, spread


def join(ref, width):
    elems, cells, slices = ref.shape
    parts = [ref[e] for e in range(elems)]
    if elems * slices < width:
        parts.append(jnp.zeros((cells, width - elems * slices), F32))
    return jnp.concatenate(parts, axis=1)


def first_dual_kernel(maps_ref, measured_ref, *refs):
    elems, slices, cells, width = maps_ref.shape
    sides = beam_sides(cells)
    own_refs, refs = refs[: len(sides)], refs[len(sides) :]
    other_refs, refs = refs[: len(sides)], refs[len(sides) :]
    dual_z_ref, dual_x_ref, dual_y_ref, adj_ref, still_ref, *edge_refs = refs
    sub = lax.broadcasted_iota(jnp.int32, (cells, width), 0)
    lane = lax.broadcasted_iota(jnp.int32, (cells, width), 1)
    still_ref[...] = join(measured_ref, width)
    for (row, sign, there), own, other, edge in zip(sides, own_refs, other_refs, edge_refs):
        rows = pl.ds(0, elems * slices)
        edge[...] = clip(0.5 * face(own[rows], other[rows], sign, there))
    def step(z, behind):
        at_end = z == slices - 1
        duals = []
        for e in range(elems):
            tile = maps_ref[e, z]
            ahead = maps_ref[e, jnp.minimum(z + 1, slices - 1)]
            dual_z = jnp.where(at_end, 0.0, clip(0.5 * (ahead - tile)))
            dual_x, dual_y, spread = tile_duals(tile, None, None, sub, lane, (cells, width))
            dual_z_ref[e, z] = dual_z
            dual_x_ref[e, z] = dual_x
            dual_y_ref[e, z] = dual_y
            spread = spread + (behind[e] - dual_z)
            for (row, sign, there), edge in zip(sides, edge_refs):
                spread = spread + jnp.where(sub == row, sign * edge[pl.ds(e * slices + z, 1)], 0.0)
            adj_ref[e, z] = spread
            duals.append(dual_z)
        return tuple(duals)

    zero = jnp.zeros((cells, width), F32)
    lax.fori_loop(0, slices, step, (zero,) * elems, unroll=UNROLL)


def part(ref, pack):
    slices = ref.shape[2]
    for e in range(ref.shape[0]):
        ref[e] = pack[:, e * slices : (e + 1) * slices]


def first_update_kernel(total, size, maps_ref, weight_ref, adj_ref, still_ref, far_ref, pack_ref, zone_ref, ztwo_ref,
                        *refs):
    elems, slices, cells, width = maps_ref.shape
    pack_refs, refs = refs[:-12], refs[-12:]
    pull_ref, tau_ref, cur_ref, ext_ref, dd_ref, yedge_ref, zdual_ref, out_ref, emission_ref, *refs = refs
    parts_ref, own_ref, dual_ref = refs
    count, rank = lax.axis_size("gz"), lax.axis_index("gz")
    mine = lax.axis_index("path")
    pack_shape = (cells, width)
    lane = lax.broadcasted_iota(jnp.int32, pack_shape, 1)
    rim = (lane == 0) | (lane == width - 1)
    packs, state = merge_all(size // 2, -1.0 / total, pack_refs, far_ref[3] != 0.0, 3)
    image, weights = packs[3], packs[4]
    ahead, behind, base = state
    own = jnp.exp(base * (-1.0 / total))
    sig = 1.0 / weights
    data_dual = sig * (image - still_ref[...]) / (1.0 + sig)
    dd_ref[0] = data_dual
    dd_ref[1] = sig
    part(emission_ref, image * (1.0 / total))
    y_ahead = jnp.where(mine < size - 1, clip(0.5 * (ahead - pack_ref[1])), 0.0)
    y_behind = jnp.where(mine > 0, clip(0.5 * (pack_ref[0] - behind)), 0.0)
    joined = join_edges(y_behind, -y_ahead, lane)
    yedge_ref[0] = y_ahead
    yedge_ref[1] = y_behind

    spread(own, lane, elems, slices, parts_ref, own_ref)
    spread(data_dual, lane, elems, slices, parts_ref, dual_ref)
    edges = [jnp.zeros(pack_shape, F32)] * 2
    for e in range(elems):
        ahead, behind = pair_order(zone_ref[e], ztwo_ref[e])
        behind = jnp.where(rank > 0, clip(0.5 * (maps_ref[e, 0] - behind)), 0.0)
        ahead = jnp.where(rank < count - 1, clip(0.5 * (ahead - maps_ref[e, slices - 1])), 0.0)
        zdual_ref[0, e] = behind
        zdual_ref[1, e] = ahead
        rows = []
        for z in range(slices):
            k = e * slices + z
            at = slice(k * cells, (k + 1) * cells)
            tile = maps_ref[e, z]
            weight = weight_ref[e, z] * own_ref[at]
            tau = reciprocal(weight + 6.0)
            step = weight * dual_ref[at] + adj_ref[e, z] + edge_columns(joined[k % 2], rim, k)
            if z == 0:
                step = step + behind
            if z == slices - 1:
                step = step - ahead
            new = jnp.maximum(tile - step * tau, 0.0)
            ext = 2.0 * new - tile
            tau_ref[e, z] = tau
            pull_ref[e, z] = tau * weight
            cur_ref[e, z] = new
            ext_ref[e, z] = ext
            rows.append(weight * ext)
            edges[k % 2] = gather_edges(edges[k % 2], ext, lane, k)
        put_rows(parts_ref, e, jnp.stack(rows))
    out_ref[0], out_ref[1] = packed_edges(edges, lane)
    row_sums(parts_ref, own_ref)
    out_ref[2] = packed_sums(own_ref, lane)
    for i in range(3, out_ref.shape[0]):
        out_ref[i] = jnp.zeros(pack_shape, F32)


def face_kernel(ext_ref, zone_ref, ztwo_ref, *face_refs):
    elems, slices, cells, _ = ext_ref.shape
    for e in range(elems):
        for z in range(slices):
            rows = beam_rows(ext_ref[e, z, 0:1], ext_ref[e, z, cells - 1 : cells])
            for ref, row in zip(face_refs, rows):
                ref[e * slices + z : e * slices + z + 1] = row
        zone_ref[e], ztwo_ref[e] = pair_order(ext_ref[e, slices - 1], ext_ref[e, 0])


def second_dual_kernel(ext_ref, dual_z_ref, dual_x_ref, dual_y_ref, adj_ref):
    elems, slices, cells, width = ext_ref.shape
    sub = lax.broadcasted_iota(jnp.int32, (cells, width), 0)
    lane = lax.broadcasted_iota(jnp.int32, (cells, width), 1)

    def step(z, behind):
        at_end = z == slices - 1
        duals = []
        for e in range(elems):
            tile = ext_ref[e, z]
            ahead = ext_ref[e, jnp.minimum(z + 1, slices - 1)]
            dual_z = jnp.where(at_end, 0.0, clip(dual_z_ref[e, z] + 0.5 * (ahead - tile)))
            _, _, spread = tile_duals(tile, dual_x_ref[e, z], dual_y_ref[e, z], sub, lane, (cells, width))
            adj_ref[e, z] = spread + (behind[e] - dual_z)
            duals.append(dual_z)
        return tuple(duals)

    zero = jnp.zeros((cells, width), F32)
    lax.fori_loop(0, slices, step, (zero,) * elems, unroll=UNROLL)


def second_face_kernel(cur_ref, ext_ref, tau_ref, adj_ref, zdual_ref, zone_ref, ztwo_ref, *refs):
    elems, slices, cells, width = cur_ref.shape
    sides = beam_sides(cells)
    edge_refs, refs = refs[: len(sides)], refs[len(sides) :]
    own_refs, refs = refs[: len(sides)], refs[len(sides) :]
    other_refs, refs = refs[: len(sides)], refs[len(sides) :]
    base_ref, *face_refs = refs
    count, rank = lax.axis_size("gz"), lax.axis_index("gz")
    sub = lax.broadcasted_iota(jnp.int32, (cells, width), 0)
    for (row, sign, there), edge, own, other, out in zip(sides, edge_refs, own_refs, other_refs, face_refs):
        out[...] = clip(edge[...] + 0.5 * face(own[...], other[...], sign, there)) * sign
    for e in range(elems):
        ahead, behind = pair_order(zone_ref[e], ztwo_ref[e])
        behind = jnp.where(rank > 0, clip(zdual_ref[0, e] + 0.5 * (ext_ref[e, 0] - behind)), 0.0)
        ahead = clip(zdual_ref[1, e] + 0.5 * (ahead - ext_ref[e, slices - 1]))
        ahead = jnp.where(rank < count - 1, ahead, 0.0)
        for z in range(slices):
            k = e * slices + z
            adj = adj_ref[e, z]
            if z == 0:
                adj = adj + behind
            if z == slices - 1:
                adj = adj - ahead
            for (row, sign, there), out in zip(sides, face_refs):
                adj = adj + jnp.where(sub == row, out[k : k + 1], 0.0)
            base_ref[e, z] = cur_ref[e, z] - tau_ref[e, z] * adj


def last_update_kernel(size, base_ref, pull_ref, tau_ref, still_ref, dd_ref, yedge_ref, own_pack_ref, *refs):
    elems, slices, cells, width = base_ref.shape
    *pack_refs, new_ref, dual_ref, parts_ref, sums_ref = refs
    mine = lax.axis_index("path")
    packs, (ahead, behind) = merge_all(size // 2, None, pack_refs, None, 2)
    image = packs[2]
    sig = dd_ref[1]
    data_dual = (dd_ref[0] + sig * (image - still_ref[...])) / (1.0 + sig)
    part(dual_ref, data_dual)
    y_ahead = jnp.where(mine < size - 1, clip(yedge_ref[0] + 0.5 * (ahead - own_pack_ref[1])), 0.0)
    y_behind = jnp.where(mine > 0, clip(yedge_ref[1] + 0.5 * (own_pack_ref[0] - behind)), 0.0)
    lane = lax.broadcasted_iota(jnp.int32, (cells, width), 1)
    rim = (lane == 0) | (lane == width - 1)
    joined = join_edges(y_behind, -y_ahead, lane)

    spread(data_dual, lane, elems, slices, parts_ref, sums_ref)
    for e in range(elems):
        for z in range(slices):
            k = e * slices + z
            new = base_ref[e, z] - pull_ref[e, z] * sums_ref[k * cells : (k + 1) * cells]
            new = new - tau_ref[e, z] * edge_columns(joined[k % 2], rim, k)
            new_ref[e, z] = jnp.maximum(new, 0.0)


def shards(maps, measured, beta_table, view, kappa, line_of, side):
    elems, slices, cells, width = maps.shape
    total_x = cells * lax.axis_size("beam")
    total_y = width * lax.axis_size("path")
    size = lax.axis_size("path")
    block = f32(elems, slices, cells, width)
    plane = f32(elems, cells, width)
    rows = f32(elems * slices, width)
    faces = len(beam_sides(cells))
    measured = measured.transpose(0, 2, 1)
    kappa = kappa.T
    view = view.reshape(1, 1)

    tall = f32((elems + 1) * slices, width)
    parts = pltpu.VMEM((elems * slices * cells, 2 * width), jnp.bfloat16)
    sums = pltpu.VMEM((elems * slices * cells, width), F32)
    maps, inside, coef, *own = call(
        functools.partial(open_kernel, total_x),
        [view] + [pltpu.with_memory_space_constraint(a, pltpu.HBM) for a in (maps, beta_table, kappa, line_of, side)],
        [block, f32(slices, cells, width), f32(elems * elems + elems, width), tall] + [rows] * (faces - 1),
        [SMEM] + [pltpu.HBM] * 5,
        [
            pltpu.SMEM(beta_table.shape, F32),
            pltpu.SMEM(kappa.shape, F32),
            pltpu.SMEM(line_of.shape, jnp.int32),
            pltpu.SMEM(side.shape, jnp.int32),
            pltpu.SemaphoreType.DMA((4 + PARTS,)),
        ],
    )
    other = exchange_beam(own)
    carry, skip = other[-1], elems * slices
    beams = lax.axis_size("beam")
    if beams > 2:
        carry, skip = carry[skip:], 0
        reach = 1
        while reach < beams - 1:
            far = lax.axis_index("beam") > reach
            carry = carry + jnp.where(far, shifted(carry, "beam", reach), 0.0)
            reach *= 2
    local, still = call(
        functools.partial(depth_kernel, total_y),
        [maps, coef],
        [block, f32(4, cells, width)],
        [VMEM] * 2,
        [
            pltpu.VMEM(maps.shape, F32),
            parts,
            pltpu.VMEM((elems * slices * cells, 2 * width), F32),
        ],
    )
    weight, pack, zone, ztwo = call(
        functools.partial(weight_kernel, total_x, skip),
        [maps, inside, carry, local, still],
        [block, f32(5, cells, width), plane, plane],
        [VMEM] * 5,
        [parts, parts, sums],
    )
    packs = around(pack, "path", -1.0 / total_y, still)
    zone, ztwo = swapped(zone, 0), swapped(ztwo, 1)
    dual_z, dual_x, dual_y, adj, counts, *edge = call(
        first_dual_kernel,
        [maps, measured, *own, *other],
        [block, block, block, block, f32(cells, width)] + [rows] * faces,
        [VMEM] * (2 + 2 * faces),
    )
    pull, tau, current, extrap, dd, yedge, zdual, pack, emission = call(
        functools.partial(first_update_kernel, total_y, size),
        [maps, weight, adj, counts, still, pack, zone, ztwo, *packs],
        [block, block, block, block, f32(2, cells, width), f32(2, cells, width), f32(2, elems, cells, width),
         f32(5, cells, width), f32(elems, cells, slices)],
        [VMEM] * (8 + len(packs)),
        [parts, sums, sums],
    )
    packs = around(pack, "path", None)
    zone, ztwo, *own = call(face_kernel, [extrap], [plane, plane] + [rows] * faces, [VMEM])
    zone, ztwo = swapped(zone, 0), swapped(ztwo, 1)
    other = exchange_beam(own)
    (adj,) = call(second_dual_kernel, [extrap, dual_z, dual_x, dual_y], [block], [VMEM] * 4)
    (base,) = call(
        second_face_kernel,
        [current, extrap, tau, adj, zdual, zone, ztwo, *edge, *own, *other],
        [block],
        [VMEM] * (7 + 3 * faces),
        [pltpu.VMEM((elems * slices, width), F32)] * faces,
    )
    current, data_dual = call(
        functools.partial(last_update_kernel, size),
        [base, pull, tau, counts, dd, yedge, pack, *packs],
        [block, f32(elems, cells, slices)],
        [VMEM] * (7 + len(packs)),
        [parts, sums],
    )
    return emission.transpose(0, 2, 1), current, data_dual.transpose(0, 2, 1)


def solution(mesh):
    return jax.shard_map(
        shards,
        mesh=mesh,
        in_specs=(P(None, "gz", "beam", "path"), P(None, "gz", "beam"), P(), P(), P(), P(), P()),
        out_specs=(P(None, "gz", "beam"), P(None, "gz", "beam", "path"), P(None, "gz", "beam")),
        check_vma=False,
    )
```

```python
import functools

import jax
import jax.numpy as jnp
from jax import lax
from jax.experimental import pallas as pl
from jax.experimental.pallas import tpu as pltpu
from jax.sharding import PartitionSpec as P

ITERS = 2
LAM = 0.1
F32 = jnp.float32
VMEM = pltpu.VMEM
SMEM = pltpu.SMEM
UNROLL = 4
VMEM_LIMIT = 32 * 1024 * 1024


def clip(value):
    return jnp.clip(value, -LAM, LAM)


def call(body, ins, outs, spaces, scratch=(), flops=1_000_000):
    specs = [pl.BlockSpec(memory_space=space) for space in spaces]
    moved = sum(a.size * 4 for a in ins) + sum(o.size * 4 for o in outs)
    return pl.pallas_call(
        body,
        out_shape=outs,
        in_specs=specs,
        out_specs=[pl.BlockSpec(memory_space=VMEM)] * len(outs),
        scratch_shapes=list(scratch),
        compiler_params=pltpu.CompilerParams(vmem_limit_bytes=VMEM_LIMIT),
        cost_estimate=pl.CostEstimate(flops=flops, bytes_accessed=moved, transcendentals=0),
    )(*ins)


def f32(*shape):
    return jax.ShapeDtypeStruct(shape, F32)


def shifted(block, axis, distance):
    n = lax.axis_size(axis)
    return lax.ppermute(block, axis, [((i - distance) % n, i) for i in range(n)])


def swapped(block, start):
    n, paths = lax.axis_size("gz"), lax.axis_size("path")
    route = []
    for p in range(paths):
        for z in range(n):
            other = z + 1 if (z - start) % 2 == 0 else z - 1
            there = (p, other) if 0 <= other < n else (p ^ 1, z)
            route.append((p * n + z, there[0] * n + there[1]))
    return lax.ppermute(block, ("path", "gz"), route)


def pair_order(ahead, behind):
    even = lax.rem(lax.axis_index("gz"), 2) == 0
    return jnp.where(even, ahead, behind), jnp.where(even, behind, ahead)


def merged(mine, other, far, scale, bit):
    upper = (lax.axis_index("path") & bit) != 0
    low = [jnp.where(upper, o, m) for m, o in zip(mine, other)]
    high = [jnp.where(upper, m, o) for m, o in zip(mine, other)]
    if far is None:
        return [low[0], high[1]] + [a + b for a, b in zip(low[2:], high[2:])]
    low_factor = jnp.where(far, jnp.exp(high[2] * scale), 1.0)
    high_factor = jnp.where(far, 1.0, jnp.exp(low[2] * scale))
    sums = [low_factor * a + high_factor * b for a, b in zip(low[3:], high[3:])]
    return [low[0], high[1], low[2] + high[2]] + sums


def passed(state, other, far, bit):
    mine = lax.axis_index("path")
    ahead = jnp.where(mine & (2 * bit - 1) == bit - 1, other[0], state[0])
    behind = jnp.where(mine & (2 * bit - 1) == bit, other[1], state[1])
    if far is None:
        return [ahead, behind]
    upper = (mine & bit) != 0
    in_way = jnp.where(upper, jnp.where(far, 0.0, other[2]), jnp.where(far, other[2], 0.0))
    return [ahead, behind, state[2] + in_way]


def rows_of(ref):
    return [ref[i] for i in range(ref.shape[0])]


def merge_all(bit, scale, refs, far, kept):
    mine_ref, other_ref, *state_refs = refs
    state = rows_of(state_refs[0]) if state_refs else [jnp.zeros(mine_ref.shape[1:], F32)] * kept
    mine, other = rows_of(mine_ref), rows_of(other_ref)
    return merged(mine, other, far, scale, bit), passed(state, other, far, bit)


def merge_kernel(bit, scale, kept, *refs):
    *refs, out_ref, state_ref = refs
    far = None
    if kept == 3:
        far_ref, *refs = refs
        far = far_ref[3] != 0.0
    packs, state = merge_all(bit, scale, refs, far, kept)
    for ref, values in ((out_ref, packs), (state_ref, state)):
        for i, value in enumerate(values):
            ref[i] = value


def around(block, axis, scale, far=None):
    n = lax.axis_size(axis)
    if n < 2 or n & (n - 1):
        raise ValueError("path size")
    kept = 2 if far is None else 3
    state = []
    bit = 1
    while True:
        other = lax.ppermute(block, axis, [(i, i ^ bit) for i in range(n)])
        if 2 * bit == n:
            return [block, other] + state
        ins = ([] if far is None else [far]) + [block, other] + state
        block, *state = call(
            functools.partial(merge_kernel, bit, scale, kept),
            ins,
            [f32(*block.shape), f32(kept, *block.shape[1:])],
            [VMEM] * len(ins),
        )
        bit *= 2


def split(flat):
    high = flat.astype(jnp.bfloat16)
    return high, (flat - high.astype(F32)).astype(jnp.bfloat16)


def put_rows(parts_ref, e, tiles):
    slices, cells, width = tiles.shape
    at = slice(e * slices * cells, (e + 1) * slices * cells)
    parts_ref[at, 0:width], parts_ref[at, width:] = split(tiles.reshape(slices * cells, width))


def row_sums(parts_ref, sums_ref):
    depth, width = parts_ref.shape[1], sums_ref.shape[1]
    ones = jnp.ones((depth, width), jnp.bfloat16)
    sums_ref[...] = jnp.dot(parts_ref[...], ones, preferred_element_type=F32)


def packed_sums(sums_ref, lane):
    cells, width = lane.shape
    pack = jnp.zeros((cells, width), F32)
    for k in range(sums_ref.shape[0] // cells):
        pack = jnp.where(lane == k, sums_ref[k * cells : (k + 1) * cells], pack)
    return pack


def spread(pack, lane, elems, slices, parts_ref, sums_ref):
    cells, width = pack.shape
    rows = slices * cells
    halves = [part.astype(F32) for part in split(pack)]
    for e in range(elems):
        masks = [lane == e * slices + z for z in range(slices)]
        for i, half in enumerate(halves):
            flat = jnp.stack([jnp.where(mask, half, 0.0) for mask in masks]).reshape(rows, width)
            parts_ref[e * rows : (e + 1) * rows, i * width : (i + 1) * width] = flat.astype(jnp.bfloat16)
    row_sums(parts_ref, sums_ref)


def gather_edges(pack, tile, lane, k):
    width = tile.shape[1]
    here = (lane == k) | (lane == (k - 1) % width)
    return jnp.where(here, pltpu.roll(tile, k, axis=1) if k else tile, pack)


def packed_edges(edges, lane):
    even = lane % 2 == 0
    first = jnp.where(even, edges[0], edges[1])
    return first, pltpu.roll(jnp.where(even, edges[1], edges[0]), 1, axis=1)


def join_edges(first, last, lane):
    width = first.shape[1]
    last = pltpu.roll(last, width - 1, axis=1)
    even = lane % 2 == 0
    return jnp.where(even, first, last), jnp.where(even, last, first)


def edge_columns(pack, rim, k):
    return jnp.where(rim, pltpu.roll(pack, pack.shape[1] - k, axis=1) if k else pack, 0.0)


def reciprocal(value):
    guess = pl.reciprocal(value, approx=True)
    return guess * (2.0 - value * guess)


def beam_sides(cells):
    count, rank = lax.axis_size("beam"), lax.axis_index("beam")
    if count == 2:
        return [
            (
                jnp.where(rank == 0, cells - 1, 0),
                jnp.where(rank == 0, F32(-1.0), F32(1.0)),
                None,
            )
        ]
    return [(cells - 1, F32(-1.0), rank < count - 1), (0, F32(1.0), rank > 0)]


def beam_rows(first, last):
    count, rank = lax.axis_size("beam"), lax.axis_index("beam")
    if count == 2:
        return [jnp.where(rank == 0, last, first)]
    return [last, first]


def face(own, other, sign, there):
    step = (own - other) * sign
    return step if there is None else jnp.where(there, step, 0.0)


def exchange_beam(rows):
    if lax.axis_size("beam") == 2:
        return [lax.ppermute(rows[0], "beam", [(0, 1), (1, 0)])]
    return [shifted(rows[1], "beam", -1), shifted(rows[0], "beam", 1)]


def open_kernel(total, view_ref, source_ref, *refs):
    small, refs = refs[:4], refs[4:]
    maps_ref, inside_ref, coef_ref, *refs = refs
    elems, slices, cells, width = maps_ref.shape
    faces = len(beam_sides(cells))
    face_refs, refs = refs[:faces], refs[faces:]
    beta_ref, kappa_ref, line_ref, side_ref, sems = refs
    half = slices // 2
    parts = [pl.ds(0, half), pl.ds(half, slices - half)] if half else [pl.ds(0, slices)]
    fetch = []
    for i, (ref, kept) in enumerate(zip(small, (beta_ref, kappa_ref, line_ref, side_ref))):
        fetch.append(pltpu.make_async_copy(ref, kept, sems.at[i]))
    large = []
    for i, at in enumerate(parts):
        large.append(pltpu.make_async_copy(source_ref.at[:, at], maps_ref.at[:, at], sems.at[len(small) + i]))
    for copy in large[:1] + fetch + large[1:]:
        copy.start()
    for copy in fetch:
        copy.wait()
    for e in range(elems):
        line = line_ref[e]
        for f in range(elems):
            coef_ref[e * elems + f : e * elems + f + 1] = jnp.full((1, width), kappa_ref[f, line])
        coef_ref[elems * elems + e : elems * elems + e + 1] = jnp.full((1, width), side_ref[e].astype(F32))
    view = view_ref[0, 0]
    beta = [beta_ref[view, e] for e in range(elems)]
    sub = lax.broadcasted_iota(jnp.int32, maps_ref.shape[2:], 0)
    for z in range(slices):
        if z == 0 or z == half:
            large[1 if z else 0].wait()
        tiles = [maps_ref[e, z] for e in range(elems)]
        mu = beta[0] * tiles[0]
        for e in range(1, elems):
            mu = mu + beta[e] * tiles[e]
        run = mu
        reach = 1
        while reach < cells:
            run = run + jnp.where(sub >= reach, pltpu.roll(run, reach, axis=0), 0.0)
            reach *= 2
        inside_ref[z] = jnp.where(sub >= 1, pltpu.roll(run, 1, axis=0), 0.0)
        face_refs[0][elems * slices + z : elems * slices + z + 1] = run[cells - 1 : cells]
        for e in range(elems):
            rows = beam_rows(tiles[e][0:1], tiles[e][cells - 1 : cells])
            for ref, row in zip(face_refs, rows):
                ref[e * slices + z : e * slices + z + 1] = row


def depth_kernel(total, maps_ref, coef_ref, local_ref, pack_ref, mu_ref, parts_ref, sums_ref):
    elems, slices, cells, width = maps_ref.shape
    rows = slices * cells
    row = lax.broadcasted_iota(jnp.int32, (2 * width, 2 * width), 0)
    col = lax.broadcasted_iota(jnp.int32, (2 * width, 2 * width), 1)
    row = jnp.where(row >= width, row - width, row)
    table = jnp.where((row < col) | (col >= width), 1.0, 0.0).astype(jnp.bfloat16)
    for e in range(elems):
        mu = coef_ref[e * elems : e * elems + 1][None] * maps_ref[0]
        for f in range(1, elems):
            mu = mu + coef_ref[e * elems + f : e * elems + f + 1][None] * maps_ref[f]
        mu_ref[e] = mu
        put_rows(parts_ref, e, mu)
    sums_ref[...] = jnp.dot(parts_ref[...], table, preferred_element_type=F32)
    lane = lax.broadcasted_iota(jnp.int32, (cells, width), 1)
    scale = -1.0 / total
    strip = jnp.zeros((cells, width), F32)
    edges = [strip, strip]
    for e in range(elems):
        forward = coef_ref[elems * elems + e : elems * elems + e + 1] == 0.0
        for z in range(slices):
            k = e * slices + z
            before = sums_ref[k * cells : (k + 1) * cells, 0:width]
            whole = sums_ref[k * cells : (k + 1) * cells, width:]
            after = whole - before - mu_ref[e, z]
            local_ref[e, z] = jnp.exp(jnp.where(forward, before, after) * scale)
            strip = jnp.where(lane == k, whole, strip)
            edges[k % 2] = gather_edges(edges[k % 2], maps_ref[e, z], lane, k)
    pack_ref[0], pack_ref[1] = packed_edges(edges, lane)
    pack_ref[2] = strip
    far = jnp.zeros((cells, width), F32)
    for e in range(elems):
        inside = (lane >= e * slices) & (lane < (e + 1) * slices)
        far = jnp.where(inside, coef_ref[elems * elems + e : elems * elems + e + 1][:, 0:1], far)
    pack_ref[3] = far


def weight_kernel(total, skip, maps_ref, inside_ref, carry_ref, local_ref, pack_ref, weight_ref, out_ref, zone_ref,
                  ztwo_ref, proj_ref, whole_ref, sums_ref):
    elems, slices, cells, width = maps_ref.shape
    lane = lax.broadcasted_iota(jnp.int32, (cells, width), 1)
    there = lax.axis_index("beam") > 0
    carry = jnp.where(there, carry_ref[skip : skip + slices], 0.0)
    att = jnp.exp((inside_ref[...] + carry[:, None]) * (-1.0 / total))
    for e in range(elems):
        weight = att * local_ref[e]
        weight_ref[e] = weight
        put_rows(whole_ref, e, weight)
        put_rows(proj_ref, e, weight * maps_ref[e])
    row_sums(proj_ref, sums_ref)
    out_ref[3] = packed_sums(sums_ref, lane)
    row_sums(whole_ref, sums_ref)
    out_ref[4] = packed_sums(sums_ref, lane)
    for i in range(3):
        out_ref[i] = pack_ref[i]
    for e in range(elems):
        zone_ref[e], ztwo_ref[e] = pair_order(maps_ref[e, slices - 1], maps_ref[e, 0])


def dual_step(field, ahead, dual, last):
    step = 0.5 * (ahead - field)
    return jnp.where(last, 0.0, clip(step if dual is None else dual + step))


def tile_duals(tile, dual_x, dual_y, sub, lane, shape):
    cells, width = shape
    new_x = dual_step(tile, pltpu.roll(tile, cells - 1, axis=0), dual_x, sub == cells - 1)
    new_y = dual_step(tile, pltpu.roll(tile, width - 1, axis=1), dual_y, lane == width - 1)
    spread = pltpu.roll(new_x, 1, axis=0) - new_x + (pltpu.roll(new_y, 1, axis=1) - new_y)
    return new_x, new_y, spread


def join(ref, width):
    elems, cells, slices = ref.shape
    parts = [ref[e] for e in range(elems)]
    if elems * slices < width:
        parts.append(jnp.zeros((cells, width - elems * slices), F32))
    return jnp.concatenate(parts, axis=1)


def first_dual_kernel(maps_ref, measured_ref, *refs):
    elems, slices, cells, width = maps_ref.shape
    sides = beam_sides(cells)
    own_refs, refs = refs[: len(sides)], refs[len(sides) :]
    other_refs, refs = refs[: len(sides)], refs[len(sides) :]
    dual_z_ref, dual_x_ref, dual_y_ref, adj_ref, still_ref, *edge_refs = refs
    sub = lax.broadcasted_iota(jnp.int32, (cells, width), 0)
    lane = lax.broadcasted_iota(jnp.int32, (cells, width), 1)
    still_ref[...] = join(measured_ref, width)
    for (row, sign, there), own, other, edge in zip(sides, own_refs, other_refs, edge_refs):
        rows = pl.ds(0, elems * slices)
        edge[...] = clip(0.5 * face(own[rows], other[rows], sign, there))
    def step(z, behind):
        at_end = z == slices - 1
        duals = []
        for e in range(elems):
            tile = maps_ref[e, z]
            ahead = maps_ref[e, jnp.minimum(z + 1, slices - 1)]
            dual_z = jnp.where(at_end, 0.0, clip(0.5 * (ahead - tile)))
            dual_x, dual_y, spread = tile_duals(tile, None, None, sub, lane, (cells, width))
            dual_z_ref[e, z] = dual_z
            dual_x_ref[e, z] = dual_x
            dual_y_ref[e, z] = dual_y
            spread = spread + (behind[e] - dual_z)
            for (row, sign, there), edge in zip(sides, edge_refs):
                spread = spread + jnp.where(sub == row, sign * edge[pl.ds(e * slices + z, 1)], 0.0)
            adj_ref[e, z] = spread
            duals.append(dual_z)
        return tuple(duals)

    zero = jnp.zeros((cells, width), F32)
    lax.fori_loop(0, slices, step, (zero,) * elems, unroll=UNROLL)


def part(ref, pack):
    slices = ref.shape[2]
    for e in range(ref.shape[0]):
        ref[e] = pack[:, e * slices : (e + 1) * slices]


def first_update_kernel(total, size, maps_ref, weight_ref, adj_ref, still_ref, far_ref, pack_ref, zone_ref, ztwo_ref,
                        *refs):
    elems, slices, cells, width = maps_ref.shape
    pack_refs, refs = refs[:-12], refs[-12:]
    pull_ref, tau_ref, cur_ref, ext_ref, dd_ref, yedge_ref, zdual_ref, out_ref, emission_ref, *refs = refs
    parts_ref, own_ref, dual_ref = refs
    count, rank = lax.axis_size("gz"), lax.axis_index("gz")
    mine = lax.axis_index("path")
    pack_shape = (cells, width)
    lane = lax.broadcasted_iota(jnp.int32, pack_shape, 1)
    rim = (lane == 0) | (lane == width - 1)
    packs, state = merge_all(size // 2, -1.0 / total, pack_refs, far_ref[3] != 0.0, 3)
    image, weights = packs[3], packs[4]
    ahead, behind, base = state
    own = jnp.exp(base * (-1.0 / total))
    sig = 1.0 / weights
    data_dual = sig * (image - still_ref[...]) / (1.0 + sig)
    dd_ref[0] = data_dual
    dd_ref[1] = sig
    part(emission_ref, image * (1.0 / total))
    y_ahead = jnp.where(mine < size - 1, clip(0.5 * (ahead - pack_ref[1])), 0.0)
    y_behind = jnp.where(mine > 0, clip(0.5 * (pack_ref[0] - behind)), 0.0)
    joined = join_edges(y_behind, -y_ahead, lane)
    yedge_ref[0] = y_ahead
    yedge_ref[1] = y_behind

    spread(own, lane, elems, slices, parts_ref, own_ref)
    spread(data_dual, lane, elems, slices, parts_ref, dual_ref)
    edges = [jnp.zeros(pack_shape, F32)] * 2
    for e in range(elems):
        ahead, behind = pair_order(zone_ref[e], ztwo_ref[e])
        behind = jnp.where(rank > 0, clip(0.5 * (maps_ref[e, 0] - behind)), 0.0)
        ahead = jnp.where(rank < count - 1, clip(0.5 * (ahead - maps_ref[e, slices - 1])), 0.0)
        zdual_ref[0, e] = behind
        zdual_ref[1, e] = ahead
        rows = []
        for z in range(slices):
            k = e * slices + z
            at = slice(k * cells, (k + 1) * cells)
            tile = maps_ref[e, z]
            weight = weight_ref[e, z] * own_ref[at]
            tau = reciprocal(weight + 6.0)
            step = weight * dual_ref[at] + adj_ref[e, z] + edge_columns(joined[k % 2], rim, k)
            if z == 0:
                step = step + behind
            if z == slices - 1:
                step = step - ahead
            new = jnp.maximum(tile - step * tau, 0.0)
            ext = 2.0 * new - tile
            tau_ref[e, z] = tau
            pull_ref[e, z] = tau * weight
            cur_ref[e, z] = new
            ext_ref[e, z] = ext
            rows.append(weight * ext)
            edges[k % 2] = gather_edges(edges[k % 2], ext, lane, k)
        put_rows(parts_ref, e, jnp.stack(rows))
    out_ref[0], out_ref[1] = packed_edges(edges, lane)
    row_sums(parts_ref, own_ref)
    out_ref[2] = packed_sums(own_ref, lane)
    for i in range(3, out_ref.shape[0]):
        out_ref[i] = jnp.zeros(pack_shape, F32)


def face_kernel(ext_ref, zone_ref, ztwo_ref, *face_refs):
    elems, slices, cells, _ = ext_ref.shape
    for e in range(elems):
        for z in range(slices):
            rows = beam_rows(ext_ref[e, z, 0:1], ext_ref[e, z, cells - 1 : cells])
            for ref, row in zip(face_refs, rows):
                ref[e * slices + z : e * slices + z + 1] = row
        zone_ref[e], ztwo_ref[e] = pair_order(ext_ref[e, slices - 1], ext_ref[e, 0])


def second_dual_kernel(ext_ref, dual_z_ref, dual_x_ref, dual_y_ref, adj_ref):
    elems, slices, cells, width = ext_ref.shape
    sub = lax.broadcasted_iota(jnp.int32, (cells, width), 0)
    lane = lax.broadcasted_iota(jnp.int32, (cells, width), 1)

    def step(z, behind):
        at_end = z == slices - 1
        duals = []
        for e in range(elems):
            tile = ext_ref[e, z]
            ahead = ext_ref[e, jnp.minimum(z + 1, slices - 1)]
            dual_z = jnp.where(at_end, 0.0, clip(dual_z_ref[e, z] + 0.5 * (ahead - tile)))
            _, _, spread = tile_duals(tile, dual_x_ref[e, z], dual_y_ref[e, z], sub, lane, (cells, width))
            adj_ref[e, z] = spread + (behind[e] - dual_z)
            duals.append(dual_z)
        return tuple(duals)

    zero = jnp.zeros((cells, width), F32)
    lax.fori_loop(0, slices, step, (zero,) * elems, unroll=UNROLL)


def second_face_kernel(cur_ref, ext_ref, tau_ref, adj_ref, zdual_ref, zone_ref, ztwo_ref, *refs):
    elems, slices, cells, width = cur_ref.shape
    sides = beam_sides(cells)
    edge_refs, refs = refs[: len(sides)], refs[len(sides) :]
    own_refs, refs = refs[: len(sides)], refs[len(sides) :]
    other_refs, refs = refs[: len(sides)], refs[len(sides) :]
    base_ref, *face_refs = refs
    count, rank = lax.axis_size("gz"), lax.axis_index("gz")
    sub = lax.broadcasted_iota(jnp.int32, (cells, width), 0)
    for (row, sign, there), edge, own, other, out in zip(sides, edge_refs, own_refs, other_refs, face_refs):
        out[...] = clip(edge[...] + 0.5 * face(own[...], other[...], sign, there)) * sign
    for e in range(elems):
        ahead, behind = pair_order(zone_ref[e], ztwo_ref[e])
        behind = jnp.where(rank > 0, clip(zdual_ref[0, e] + 0.5 * (ext_ref[e, 0] - behind)), 0.0)
        ahead = clip(zdual_ref[1, e] + 0.5 * (ahead - ext_ref[e, slices - 1]))
        ahead = jnp.where(rank < count - 1, ahead, 0.0)
        for z in range(slices):
            k = e * slices + z
            adj = adj_ref[e, z]
            if z == 0:
                adj = adj + behind
            if z == slices - 1:
                adj = adj - ahead
            for (row, sign, there), out in zip(sides, face_refs):
                adj = adj + jnp.where(sub == row, out[k : k + 1], 0.0)
            base_ref[e, z] = cur_ref[e, z] - tau_ref[e, z] * adj


def last_update_kernel(size, base_ref, pull_ref, tau_ref, still_ref, dd_ref, yedge_ref, own_pack_ref, *refs):
    elems, slices, cells, width = base_ref.shape
    *pack_refs, new_ref, dual_ref, parts_ref, sums_ref = refs
    mine = lax.axis_index("path")
    packs, (ahead, behind) = merge_all(size // 2, None, pack_refs, None, 2)
    image = packs[2]
    sig = dd_ref[1]
    data_dual = (dd_ref[0] + sig * (image - still_ref[...])) / (1.0 + sig)
    part(dual_ref, data_dual)
    y_ahead = jnp.where(mine < size - 1, clip(yedge_ref[0] + 0.5 * (ahead - own_pack_ref[1])), 0.0)
    y_behind = jnp.where(mine > 0, clip(yedge_ref[1] + 0.5 * (own_pack_ref[0] - behind)), 0.0)
    lane = lax.broadcasted_iota(jnp.int32, (cells, width), 1)
    rim = (lane == 0) | (lane == width - 1)
    joined = join_edges(y_behind, -y_ahead, lane)

    spread(data_dual, lane, elems, slices, parts_ref, sums_ref)
    for e in range(elems):
        for z in range(slices):
            k = e * slices + z
            new = base_ref[e, z] - pull_ref[e, z] * sums_ref[k * cells : (k + 1) * cells]
            new = new - tau_ref[e, z] * edge_columns(joined[k % 2], rim, k)
            new_ref[e, z] = jnp.maximum(new, 0.0)


def shards(maps, measured, beta_table, view, kappa, line_of, side):
    elems, slices, cells, width = maps.shape
    total_x = cells * lax.axis_size("beam")
    total_y = width * lax.axis_size("path")
    size = lax.axis_size("path")
    block = f32(elems, slices, cells, width)
    plane = f32(elems, cells, width)
    rows = f32(elems * slices, width)
    faces = len(beam_sides(cells))
    measured = measured.transpose(0, 2, 1)
    kappa = kappa.T
    view = view.reshape(1, 1)

    tall = f32((elems + 1) * slices, width)
    parts = pltpu.VMEM((elems * slices * cells, 2 * width), jnp.bfloat16)
    sums = pltpu.VMEM((elems * slices * cells, width), F32)
    maps, inside, coef, *own = call(
        functools.partial(open_kernel, total_x),
        [view] + [pltpu.with_memory_space_constraint(a, pltpu.HBM) for a in (maps, beta_table, kappa, line_of, side)],
        [block, f32(slices, cells, width), f32(elems * elems + elems, width), tall] + [rows] * (faces - 1),
        [SMEM] + [pltpu.HBM] * 5,
        [
            pltpu.SMEM(beta_table.shape, F32),
            pltpu.SMEM(kappa.shape, F32),
            pltpu.SMEM(line_of.shape, jnp.int32),
            pltpu.SMEM(side.shape, jnp.int32),
            pltpu.SemaphoreType.DMA((6,)),
        ],
    )
    other = exchange_beam(own)
    carry, skip = other[-1], elems * slices
    beams = lax.axis_size("beam")
    if beams > 2:
        carry, skip = carry[skip:], 0
        reach = 1
        while reach < beams - 1:
            far = lax.axis_index("beam") > reach
            carry = carry + jnp.where(far, shifted(carry, "beam", reach), 0.0)
            reach *= 2
    local, still = call(
        functools.partial(depth_kernel, total_y),
        [maps, coef],
        [block, f32(4, cells, width)],
        [VMEM] * 2,
        [
            pltpu.VMEM(maps.shape, F32),
            parts,
            pltpu.VMEM((elems * slices * cells, 2 * width), F32),
        ],
    )
    weight, pack, zone, ztwo = call(
        functools.partial(weight_kernel, total_x, skip),
        [maps, inside, carry, local, still],
        [block, f32(5, cells, width), plane, plane],
        [VMEM] * 5,
        [parts, parts, sums],
    )
    packs = around(pack, "path", -1.0 / total_y, still)
    zone, ztwo = swapped(zone, 0), swapped(ztwo, 1)
    dual_z, dual_x, dual_y, adj, counts, *edge = call(
        first_dual_kernel,
        [maps, measured, *own, *other],
        [block, block, block, block, f32(cells, width)] + [rows] * faces,
        [VMEM] * (2 + 2 * faces),
    )
    pull, tau, current, extrap, dd, yedge, zdual, pack, emission = call(
        functools.partial(first_update_kernel, total_y, size),
        [maps, weight, adj, counts, still, pack, zone, ztwo, *packs],
        [block, block, block, block, f32(2, cells, width), f32(2, cells, width), f32(2, elems, cells, width),
         f32(5, cells, width), f32(elems, cells, slices)],
        [VMEM] * (8 + len(packs)),
        [parts, sums, sums],
    )
    packs = around(pack, "path", None)
    zone, ztwo, *own = call(face_kernel, [extrap], [plane, plane] + [rows] * faces, [VMEM])
    zone, ztwo = swapped(zone, 0), swapped(ztwo, 1)
    other = exchange_beam(own)
    (adj,) = call(second_dual_kernel, [extrap, dual_z, dual_x, dual_y], [block], [VMEM] * 4)
    (base,) = call(
        second_face_kernel,
        [current, extrap, tau, adj, zdual, zone, ztwo, *edge, *own, *other],
        [block],
        [VMEM] * (7 + 3 * faces),
        [pltpu.VMEM((elems * slices, width), F32)] * faces,
    )
    current, data_dual = call(
        functools.partial(last_update_kernel, size),
        [base, pull, tau, counts, dd, yedge, pack, *packs],
        [block, f32(elems, cells, slices)],
        [VMEM] * (7 + len(packs)),
        [parts, sums],
    )
    return emission.transpose(0, 2, 1), current, data_dual.transpose(0, 2, 1)


def solution(mesh):
    return jax.shard_map(
        shards,
        mesh=mesh,
        in_specs=(P(None, "gz", "beam", "path"), P(None, "gz", "beam"), P(), P(), P(), P(), P()),
        out_specs=(P(None, "gz", "beam"), P(None, "gz", "beam", "path"), P(None, "gz", "beam")),
        check_vma=False,
    )
```
